32 devices in a mesh: gz: 16 (over z, y, x), gy: 2 (over core).
Axes of the slice: x: 2, y: 2, z: 4, core: 2. Of those that a mesh axis runs over, the one named last changes fastest.
Arguments:
- starting_densities: float32 [16, 4, 128, 128], P(None, 'gy', 'gz'), may hold values from -3 to 5
- medium_admittance: float32 [4, 128, 128], P('gy', 'gz'), may hold values from 0.25 to 2
- local_warmth: float32 [4, 128, 128], P('gy', 'gz'), may hold values from 0.5 to 2
- spreading_coefficient: float32 [16], replicated, may hold values from 1 to 8
- frequency_factors: float32 [16], replicated, may hold values from 0.5 to 2
- barrier_energies: float32 [16], replicated, may hold values from 1 to 4
- molar_proportions: float32 [16, 16], replicated, may hold values from -1.5 to 1.5
Outputs:
- updated: float32 [16, 4, 128, 128], P(None, 'gy', 'gz')
The draws below stay inside these ranges and needn't reach their ends.
All inputs are finite; a program needn't handle non-finite values.
Results may differ from the reference program's by a relative error of at most 0.0003.
Values sent between devices are 32-bit elements; how exact they have to be, the bound alone decides.
No kernel may reach another device: no remote copies, remote signals or barrier semaphores. Data moves between devices by JAX's collectives and lax.ppermute only.
A program may use at most 64 MiB of HBM per device.

```python
import math
import jax
import jax.numpy as jnp
from jax import lax

S = 16
VOLUMES_WIDTHWISE = 128
STEPS = 2
VOLUMES_LENGTHWAY = 4
VOLUMES_UPWARD = 128


def draw_starting_densities(key, part):
    key = jax.random.fold_in(key, 11)
    rough = jax.random.truncated_normal(key, -4.0, 4.0, (S, VOLUMES_LENGTHWAY, VOLUMES_UPWARD, VOLUMES_WIDTHWISE), jnp.float32)
    return 1.0 + rough


def level_of(key, extent, cuts, least, largest):
    gain, own = 1.0, jax.random.fold_in(key, 6)
    for dim, shards_of in cuts:
        steps = jnp.exp(jax.random.uniform(jax.random.fold_in(own, dim), (shards_of,), jnp.float32, least / len(cuts), largest / len(cuts)))
        gain = gain * jnp.repeat(steps, extent[dim] // shards_of).reshape([-1 if axis == dim else 1 for axis in range(len(extent))])
    return gain


def scatter_about(rng, shape, scale, bound, kind=jnp.bfloat16):
    return jnp.clip(scale * jax.random.normal(rng, shape, jnp.float32), -bound, bound).astype(kind)


def setup_inputs(seed: int = 0) -> dict:
    splits = jax.random.split(jax.random.key(seed), 8)
    starting_densities = draw_starting_densities(jax.random.fold_in(splits[7], 71), 0)
    medium_admittance = jnp.clip(0.25 + 1.75 * jax.random.uniform(splits[1], (VOLUMES_LENGTHWAY, VOLUMES_UPWARD, VOLUMES_WIDTHWISE), jnp.float32) ** level_of(splits[1], (VOLUMES_LENGTHWAY, VOLUMES_UPWARD, VOLUMES_WIDTHWISE), ((0, 2), (1, 16)), -0.2, 0.2), 0.25, 2.0)
    local_warmth = jnp.clip(jnp.exp(math.log(2.0) - 1.3862944 * jax.random.uniform(splits[2], (VOLUMES_LENGTHWAY, VOLUMES_UPWARD, VOLUMES_WIDTHWISE), jnp.float32) ** level_of(splits[2], (VOLUMES_LENGTHWAY, VOLUMES_UPWARD, VOLUMES_WIDTHWISE), ((0, 2), (1, 16)), -0.2, 0.2)), 0.5, 2.0)
    spreading_coefficient = jnp.clip(jnp.exp(jax.random.uniform(splits[3], (S,), jnp.float32, math.log(1.0), math.log(8.0))), 1.0, 8.0)
    frequency_factors = jnp.clip(jnp.exp(jax.random.uniform(splits[4], (S,), jnp.float32, math.log(0.5), math.log(2.0))), 0.5, 2.0)
    barrier_energies = jnp.clip(jnp.exp(jax.random.uniform(splits[5], (S,), jnp.float32, math.log(1.0), math.log(4.0))), 1.0, 4.0)
    molar_proportions = scatter_about(splits[6], (S, S), S ** -0.5, 1.5, jnp.float32)
    return dict(starting_densities=starting_densities, medium_admittance=medium_admittance, local_warmth=local_warmth, spreading_coefficient=spreading_coefficient, frequency_factors=frequency_factors, barrier_energies=barrier_energies, molar_proportions=molar_proportions)


def neighbours(field, along):
    length = field.shape[along]
    widths = [(0, 0)] * field.ndim
    widths[along] = (1, 1)
    padded = jnp.pad(field, widths)
    after = lax.slice_in_dim(padded, 2, length + 2, axis=along)
    before = lax.slice_in_dim(padded, 0, length, axis=along)
    return (after, before)

def face_pair(medium_admittance, along):
    after, before = neighbours(medium_admittance, along)
    return (0.5 * (medium_admittance + after), 0.5 * (medium_admittance + before))

def directional(field, faces, rate, along):
    after, before = neighbours(field, along)
    return rate * (faces[0] * (after - field) - faces[1] * (field - before))

def line_system(right, faces, rate, along):
    lower = jnp.moveaxis(-0.5 * rate * faces[1], along, -1)
    upper = jnp.moveaxis(-0.5 * rate * faces[0], along, -1)
    middle = jnp.moveaxis(1.0 + 0.5 * rate * (faces[0] + faces[1]), along, -1)
    lower = lower.at[..., 0].set(0.0)
    upper = upper.at[..., -1].set(0.0)
    target = jnp.moveaxis(right, along, -1)[..., None]
    solved = lax.linalg.tridiagonal_solve(lower, middle, upper, target)[..., 0]
    return jnp.moveaxis(solved, -1, along)

def reference(starting_densities, medium_admittance, local_warmth, spreading_coefficient, frequency_factors, barrier_energies, molar_proportions):
    faces_x = face_pair(medium_admittance, 2)
    faces_y = face_pair(medium_admittance, 0)
    faces_z = face_pair(medium_admittance, 1)
    heat_liberated = 1.0 - 1.0 / local_warmth
    current = starting_densities
    for number in range(STEPS):
        reacting = frequency_factors[:, None, None, None] * jnp.exp(barrier_energies[:, None, None, None] * heat_liberated[None]) * jnp.tanh(current)

        def advance(pieces):
            field, weights, rate = pieces
            source = jnp.tensordot(weights, reacting, axes=1, precision=lax.Precision.HIGHEST)
            lap_x = directional(field, faces_x, 8.0 * rate, 2)
            lap_y = directional(field, faces_y, 0.015 * rate, 0)
            lap_z = directional(field, faces_z, 4096.0 * rate, 1)
            section = line_system(field + 0.5 * lap_x + lap_y + lap_z + source, faces_x, 8.0 * rate, 2)
            return line_system(section - 0.5 * lap_z, faces_z, 4096.0 * rate, 1)
        current = lax.map(advance, (current, molar_proportions, spreading_coefficient))
    return current
```

```python
import functools

import jax
import jax.numpy as jnp
from jax import lax
from jax.experimental import pallas as pl
from jax.experimental.pallas import tpu as pltpu
from jax.sharding import PartitionSpec as P

STEPS = 2
LARGE = 1e30
F32 = jnp.float32


class Sizes:
    def __init__(self, mesh, block):
        self.species, self.ny, self.nz, self.nx = block
        self.tiles = self.ny * self.nz
        self.lines = self.ny * self.species
        self.devices = mesh.shape["gz"]
        self.gy = mesh.shape["gy"]
        self.levels = (self.nx - 1).bit_length()

    def loop(self, start, stop, body, init):
        count = stop - start
        return lax.fori_loop(start, stop, body, init, unroll=count if count <= 16 else 1)


def column(ref, z):
    rows = lax.broadcasted_iota(jnp.int32, (z.species, z.nx), 0)
    value = jnp.zeros((z.species, z.nx), F32)
    for s in range(z.species):
        value = jnp.where(rows == s, ref[s], value)
    return value


def spread(ref, row, z):
    return jnp.broadcast_to(ref[pl.ds(row, 1), :], (z.species, z.nx))


def along_x(v, by, nx):
    return pltpu.roll(v, by % nx, v.ndim - 1)


def y_halo(received, z):
    if z.gy == 2:
        (both,) = received
        second = lax.axis_index("gy") == 1
        below = jnp.where(second, 1.0, 0.0).astype(F32)
        return (both, below), (both, 1.0 - below)
    return (received[0], 1.0), (received[1], 1.0)


def pack_kernel(z, c_ref, k_ref, pay_ref, *y_refs):
    me = lax.axis_index("gz")
    k = k_ref[...]
    for y in range(z.ny):
        base = z.tiles + y * z.species
        first = c_ref[pl.ds(y * z.nz, z.species, stride=z.tiles), :]
        last = c_ref[pl.ds(y * z.nz + z.nz - 1, z.species, stride=z.tiles), :]

        def fill(dest, carry):
            if y == 0:
                pay_ref[dest, 0 : z.tiles, :] = k
            pay_ref[dest, base : base + z.species, :] = jnp.where(dest > me, last, first)
            return carry

        z.loop(0, z.devices, fill, 0)
    if z.gy == 2:
        picks = [jnp.where(lax.axis_index("gy") == 1, 0, z.ny - 1)]
    else:
        picks = [z.ny - 1, 0]
    for ref, y in zip(y_refs, picks):
        for i in range(z.nz):
            ref[i * z.species : (i + 1) * z.species, :] = c_ref[
                pl.ds(y * z.nz + i, z.species, stride=z.tiles), :
            ]
        start = y * z.nz if isinstance(y, int) else pl.multiple_of(y * z.nz, z.nz)
        ref[z.nz * z.species :, :] = k_ref[pl.ds(start, z.nz), :]


def x_coefficients(z, faces, rho, left_ref, right_ref, inverse_ref):
    lanes = lax.broadcasted_iota(jnp.int32, (z.species, z.nx), 1)
    group = 4
    for base in range(0, z.tiles, group):
        tiles = range(base, base + group)
        e, d = [], []
        for t in tiles:
            before = rho * spread(faces.at[0], t, z)
            after = rho * spread(faces.at[1], t, z)
            d.append(1.0 + (before + after))
            e.append(jnp.where(lanes == 0, 0.0, before))
        for level in range(z.levels):
            stride = 1 << level
            for i, t in enumerate(tiles):
                r = 1.0 / d[i]
                above = along_x(e[i], -stride, z.nx)
                left = e[i] * along_x(r, stride, z.nx)
                right = above * along_x(r, -stride, z.nx)
                left_ref[level, t] = left
                right_ref[level, t] = right
                d[i] = d[i] - e[i] * left - above * right
                e[i] = left * along_x(e[i], stride, z.nx)
        for i, t in enumerate(tiles):
            inverse_ref[t] = 1.0 / d[i]


def right_sides(z, c, z_halo, y_low, y_high, faces, arrhenius, proportions, sigma, left, right, inverse, f_ref):
    lanes = lax.broadcasted_iota(jnp.int32, (z.species, z.nx), 1)
    rate_x, rate_y, rate_z = 4.0 * sigma, 0.015 * sigma, 4096.0 * sigma
    group = 4
    weights = proportions[...]
    for base in range(0, z.tiles, group):
        tiles = range(base, base + group)
        values = [c(t) for t in tiles]
        reacting = jnp.concatenate(
            [arrhenius[t] * jnp.tanh(v) for t, v in zip(tiles, values)], axis=1
        )
        source = jnp.dot(
            weights, reacting, precision=lax.Precision.HIGHEST, preferred_element_type=F32
        )
        section, lap = [], []
        for i, t in enumerate(tiles):
            y, row = divmod(t, z.nz)
            v = values[i]
            z_before = c(t - 1) if row else z_halo(0, y)
            z_after = c(t + 1) if row < z.nz - 1 else z_halo(1, y)
            y_before = c(t - z.nz) if y else y_low(row)
            y_after = c(t + z.nz) if y < z.ny - 1 else y_high(row)
            x_before = jnp.where(lanes == 0, 0.0, along_x(v, 1, z.nx))
            x_after = jnp.where(lanes == z.nx - 1, 0.0, along_x(v, -1, z.nx))
            flux = [spread(faces.at[n], t, z) for n in range(6)]
            lap_x = rate_x * (flux[1] * (x_after - v) - flux[0] * (v - x_before))
            lap_y = rate_y * (flux[3] * (y_after - v) - flux[2] * (v - y_before))
            lap_z = rate_z * (flux[5] * (z_after - v) - flux[4] * (v - z_before))
            lap.append(lap_z)
            section.append(v + lap_x + lap_y + lap_z + source[:, i * z.nx : (i + 1) * z.nx])
        for level in range(z.levels):
            stride = 1 << level
            for i, t in enumerate(tiles):
                section[i] = (
                    section[i]
                    + left[level, t] * along_x(section[i], stride, z.nx)
                    + right[level, t] * along_x(section[i], -stride, z.nx)
                )
        for i, t in enumerate(tiles):
            f_ref[t] = section[i] * inverse[t] - 0.5 * lap[i]


def local_lines(z, me, f_ref, m_ref, n_ref, g_ref, x_ref, ends_ref, pay_ref):
    for y in range(z.ny):
        base = y * z.nz
        forward = [f_ref[base]]
        for i in range(1, z.nz):
            forward.append(f_ref[base + i] + m_ref[base + i] * forward[-1])
        backward = f_ref[base + z.nz - 1]
        for i in reversed(range(z.nz)):
            t = base + i
            f = f_ref[t]
            if i < z.nz - 1:
                backward = f + n_ref[t] * backward
            x_ref[t] = (forward[i] + backward - f) * g_ref[t]
        first, last = backward, forward[-1]
        ends_ref[y] = first
        ends_ref[z.ny + y] = last

        def fill(dest, carry):
            pay_ref[dest, y * z.species : (y + 1) * z.species, :] = jnp.where(dest > me, last, first)
            return carry

        z.loop(0, z.devices, fill, 0)


def first_kernel(
    z,
    c_ref,
    k_ref,
    warm_ref,
    sigma_ref,
    frequency_ref,
    barrier_ref,
    proportions_ref,
    gathered,
    *refs,
):
    halos = 1 if z.gy == 2 else 2
    received = refs[:halos]
    (
        pay_ref,
        x_ref,
        ends_ref,
        m_ref,
        n_ref,
        g_ref,
        gm_ref,
        gn_ref,
        carry_ref,
        edge_ref,
        left_ref,
        right_ref,
        inverse_ref,
        arrhenius_ref,
        faces,
        all_faces,
        alpha_at,
        gamma_at,
        transfer_back,
        f_ref,
    ) = refs[halos:]
    me = lax.axis_index("gz")
    shape = (z.species, z.nx)
    sigma = column(sigma_ref, z)
    frequency = column(frequency_ref, z)
    barrier = column(barrier_ref, z)

    heat = 1.0 - 1.0 / warm_ref[...]
    faces[4] = heat
    for t in range(z.tiles):
        arrhenius_ref[t] = frequency * jnp.exp(barrier * spread(faces.at[4], t, z))

    k = k_ref[...]
    lanes = lax.broadcasted_iota(jnp.int32, k.shape, 1)
    faces[0] = 0.5 * (k + jnp.where(lanes == 0, 0.0, along_x(k, 1, z.nx)))
    faces[1] = 0.5 * (k + jnp.where(lanes == z.nx - 1, 0.0, along_x(k, -1, z.nx)))
    (low, low_mask), (high, high_mask) = y_halo(received, z)
    k_base = z.nz * z.species
    below = jnp.concatenate([low[k_base:, :] * low_mask, k[: z.tiles - z.nz]], axis=0)
    above = jnp.concatenate([k[z.nz :], high[k_base:, :] * high_mask], axis=0)
    faces[2] = 0.5 * (k + below)
    faces[3] = 0.5 * (k + above)

    x_coefficients(z, faces, 4.0 * sigma, left_ref, right_ref, inverse_ref)

    rows = lax.broadcasted_iota(jnp.int32, (z.nz, z.nx), 0)
    for y in range(z.ny):

        def add_up(j, last):
            here = gathered[j, y * z.nz : (y + 1) * z.nz, :]
            shifted = jnp.where(rows == 0, last, pltpu.roll(here, 1, 0))
            all_faces[y, pl.ds(pl.multiple_of(j * z.nz, z.nz), z.nz), :] = here + shifted
            return jnp.broadcast_to(here[z.nz - 1 :, :], here.shape)

        last = z.loop(0, z.devices, add_up, jnp.zeros((z.nz, z.nx), F32))
        all_faces[y, z.devices * z.nz :, :] = last

    rho = 1024.0 * sigma

    def face(y, row):
        return rho * spread(all_faces.at[y], row, z)

    def sweep(j, state):
        state = list(state)
        back = z.devices - 1 - j
        for y in range(z.ny):
            alpha_at[j, y] = state[2 * y]
            gamma_at[back, y] = state[2 * y + 1]
        product = [jnp.ones(shape, F32)] * (2 * z.ny)
        for i in range(z.nz):
            for y in range(z.ny):
                for side in range(2):
                    n = 2 * y + side
                    row = j * z.nz + i if side == 0 else (back + 1) * z.nz - i
                    a = face(y, row)
                    grounded = 1.0 + state[n]
                    factor = a / (grounded + a)
                    product[n] = product[n] * factor
                    state[n] = factor * grounded
        for y in range(z.ny):
            carry_ref[j, y] = product[2 * y]
            transfer_back[back, y] = product[2 * y + 1]
        return tuple(state)

    lax.fori_loop(0, z.devices, sweep, (jnp.full(shape, LARGE, F32),) * (2 * z.ny))

    def keep_back(j, carry):
        carry_ref[j] = transfer_back[j]
        return carry

    lax.fori_loop(me + 1, z.devices, keep_back, 0)

    start = me * z.nz
    inner_low = jnp.where(me > 0, 1.0, 0.0).astype(F32)
    inner_high = jnp.where(me < z.devices - 1, 1.0, 0.0).astype(F32)
    for y in range(z.ny):
        base = y * z.nz
        a = [face(y, start + i) for i in range(z.nz + 1)]
        for i in range(z.nz):
            faces[4, base + i : base + i + 1, :] = 0.5 * all_faces[y, pl.ds(start + i, 1), :]
            faces[5, base + i : base + i + 1, :] = 0.5 * all_faces[y, pl.ds(start + i + 1, 1), :]
        alpha_in, gamma_in = alpha_at[me, y], gamma_at[me, y]
        alpha, down = [], []
        state = alpha_in
        through = jnp.ones(shape, F32)
        for i in range(z.nz):
            factor = a[i] / (1.0 + state + a[i])
            state = factor * (1.0 + state)
            through = through * factor
            m_ref[base + i] = factor
            alpha.append(state)
            down.append(through)
        state = gamma_in
        through = jnp.ones(shape, F32)
        for i in reversed(range(z.nz)):
            factor = a[i + 1] / (1.0 + state + a[i + 1])
            state = factor * (1.0 + state)
            through = through * factor
            n_ref[base + i] = factor
            g = 1.0 / (1.0 + alpha[i] + state)
            g_ref[base + i] = g
            gm_ref[base + i] = g * down[i]
            gn_ref[base + i] = g * through
        factor = a[0] / (1.0 + state + a[0])
        g = inner_low / (1.0 + alpha_in + factor * (1.0 + state))
        edge_ref[y] = g
        edge_ref[z.ny + y] = g * factor
        edge_ref[2 * z.ny + y] = through
        factor = a[z.nz] / (1.0 + alpha[-1] + a[z.nz])
        g = inner_high / (1.0 + gamma_in + factor * (1.0 + alpha[-1]))
        edge_ref[3 * z.ny + y] = g
        edge_ref[4 * z.ny + y] = g * factor
        edge_ref[5 * z.ny + y] = down[-1]

    def c(t):
        return c_ref[pl.ds(t, z.species, stride=z.tiles), :]

    def z_halo(side, y):
        base = z.tiles + y * z.species
        other = jnp.minimum(me + 1, z.devices - 1) if side else jnp.maximum(me - 1, 0)
        return gathered[other, base : base + z.species, :] * (inner_high if side else inner_low)

    def y_low(row):
        return low[row * z.species : (row + 1) * z.species, :] * low_mask

    def y_high(row):
        return high[row * z.species : (row + 1) * z.species, :] * high_mask

    right_sides(
        z, c, z_halo, y_low, y_high, faces, arrhenius_ref, proportions_ref, sigma,
        left_ref, right_ref, inverse_ref, f_ref,
    )
    local_lines(z, me, f_ref, m_ref, n_ref, g_ref, x_ref, ends_ref, pay_ref)


def incoming(z, me, received, carry_ref, y):
    lanes = slice(y * z.species, (y + 1) * z.species)
    zero = jnp.zeros((z.species, z.nx), F32)
    below = lax.fori_loop(0, me, lambda j, v: received[j, lanes, :] + carry_ref[j, y] * v, zero)

    def down(i, v):
        j = z.devices - 1 - i
        return received[j, lanes, :] + carry_ref[j, y] * v

    above = lax.fori_loop(0, z.devices - 1 - me, down, zero)
    return below, above


def middle_kernel(z, received, carry_ref, x_ref, gm_ref, gn_ref, ends_ref, edge_ref, c_ref, halo_ref, *y_refs):
    me = lax.axis_index("gz")
    for y in range(z.ny):
        below, above = incoming(z, me, received, carry_ref, y)
        for i in range(z.nz):
            t = y * z.nz + i
            c_ref[t] = x_ref[t] + gm_ref[t] * below + gn_ref[t] * above
        first = ends_ref[y] + edge_ref[2 * z.ny + y] * above
        last = ends_ref[z.ny + y] + edge_ref[5 * z.ny + y] * below
        halo_ref[y] = edge_ref[y] * below + edge_ref[z.ny + y] * first
        halo_ref[z.ny + y] = edge_ref[3 * z.ny + y] * above + edge_ref[4 * z.ny + y] * last
    if z.gy == 2:
        picks = [jnp.where(lax.axis_index("gy") == 1, 0, z.ny - 1)]
    else:
        picks = [z.ny - 1, 0]
    for ref, y in zip(y_refs, picks):
        for i in range(z.nz):
            ref[i * z.species : (i + 1) * z.species, :] = c_ref[y * z.nz + i]


def second_kernel(
    z, c_ref, halo_ref, sigma_ref, proportions_ref, faces, arrhenius_ref, left_ref, right_ref,
    inverse_ref, m_ref, n_ref, g_ref, *refs
):
    halos = 1 if z.gy == 2 else 2
    received = refs[:halos]
    pay_ref, x_ref, ends_ref, f_ref = refs[halos:]
    me = lax.axis_index("gz")
    sigma = column(sigma_ref, z)
    (low, low_mask), (high, high_mask) = y_halo(received, z)
    right_sides(
        z,
        lambda t: c_ref[t],
        lambda side, y: halo_ref[side * z.ny + y],
        lambda row: low[row * z.species : (row + 1) * z.species, :] * low_mask,
        lambda row: high[row * z.species : (row + 1) * z.species, :] * high_mask,
        faces, arrhenius_ref, proportions_ref, sigma, left_ref, right_ref, inverse_ref, f_ref,
    )
    local_lines(z, me, f_ref, m_ref, n_ref, g_ref, x_ref, ends_ref, pay_ref)


def last_kernel(z, received, carry_ref, x_ref, gm_ref, gn_ref, out_ref):
    me = lax.axis_index("gz")
    for y in range(z.ny):
        below, above = incoming(z, me, received, carry_ref, y)
        for i in range(z.nz):
            t = y * z.nz + i
            out_ref[pl.ds(t, z.species, stride=z.tiles), :] = (
                x_ref[t] + gm_ref[t] * below + gn_ref[t] * above
            )


def per_device(z, c, k, warm, sigma, frequency, barrier, proportions):
    vmem = pl.BlockSpec(memory_space=pltpu.VMEM)
    smem = pl.BlockSpec(memory_space=pltpu.SMEM)
    params = pltpu.CompilerParams(vmem_limit_bytes=48 * 2**20)

    def shaped(*shape):
        return jax.ShapeDtypeStruct(shape, F32)

    def call(kernel, outs, ins, scratch=()):
        return pl.pallas_call(
            functools.partial(kernel, z),
            out_shape=outs,
            in_specs=[spec for spec, _ in ins],
            out_specs=jax.tree.map(lambda _: vmem, outs),
            scratch_shapes=list(scratch),
            compiler_params=params,
        )(*[value for _, value in ins])

    def swap(sends):
        count = z.gy
        if count == 2:
            return [lax.ppermute(sends[0], "gy", [(0, 1), (1, 0)])]
        up = [(i, i + 1) for i in range(count - 1)]
        down = [(i + 1, i) for i in range(count - 1)]
        return [lax.ppermute(sends[0], "gy", up), lax.ppermute(sends[1], "gy", down)]

    c = c.reshape(z.species * z.tiles, z.nx)
    k = k.reshape(z.tiles, z.nx)
    warm = warm.reshape(z.tiles, z.nx)
    halos = 1 if z.gy == 2 else 2
    tile = (z.species, z.nx)
    block = shaped(z.tiles, *tile)

    pay, *sends = call(
        pack_kernel,
        [shaped(z.devices, z.tiles + z.lines, z.nx)] + [shaped(z.nz * (z.species + 1), z.nx)] * halos,
        [(vmem, c), (vmem, k)],
    )
    received = swap(sends)
    gathered = lax.all_to_all(pay, "gz", 0, 0, tiled=True)
    per_line = shaped(z.devices, z.lines, z.nx)
    (pay, x, ends, m, n, g, gm, gn, carry, edge, left, right, inverse, arrhenius, faces) = call(
        first_kernel,
        [
            per_line,
            block,
            shaped(2 * z.ny, *tile),
            block,
            block,
            block,
            block,
            block,
            shaped(z.devices, z.ny, *tile),
            shaped(6 * z.ny, *tile),
            shaped(z.levels, z.tiles, *tile),
            shaped(z.levels, z.tiles, *tile),
            block,
            block,
            shaped(6, z.tiles, z.nx),
        ],
        [
            (vmem, c),
            (vmem, k),
            (vmem, warm),
            (smem, sigma),
            (smem, frequency),
            (smem, barrier),
            (vmem, proportions),
            (vmem, gathered),
        ]
        + [(vmem, v) for v in received],
        [
            pltpu.VMEM((z.ny, z.devices * z.nz + z.nz, z.nx), F32),
            pltpu.VMEM((z.devices, z.ny, *tile), F32),
            pltpu.VMEM((z.devices, z.ny, *tile), F32),
            pltpu.VMEM((z.devices, z.ny, *tile), F32),
            pltpu.VMEM((z.tiles, *tile), F32),
        ],
    )
    for _ in range(STEPS - 1):
        below_above = lax.all_to_all(pay, "gz", 0, 0, tiled=True)
        c, halo, *sends = call(
            middle_kernel,
            [block, shaped(2 * z.ny, *tile)] + [shaped(z.nz * z.species, z.nx)] * halos,
            [(vmem, v) for v in (below_above, carry, x, gm, gn, ends, edge)],
        )
        received = swap(sends)
        pay, x, ends = call(
            second_kernel,
            [per_line, block, shaped(2 * z.ny, *tile)],
            [(vmem, c), (vmem, halo), (smem, sigma), (vmem, proportions)]
            + [(vmem, v) for v in (faces, arrhenius, left, right, inverse, m, n, g, *received)],
            [pltpu.VMEM((z.tiles, *tile), F32)],
        )
    below_above = lax.all_to_all(pay, "gz", 0, 0, tiled=True)
    out = call(
        last_kernel,
        shaped(z.species * z.tiles, z.nx),
        [(vmem, v) for v in (below_above, carry, x, gm, gn)],
    )
    return out.reshape(z.species, z.ny, z.nz, z.nx)


def solution(mesh):
    def device_program(starting_densities, *others):
        sizes = Sizes(mesh, starting_densities.shape)
        return per_device(sizes, starting_densities, *others)

    return jax.shard_map(
        device_program,
        mesh=mesh,
        in_specs=(
            P(None, "gy", "gz", None),
            P("gy", "gz", None),
            P("gy", "gz", None),
            P(),
            P(),
            P(),
            P(),
        ),
        out_specs=P(None, "gy", "gz", None),
        check_vma=False,
    )
```

```python
import functools

import jax
import jax.numpy as jnp
from jax import lax
from jax.experimental import pallas as pl
from jax.experimental.pallas import tpu as pltpu
from jax.sharding import PartitionSpec as P

STEPS = 2
F32 = jnp.float32


class Sizes:
    def __init__(self, mesh, block):
        self.species, self.ny, self.nz, self.nx = block
        self.tiles = self.ny * self.nz
        self.lines = self.ny * self.species
        self.devices = mesh.shape["gz"]
        self.gy = mesh.shape["gy"]
        self.levels = (self.nx - 1).bit_length()
        self.tile = (self.species, self.nx)

    def per_device(self, body):
        if self.devices <= 16:
            for j in range(self.devices):
                body(j)
        else:

            def step(j, carry):
                body(j)
                return carry

            lax.fori_loop(0, self.devices, step, 0)

    def groups(self, size):
        for base in range(0, self.tiles, size):
            yield range(base, min(base + size, self.tiles))


def column(ref, z):
    rows = lax.broadcasted_iota(jnp.int32, z.tile, 0)
    value = jnp.zeros(z.tile, F32)
    for s in range(z.species):
        value = jnp.where(rows == s, ref[s], value)
    return value


def spread(ref, row, z):
    return jnp.broadcast_to(ref[pl.ds(row, 1), :], z.tile)


def along_x(v, by, nx):
    return pltpu.roll(v, by % nx, v.ndim - 1)


def flag(condition):
    return jnp.where(condition, 1.0, 0.0).astype(F32)


def inner(axis, count):
    me = lax.axis_index(axis)
    return flag(me > 0), flag(me < count - 1)


def spread_kernel(z, k_ref, pay_ref):
    k = k_ref[...]

    def fill(dest):
        pay_ref[dest] = k

    z.per_device(fill)


def edges_kernel(z, c_ref, k_ref, up_ref, down_ref, *y_refs):
    for y in range(z.ny):
        lines = slice(y * z.species, (y + 1) * z.species)
        down_ref[lines, :] = c_ref[pl.ds(y * z.nz, z.species, stride=z.tiles), :]
        up_ref[lines, :] = c_ref[pl.ds(y * z.nz + z.nz - 1, z.species, stride=z.tiles), :]
    for ref, y in zip(y_refs, y_picks(z)):
        for i in range(z.nz):
            ref[i * z.species : (i + 1) * z.species, :] = c_ref[
                pl.ds(y * z.nz + i, z.species, stride=z.tiles), :
            ]
        start = y * z.nz if isinstance(y, int) else pl.multiple_of(y * z.nz, z.nz)
        ref[z.nz * z.species :, :] = k_ref[pl.ds(start, z.nz), :]


def y_picks(z):
    if z.gy == 2:
        return [jnp.where(lax.axis_index("gy") == 1, 0, z.ny - 1)]
    return [z.ny - 1, 0]


def setup_kernel(
    z, c_ref, k_ref, warm_ref, sigma_ref, frequency_ref, barrier_ref, proportions_ref,
    tiles_ref, rates_ref, faces, arrhenius_ref, left_ref, right_ref, inverse_ref, base_ref, heat_ref,
):
    sigma = column(sigma_ref, z)
    frequency = column(frequency_ref, z)
    barrier = column(barrier_ref, z)
    rates_ref[0] = 4.0 * sigma
    rates_ref[1] = 0.015 * sigma
    rates_ref[2] = 4096.0 * sigma
    rates_ref[3] = 1.0 / (1024.0 * sigma)
    heat_ref[...] = 1.0 - 1.0 / warm_ref[...]
    k = k_ref[...]
    lanes = lax.broadcasted_iota(jnp.int32, k.shape, 1)
    faces[0] = 0.5 * (k + jnp.where(lanes == 0, 0.0, along_x(k, 1, z.nx)))
    faces[1] = 0.5 * (k + jnp.where(lanes == z.nx - 1, 0.0, along_x(k, -1, z.nx)))
    for t in range(z.tiles):
        tiles_ref[t] = c_ref[pl.ds(t, z.species, stride=z.tiles), :]
        arrhenius_ref[t] = frequency * jnp.exp(barrier * spread(heat_ref, t, z))
    base_sides(z, tiles_ref, rates_ref, faces, arrhenius_ref, proportions_ref, base_ref)

    lanes = lax.broadcasted_iota(jnp.int32, z.tile, 1)
    rho = rates_ref[0]
    for tiles in z.groups(8):
        e, d = [], []
        for t in tiles:
            before = rho * spread(faces.at[0], t, z)
            after = rho * spread(faces.at[1], t, z)
            d.append(1.0 + (before + after))
            e.append(jnp.where(lanes == 0, 0.0, before))
        for level in range(z.levels):
            stride = 1 << level
            for i, t in enumerate(tiles):
                r = 1.0 / d[i]
                above = along_x(e[i], -stride, z.nx)
                left = e[i] * along_x(r, stride, z.nx)
                right = above * along_x(r, -stride, z.nx)
                left_ref[level, t] = left
                right_ref[level, t] = right
                d[i] = d[i] - e[i] * left - above * right
                e[i] = left * along_x(e[i], stride, z.nx)
        for i, t in enumerate(tiles):
            inverse_ref[t] = 1.0 / d[i]


def base_sides(z, tiles_ref, rates_ref, faces, arrhenius_ref, proportions_ref, base_ref):
    lanes = lax.broadcasted_iota(jnp.int32, z.tile, 1)
    rate = rates_ref[0]
    reacting = jnp.concatenate(
        [arrhenius_ref[t] * jnp.tanh(tiles_ref[t]) for t in range(z.tiles)], axis=1
    )
    source = jnp.dot(
        proportions_ref[...],
        reacting,
        precision=lax.Precision.HIGHEST,
        preferred_element_type=F32,
    )
    for t in range(z.tiles):
        v = tiles_ref[t]
        before = jnp.where(lanes == 0, 0.0, along_x(v, 1, z.nx))
        after = jnp.where(lanes == z.nx - 1, 0.0, along_x(v, -1, z.nx))
        lap = rate * (
            spread(faces.at[1], t, z) * (after - v) - spread(faces.at[0], t, z) * (v - before)
        )
        base_ref[t] = v + lap + source[:, t * z.nx : (t + 1) * z.nx]


def base_kernel(z, *refs):
    base_sides(z, *refs)


def right_sides(z, tiles_ref, base_ref, z_halo, y_halo, rates_ref, faces, left, right, inverse, f_ref):
    rate_y, rate_z = rates_ref[1], rates_ref[2]
    for tiles in z.groups(8):
        section, lap = [], []
        for t in tiles:
            y, row = divmod(t, z.nz)
            v = tiles_ref[t]
            z_before = tiles_ref[t - 1] if row else z_halo(0, y)
            z_after = tiles_ref[t + 1] if row < z.nz - 1 else z_halo(1, y)
            y_before = tiles_ref[t - z.nz] if y else y_halo(0, row)
            y_after = tiles_ref[t + z.nz] if y < z.ny - 1 else y_halo(1, row)
            flux = [spread(faces.at[n], t, z) for n in range(4)]
            lap_y = rate_y * (flux[1] * (y_after - v) - flux[0] * (v - y_before))
            lap_z = rate_z * (flux[3] * (z_after - v) - flux[2] * (v - z_before))
            lap.append(lap_z)
            section.append(base_ref[t] + lap_y + lap_z)
        for level in range(z.levels):
            stride = 1 << level
            for i, t in enumerate(tiles):
                section[i] = (
                    section[i]
                    + left[level, t] * along_x(section[i], stride, z.nx)
                    + right[level, t] * along_x(section[i], -stride, z.nx)
                )
        for i, t in enumerate(tiles):
            f_ref[t] = section[i] * inverse[t] - 0.5 * lap[i]


def send_sums(z, f_ref, v_ref, u_ref, pay_ref):
    me = lax.axis_index("gz")
    for y in range(z.ny):
        tiles = range(y * z.nz, (y + 1) * z.nz)
        up = functools.reduce(jnp.add, [v_ref[t] * f_ref[t] for t in tiles])
        down = functools.reduce(jnp.add, [u_ref[t] * f_ref[t] for t in tiles])
        lines = slice(y * z.species, (y + 1) * z.species)

        def fill(dest):
            pay_ref[dest, lines, :] = jnp.where(dest > me, up, down)

        z.per_device(fill)
    pay_ref[me] = jnp.zeros((z.lines, z.nx), F32)


def first_kernel(
    z, gathered, k_ref, from_below, from_above, tiles_ref, base_ref, rates_ref, left_ref, right_ref,
    inverse_ref, *refs
):
    halos = 1 if z.gy == 2 else 2
    y_received = refs[:halos]
    pay_ref, f_ref, v_ref, u_ref, ends_ref, faces, resistance = refs[halos:]
    me = lax.axis_index("gz")
    k = k_ref[...]
    low, high = y_received[0], y_received[-1]
    low_mask, high_mask = inner("gy", z.gy)
    k_base = z.nz * z.species
    below = jnp.concatenate([low[k_base:, :] * low_mask, k[: z.tiles - z.nz]], axis=0)
    above = jnp.concatenate([k[z.nz :], high[k_base:, :] * high_mask], axis=0)
    faces[0] = 0.5 * (k + below)
    faces[1] = 0.5 * (k + above)

    rows = lax.broadcasted_iota(jnp.int32, (z.nz, z.nx), 0)
    for y in range(z.ny):
        base = y * z.nz

        def invert(j):
            here = gathered[j, base : base + z.nz, :]
            before = gathered[jnp.maximum(j - 1, 0), base + z.nz - 1 : base + z.nz, :]
            before = jnp.broadcast_to(jnp.where(j > 0, before, 0.0), here.shape)
            total = here + jnp.where(rows == 0, before, pltpu.roll(here, 1, 0))
            resistance[y, pl.ds(pl.multiple_of(j * z.nz, z.nz), z.nz), :] = 1.0 / total

        z.per_device(invert)
        last = gathered[z.devices - 1, base + z.nz - 1 : base + z.nz, :]
        resistance[y, z.devices * z.nz :, :] = jnp.broadcast_to(1.0 / last, (z.nz, z.nx))

    per_species = rates_ref[3]

    def ohm(y, row):
        return per_species * spread(resistance.at[y], row, z)

    def advance(state, row):
        out = []
        for y in range(z.ny):
            v, w = state[2 * y : 2 * y + 2]
            v = v + w * ohm(y, row)
            out += [v, w + v]
        return tuple(out)

    def forward(j, state):
        for i in range(z.nz):
            state = advance(state, j * z.nz + i)
        return state

    def backward(j, state):
        for i in range(z.nz):
            state = advance(state, (z.devices - j) * z.nz - i)
        return state

    start = (jnp.zeros(z.tile, F32), jnp.ones(z.tile, F32)) * z.ny
    first = me * z.nz
    state = lax.fori_loop(0, me, forward, start)
    rising = []
    for y in range(z.ny):
        ends_ref[y] = state[2 * y]
    for i in range(z.nz + 1):
        state = advance(state, first + i)
        rising.append(state)
    for y in range(z.ny):
        ends_ref[z.ny + y] = state[2 * y]
        for i in range(z.nz):
            v_ref[y * z.nz + i] = rising[i][2 * y]
            row = first + i
            faces[2, y * z.nz + i : y * z.nz + i + 1, :] = 0.5 / resistance[y, pl.ds(row, 1), :]
            faces[3, y * z.nz + i : y * z.nz + i + 1, :] = 0.5 / resistance[y, pl.ds(row + 1, 1), :]
    state = lax.fori_loop(0, z.devices - 1 - me, backward, start)
    for y in range(z.ny):
        ends_ref[3 * z.ny + y] = state[2 * y]
    for i in reversed(range(z.nz)):
        state = advance(state, first + i + 1)
        for y in range(z.ny):
            u_ref[y * z.nz + i] = state[2 * y]
            if i == 0:
                u, wu = state[2 * y : 2 * y + 2]
                v, wv = rising[0][2 * y : 2 * y + 2]
                ends_ref[4 * z.ny + y] = 1.0 / (wv * u + v * (wu - u))
    state = advance(state, first)
    for y in range(z.ny):
        ends_ref[2 * z.ny + y] = state[2 * y]

    z_low, z_high = inner("gz", z.devices)

    def z_halo(side, y):
        lines = slice(y * z.species, (y + 1) * z.species)
        return from_above[lines, :] * z_high if side else from_below[lines, :] * z_low

    def y_halo(side, row):
        lines = slice(row * z.species, (row + 1) * z.species)
        return high[lines, :] * high_mask if side else low[lines, :] * low_mask

    right_sides(
        z, tiles_ref, base_ref, z_halo, y_halo, rates_ref, faces, left_ref, right_ref, inverse_ref, f_ref
    )
    send_sums(z, f_ref, v_ref, u_ref, pay_ref)


def solve_lines(z, received, f_ref, v_ref, u_ref, ends_ref, store):
    me = lax.axis_index("gz")
    halos = []
    for y in range(z.ny):
        lines = slice(y * z.species, (y + 1) * z.species)
        zero = jnp.zeros(z.tile, F32)
        sums = [zero, zero]

        def add(j, pair):
            value = received[j, lines, :]
            lower = j < me
            return [pair[0] + jnp.where(lower, value, 0.0), pair[1] + jnp.where(lower, 0.0, value)]

        if z.devices <= 16:
            for j in range(z.devices):
                sums = add(j, sums)
        else:
            sums = lax.fori_loop(0, z.devices, add, sums)
        below, above = sums
        scale = ends_ref[4 * z.ny + y]
        tiles = range(y * z.nz, (y + 1) * z.nz)
        after = {}
        total = above
        for t in reversed(tiles):
            after[t] = total
            total = total + u_ref[t] * f_ref[t]
        low = scale * (ends_ref[2 * z.ny + y] * below + ends_ref[y] * total)
        total = below
        for t in tiles:
            total = total + v_ref[t] * f_ref[t]
            store(t, scale * (u_ref[t] * total + v_ref[t] * after[t]))
        high = scale * (ends_ref[3 * z.ny + y] * total + ends_ref[z.ny + y] * above)
        halos.append((low, high))
    return halos


def middle_kernel(z, received, f_ref, v_ref, u_ref, ends_ref, tiles_ref, halo_ref, *y_refs):
    def store(t, value):
        tiles_ref[t] = value

    for y, (low, high) in enumerate(solve_lines(z, received, f_ref, v_ref, u_ref, ends_ref, store)):
        halo_ref[y] = low
        halo_ref[z.ny + y] = high
    for ref, y in zip(y_refs, y_picks(z)):
        for i in range(z.nz):
            ref[i * z.species : (i + 1) * z.species, :] = tiles_ref[y * z.nz + i]


def second_kernel(
    z, tiles_ref, base_ref, halo_ref, rates_ref, faces, left_ref, right_ref, inverse_ref, v_ref, u_ref,
    *refs
):
    halos = 1 if z.gy == 2 else 2
    low, high = refs[0], refs[halos - 1]
    pay_ref, f_ref = refs[halos:]
    low_mask, high_mask = inner("gy", z.gy)

    def y_halo(side, row):
        lines = slice(row * z.species, (row + 1) * z.species)
        return high[lines, :] * high_mask if side else low[lines, :] * low_mask

    right_sides(
        z, tiles_ref, base_ref, lambda side, y: halo_ref[side * z.ny + y], y_halo, rates_ref, faces,
        left_ref, right_ref, inverse_ref, f_ref,
    )
    send_sums(z, f_ref, v_ref, u_ref, pay_ref)


def last_kernel(z, received, f_ref, v_ref, u_ref, ends_ref, out_ref):
    def store(t, value):
        out_ref[pl.ds(t, z.species, stride=z.tiles), :] = value

    solve_lines(z, received, f_ref, v_ref, u_ref, ends_ref, store)


def per_device(z, c, k, warm, sigma, frequency, barrier, proportions):
    vmem = pl.BlockSpec(memory_space=pltpu.VMEM)
    smem = pl.BlockSpec(memory_space=pltpu.SMEM)
    params = pltpu.CompilerParams(vmem_limit_bytes=48 * 2**20)

    def shaped(*shape):
        return jax.ShapeDtypeStruct(shape, F32)

    def call(kernel, outs, ins, scratch=(), flops=1000000):
        specs = [spec for spec, _ in ins]
        return pl.pallas_call(
            functools.partial(kernel, z),
            out_shape=outs,
            in_specs=specs,
            out_specs=jax.tree.map(lambda _: vmem, outs),
            scratch_shapes=list(scratch),
            compiler_params=params,
            cost_estimate=pl.CostEstimate(flops=flops, bytes_accessed=1000000, transcendentals=0),
        )(*[value for _, value in ins])

    def shift(value, axis, by):
        count = lax.axis_size(axis)
        return lax.ppermute(value, axis, [(i, (i + by) % count) for i in range(count)])

    def swap(sends):
        return [shift(value, "gy", by) for value, by in zip(sends, (1, -1))]

    def in_vmem(*values):
        return [(vmem, value) for value in values]

    c = c.reshape(z.species * z.tiles, z.nx)
    k = k.reshape(z.tiles, z.nx)
    warm = warm.reshape(z.tiles, z.nx)
    halos = 1 if z.gy == 2 else 2
    block = shaped(z.tiles, *z.tile)
    per_line = shaped(z.devices, z.lines, z.nx)

    pay = call(spread_kernel, shaped(z.devices, z.tiles, z.nx), in_vmem(k))
    gathered = lax.all_to_all(pay, "gz", 0, 0, tiled=True)
    up, down, *sends = call(
        edges_kernel,
        [shaped(z.lines, z.nx)] * 2 + [shaped(z.nz * (z.species + 1), z.nx)] * halos,
        in_vmem(c, k),
    )
    from_below, from_above = shift(up, "gz", 1), shift(down, "gz", -1)
    received = swap(sends)
    tiles, rates, x_faces, arrhenius, left, right, inverse, base = call(
        setup_kernel,
        [
            block,
            shaped(4, *z.tile),
            shaped(2, z.tiles, z.nx),
            block,
            shaped(z.levels, z.tiles, *z.tile),
            shaped(z.levels, z.tiles, *z.tile),
            block,
            block,
        ],
        in_vmem(c, k, warm)
        + [(smem, sigma), (smem, frequency), (smem, barrier)]
        + in_vmem(proportions),
        [pltpu.VMEM((z.tiles, z.nx), F32)],
    )
    pay, f, v, u, ends, faces = call(
        first_kernel,
        [per_line, block, block, block, shaped(5 * z.ny, *z.tile), shaped(4, z.tiles, z.nx)],
        in_vmem(gathered, k, from_below, from_above, tiles, base, rates, left, right, inverse, *received),
        [pltpu.VMEM((z.ny, z.devices * z.nz + z.nz, z.nx), F32)],
    )
    for _ in range(STEPS - 1):
        sums = lax.all_to_all(pay, "gz", 0, 0, tiled=True)
        tiles, halo, *sends = call(
            middle_kernel,
            [block, shaped(2 * z.ny, *z.tile)] + [shaped(z.nz * z.species, z.nx)] * halos,
            in_vmem(sums, f, v, u, ends),
        )
        received = swap(sends)
        base = call(base_kernel, block, in_vmem(tiles, rates, x_faces, arrhenius, proportions))
        pay, f = call(
            second_kernel,
            [per_line, block],
            in_vmem(tiles, base, halo, rates, faces, left, right, inverse, v, u, *received),
        )
    sums = lax.all_to_all(pay, "gz", 0, 0, tiled=True)
    out = call(last_kernel, shaped(z.species * z.tiles, z.nx), in_vmem(sums, f, v, u, ends))
    return out.reshape(z.species, z.ny, z.nz, z.nx)


def solution(mesh):
    def device_program(starting_densities, *others):
        sizes = Sizes(mesh, starting_densities.shape)
        return per_device(sizes, starting_densities, *others)

    return jax.shard_map(
        device_program,
        mesh=mesh,
        in_specs=(
            P(None, "gy", "gz", None),
            P("gy", "gz", None),
            P("gy", "gz", None),
            P(),
            P(),
            P(),
            P(),
        ),
        out_specs=P(None, "gy", "gz", None),
        check_vma=False,
    )
```

```python
import functools

import jax
import jax.numpy as jnp
from jax import lax
from jax.experimental import pallas as pl
from jax.experimental.pallas import tpu as pltpu
from jax.sharding import PartitionSpec as P

STEPS = 2
F32 = jnp.float32


class Sizes:
    def __init__(self, mesh, block):
        self.species, self.ny, self.nz, self.nx = block
        self.tiles = self.ny * self.nz
        self.lines = self.ny * self.species
        self.devices = mesh.shape["gz"]
        self.gy = mesh.shape["gy"]
        self.levels = (self.nx - 1).bit_length()
        self.tile = (self.species, self.nx)
        padded = -(-self.ny // 8) * 8
        self.edge_rows = self.lines + padded
        self.members = 1 << (self.devices.bit_length() // 2)
        self.groups_z = self.devices // self.members
        self.faces_at = 2 * self.lines
        self.block_rows = self.faces_at + self.tiles + padded
        self.group_top = self.faces_at + self.members * self.tiles
        self.group_rows = self.group_top + padded

    def per_device(self, body):
        if self.devices <= 16:
            for j in range(self.devices):
                body(j)
        else:

            def step(j, carry):
                body(j)
                return carry

            lax.fori_loop(0, self.devices, step, 0)

    def groups(self, size):
        for base in range(0, self.tiles, size):
            yield range(base, min(base + size, self.tiles))


def column(ref, z):
    rows = lax.broadcasted_iota(jnp.int32, z.tile, 0)
    value = jnp.zeros(z.tile, F32)
    for s in range(z.species):
        value = jnp.where(rows == s, ref[s], value)
    return value


def spread(ref, row, z):
    return jnp.broadcast_to(ref[pl.ds(row, 1), :], z.tile)


def along_x(v, by, nx):
    return pltpu.roll(v, by % nx, v.ndim - 1)


def flag(condition):
    return jnp.where(condition, 1.0, 0.0).astype(F32)


def inner(axis, count):
    me = lax.axis_index(axis)
    return flag(me > 0), flag(me < count - 1)


def edges_kernel(z, c_ref, k_ref, up_ref, down_ref, *y_refs):
    for ref, row in ((down_ref, 0), (up_ref, z.nz - 1)):
        for y in range(z.ny):
            at = y * z.nz + row
            ref[y * z.species : (y + 1) * z.species, :] = c_ref[
                pl.ds(at, z.species, stride=z.tiles), :
            ]
            ref[z.lines + y : z.lines + y + 1, :] = k_ref[at : at + 1, :]
        ref[z.lines + z.ny :, :] = jnp.zeros((z.edge_rows - z.lines - z.ny, z.nx), F32)
    for ref, y in zip(y_refs, y_picks(z)):
        for i in range(z.nz):
            ref[i * z.species : (i + 1) * z.species, :] = c_ref[
                pl.ds(y * z.nz + i, z.species, stride=z.tiles), :
            ]
        start = y * z.nz if isinstance(y, int) else pl.multiple_of(y * z.nz, z.nz)
        ref[z.nz * z.species :, :] = k_ref[pl.ds(start, z.nz), :]


def y_picks(z):
    if z.gy == 2:
        return [jnp.where(lax.axis_index("gy") == 1, 0, z.ny - 1)]
    return [z.ny - 1, 0]


def setup_kernel(
    z, c_ref, k_ref, warm_ref, sigma_ref, frequency_ref, barrier_ref, proportions_ref,
    tiles_ref, rates_ref, faces, arrhenius_ref, left_ref, right_ref, inverse_ref, base_ref, heat_ref,
):
    sigma = column(sigma_ref, z)
    frequency = column(frequency_ref, z)
    barrier = column(barrier_ref, z)
    rates_ref[0] = 4.0 * sigma
    rates_ref[1] = 0.015 * sigma
    rates_ref[2] = 4096.0 * sigma
    rates_ref[3] = 1.0 / (1024.0 * sigma)
    heat_ref[...] = 1.0 - 1.0 / warm_ref[...]
    k = k_ref[...]
    lanes = lax.broadcasted_iota(jnp.int32, k.shape, 1)
    faces[0] = 0.5 * (k + jnp.where(lanes == 0, 0.0, along_x(k, 1, z.nx)))
    faces[1] = 0.5 * (k + jnp.where(lanes == z.nx - 1, 0.0, along_x(k, -1, z.nx)))
    for t in range(z.tiles):
        tiles_ref[t] = c_ref[pl.ds(t, z.species, stride=z.tiles), :]
        arrhenius_ref[t] = frequency * jnp.exp(barrier * spread(heat_ref, t, z))
    base_sides(z, tiles_ref, rates_ref, faces, arrhenius_ref, proportions_ref, base_ref)

    lanes = lax.broadcasted_iota(jnp.int32, z.tile, 1)
    rho = rates_ref[0]
    for tiles in z.groups(8):
        e, d = [], []
        for t in tiles:
            before = rho * spread(faces.at[0], t, z)
            after = rho * spread(faces.at[1], t, z)
            d.append(1.0 + (before + after))
            e.append(jnp.where(lanes == 0, 0.0, before))
        for level in range(z.levels):
            stride = 1 << level
            for i, t in enumerate(tiles):
                r = 1.0 / d[i]
                above = along_x(e[i], -stride, z.nx)
                left = e[i] * along_x(r, stride, z.nx)
                right = above * along_x(r, -stride, z.nx)
                left_ref[level, t] = left
                right_ref[level, t] = right
                d[i] = d[i] - e[i] * left - above * right
                e[i] = left * along_x(e[i], stride, z.nx)
        for i, t in enumerate(tiles):
            inverse_ref[t] = 1.0 / d[i]


def base_sides(z, tiles_ref, rates_ref, faces, arrhenius_ref, proportions_ref, base_ref):
    lanes = lax.broadcasted_iota(jnp.int32, z.tile, 1)
    rate = rates_ref[0]
    reacting = jnp.concatenate(
        [arrhenius_ref[t] * jnp.tanh(tiles_ref[t]) for t in range(z.tiles)], axis=1
    )
    source = jnp.dot(
        proportions_ref[...],
        reacting,
        precision=lax.Precision.HIGHEST,
        preferred_element_type=F32,
    )
    for t in range(z.tiles):
        v = tiles_ref[t]
        before = jnp.where(lanes == 0, 0.0, along_x(v, 1, z.nx))
        after = jnp.where(lanes == z.nx - 1, 0.0, along_x(v, -1, z.nx))
        lap = rate * (
            spread(faces.at[1], t, z) * (after - v) - spread(faces.at[0], t, z) * (v - before)
        )
        base_ref[t] = v + lap + source[:, t * z.nx : (t + 1) * z.nx]


def base_kernel(z, *refs):
    base_sides(z, *refs)


def right_sides(z, tiles_ref, base_ref, z_halo, y_halo, rates_ref, faces, left, right, inverse, f_ref):
    rate_y, rate_z = rates_ref[1], rates_ref[2]
    for tiles in z.groups(8):
        section, lap = [], []
        for t in tiles:
            y, row = divmod(t, z.nz)
            v = tiles_ref[t]
            z_before = tiles_ref[t - 1] if row else z_halo(0, y)
            z_after = tiles_ref[t + 1] if row < z.nz - 1 else z_halo(1, y)
            y_before = tiles_ref[t - z.nz] if y else y_halo(0, row)
            y_after = tiles_ref[t + z.nz] if y < z.ny - 1 else y_halo(1, row)
            flux = [spread(faces.at[n], t, z) for n in range(4)]
            lap_y = rate_y * (flux[1] * (y_after - v) - flux[0] * (v - y_before))
            lap_z = rate_z * (flux[3] * (z_after - v) - flux[2] * (v - z_before))
            lap.append(lap_z)
            section.append(base_ref[t] + lap_y + lap_z)
        for level in range(z.levels):
            stride = 1 << level
            for i, t in enumerate(tiles):
                section[i] = (
                    section[i]
                    + left[level, t] * along_x(section[i], stride, z.nx)
                    + right[level, t] * along_x(section[i], -stride, z.nx)
                )
        for i, t in enumerate(tiles):
            f_ref[t] = section[i] * inverse[t] - 0.5 * lap[i]


def send_sums(z, f_ref, v_ref, u_ref, pay_ref):
    me = lax.axis_index("gz")
    for y in range(z.ny):
        tiles = range(y * z.nz, (y + 1) * z.nz)
        up = functools.reduce(jnp.add, [v_ref[t] * f_ref[t] for t in tiles])
        down = functools.reduce(jnp.add, [u_ref[t] * f_ref[t] for t in tiles])
        lines = slice(y * z.species, (y + 1) * z.species)

        def fill(dest):
            pay_ref[dest, lines, :] = jnp.where(dest > me, up, down)

        z.per_device(fill)
    pay_ref[me] = jnp.zeros((z.lines, z.nx), F32)


def per_line(z, y):
    return slice(y * z.species, (y + 1) * z.species)


def first_kernel(
    z, k_ref, from_below, from_above, tiles_ref, base_ref, rates_ref, left_ref, right_ref, inverse_ref,
    *refs
):
    halos = 1 if z.gy == 2 else 2
    y_received = refs[:halos]
    pay_ref, f_ref, faces = refs[halos:]
    k = k_ref[...]
    low, high = y_received[0], y_received[-1]
    low_mask, high_mask = inner("gy", z.gy)
    k_base = z.nz * z.species
    below = jnp.concatenate([low[k_base:, :] * low_mask, k[: z.tiles - z.nz]], axis=0)
    above = jnp.concatenate([k[z.nz :], high[k_base:, :] * high_mask], axis=0)
    faces[0] = 0.5 * (k + below)
    faces[1] = 0.5 * (k + above)

    z_low, z_high = inner("gz", z.devices)
    rows = lax.broadcasted_iota(jnp.int32, (z.nz, z.nx), 0)
    pay_ref[z.faces_at + z.tiles :, :] = jnp.zeros((z.block_rows - z.faces_at - z.tiles, z.nx), F32)
    for y in range(z.ny):
        own = slice(y * z.nz, (y + 1) * z.nz)
        here = k[own]
        row = z.lines + y
        before = jnp.broadcast_to(from_below[row : row + 1, :] * z_low, here.shape)
        after = jnp.broadcast_to(from_above[row : row + 1, :] * z_high, here.shape)
        before = here + jnp.where(rows == 0, before, pltpu.roll(here, 1, 0))
        after = here + jnp.where(rows == z.nz - 1, after, pltpu.roll(here, z.nz - 1, 0))
        faces[2, own, :] = 0.5 * before
        faces[3, own, :] = 0.5 * after
        pay_ref[z.faces_at + y * z.nz : z.faces_at + (y + 1) * z.nz, :] = 1.0 / before
        top = z.faces_at + z.tiles + y
        pay_ref[top : top + 1, :] = 1.0 / after[z.nz - 1 :, :]

    def z_halo(side, y):
        lines = per_line(z, y)
        return from_above[lines, :] * z_high if side else from_below[lines, :] * z_low

    def y_halo(side, row):
        lines = per_line(z, row)
        return high[lines, :] * high_mask if side else low[lines, :] * low_mask

    right_sides(
        z, tiles_ref, base_ref, z_halo, y_halo, rates_ref, faces, left_ref, right_ref, inverse_ref, f_ref
    )
    ohms = rates_ref[3]
    zero, one = jnp.zeros(z.tile, F32), jnp.ones(z.tile, F32)
    for y in range(z.ny):
        p, q, first, second = (one, zero), (zero, one), zero, zero
        for i in range(z.nz):
            ohm = ohms * spread(pay_ref, z.faces_at + y * z.nz + i, z)
            p, q = advance(p, ohm), advance(q, ohm)
            f = f_ref[y * z.nz + i]
            first = first + p[0] * f
            second = second + q[0] * f
        pay_ref[per_line(z, y), :] = first
        pay_ref[per_line(z, z.ny + y), :] = second


def advance(state, ohm):
    v, w = state
    v = v + w * ohm
    return v, w + v


def merge_kernel(z, rates_ref, pay_ref, *refs):
    *received, group_ref, order = refs
    me = lax.axis_index("gz") % z.members
    order[me] = pay_ref[...]
    for i, ref in enumerate(received):
        order[me ^ (i + 1)] = ref[...]
    ohms = rates_ref[3]
    zero, one = jnp.zeros(z.tile, F32), jnp.ones(z.tile, F32)
    for y in range(z.ny):
        p, q, first, second = (one, zero), (zero, one), zero, zero
        for j in range(z.members):
            s1, s2 = order[j, per_line(z, y), :], order[j, per_line(z, z.ny + y), :]
            first = first + (p[0] * s1 + p[1] * s2)
            second = second + (q[0] * s1 + q[1] * s2)
            if j < z.members - 1:
                for i in range(z.nz):
                    ohm = ohms * spread(order.at[j], z.faces_at + y * z.nz + i, z)
                    p, q = advance(p, ohm), advance(q, ohm)
        group_ref[per_line(z, y), :] = first
        group_ref[per_line(z, z.ny + y), :] = second
    for j in range(z.members):
        start = z.faces_at + j * z.tiles
        group_ref[start : start + z.tiles, :] = order[j, z.faces_at : z.faces_at + z.tiles, :]
    group_ref[z.group_top :, :] = order[z.members - 1, z.faces_at + z.tiles :, :]


def both_ways(z, rates_ref, order, groups, v_ref, u_ref, ends_ref):
    me = lax.axis_index("gz")
    group, member = me // z.members, me % z.members
    ohms = rates_ref[3]
    zero, one = jnp.zeros(z.tile, F32), jnp.ones(z.tile, F32)
    ys = range(z.ny)

    def ohm(ref, row):
        return ohms * spread(ref, row, z)

    def totals(ref, y):
        return ref[per_line(z, y), :], ref[per_line(z, z.ny + y), :]

    def up_rows(ref, start, state):
        state = list(state)
        for i in range(z.nz):
            for y in ys:
                state[3 * y : 3 * y + 2] = advance(
                    state[3 * y : 3 * y + 2], ohm(ref, start + y * z.nz + i)
                )
        return tuple(state)

    def up_add(ref, state):
        state = list(state)
        for y in ys:
            s1, s2 = totals(ref, y)
            state[3 * y + 2] = state[3 * y + 2] + (state[3 * y] * s1 + state[3 * y + 1] * s2)
        return tuple(state)

    def up_group(g, state):
        ref = groups.at[g]
        return lax.fori_loop(
            0,
            z.members,
            lambda j, s: up_rows(ref, z.faces_at + j * z.tiles, s),
            up_add(ref, state),
        )

    def up_block(j, state):
        ref = order.at[j]
        return up_rows(ref, z.faces_at, up_add(ref, state))

    state = (zero, one, zero) * z.ny
    state = lax.fori_loop(0, group, up_group, state)
    state = lax.fori_loop(0, member, up_block, state)
    below, rising = [], []
    mine = order.at[member]
    for y in ys:
        pair = state[3 * y : 3 * y + 2]
        below.append(state[3 * y + 2])
        ends_ref[y] = pair[0]
        for i in range(z.nz):
            pair = advance(pair, ohm(mine, z.faces_at + y * z.nz + i))
            v_ref[y * z.nz + i] = pair[0]
            if i == 0:
                rising.append(pair)
        ends_ref[z.ny + y] = pair[0] + pair[1] * ohm(mine, z.faces_at + z.tiles + y)

    def down_rows(ref, start, state):
        state = list(state)
        for i in reversed(range(z.nz)):
            for y in ys:
                _, u, w, total = state[4 * y : 4 * y + 4]
                w = w + u
                state[4 * y : 4 * y + 4] = [u, u + w * ohm(ref, start + y * z.nz + i), w, total]
        return tuple(state)

    def down_add(ref, state):
        state = list(state)
        for y in ys:
            s1, s2 = totals(ref, y)
            state[4 * y + 3] = state[4 * y + 3] + (state[4 * y + 1] * s1 - state[4 * y + 2] * s2)
        return tuple(state)

    def down_group(i, state):
        ref = groups.at[z.groups_z - 1 - i]
        state = lax.fori_loop(
            0,
            z.members,
            lambda j, s: down_rows(ref, z.faces_at + (z.members - 1 - j) * z.tiles, s),
            state,
        )
        return down_add(ref, state)

    def down_block(i, state):
        ref = order.at[z.members - 1 - i]
        return down_add(ref, down_rows(ref, z.faces_at, state))

    state = ()
    for y in ys:
        state += (zero, ohm(groups.at[z.groups_z - 1], z.group_top + y), one, zero)
    state = lax.fori_loop(0, z.groups_z - 1 - group, down_group, state)
    state = lax.fori_loop(0, z.members - 1 - member, down_block, state)
    above = []
    for y in ys:
        last, u, w, total = state[4 * y : 4 * y + 4]
        above.append(total)
        ends_ref[3 * z.ny + y] = last
        for i in reversed(range(z.nz)):
            u_ref[y * z.nz + i] = u
            if i == 0:
                v, wv = rising[y]
                ends_ref[4 * z.ny + y] = 1.0 / (wv * u + v * w)
            w = w + u
            u = u + w * ohm(mine, z.faces_at + y * z.nz + i)
        ends_ref[2 * z.ny + y] = u
    return below, above


def gathered_sums(z, received):
    me = lax.axis_index("gz")
    below, above = [], []
    for y in range(z.ny):
        lines = per_line(z, y)
        zero = jnp.zeros(z.tile, F32)
        sums = [zero, zero]

        def add(j, pair):
            value = received[j, lines, :]
            lower = j < me
            return [pair[0] + jnp.where(lower, value, 0.0), pair[1] + jnp.where(lower, 0.0, value)]

        if z.devices <= 16:
            for j in range(z.devices):
                sums = add(j, sums)
        else:
            sums = lax.fori_loop(0, z.devices, add, sums)
        below.append(sums[0])
        above.append(sums[1])
    return below, above


def solve_lines(z, sums, f_ref, v_ref, u_ref, ends_ref, store):
    halos = []
    for y, (below, above) in enumerate(zip(*sums)):
        scale = ends_ref[4 * z.ny + y]
        tiles = range(y * z.nz, (y + 1) * z.nz)
        after = {}
        total = above
        for t in reversed(tiles):
            after[t] = total
            total = total + u_ref[t] * f_ref[t]
        low = scale * (ends_ref[2 * z.ny + y] * below + ends_ref[y] * total)
        total = below
        for t in tiles:
            total = total + v_ref[t] * f_ref[t]
            store(t, scale * (u_ref[t] * total + v_ref[t] * after[t]))
        high = scale * (ends_ref[3 * z.ny + y] * total + ends_ref[z.ny + y] * above)
        halos.append((low, high))
    return halos


def hand_on(z, halos, tiles_ref, halo_ref, y_refs):
    for y, (low, high) in enumerate(halos):
        halo_ref[y] = low
        halo_ref[z.ny + y] = high
    for ref, y in zip(y_refs, y_picks(z)):
        for i in range(z.nz):
            ref[i * z.species : (i + 1) * z.species, :] = tiles_ref[y * z.nz + i]


def meet_kernel(z, rates_ref, f_ref, pay_ref, own_group, *refs):
    inside, across = refs[: z.members - 1], refs[z.members - 1 : z.members + z.groups_z - 2]
    refs = refs[z.members + z.groups_z - 2 :]
    tiles_ref, halo_ref, v_ref, u_ref, ends_ref, *y_refs, order, groups = refs
    me = lax.axis_index("gz")
    group, member = me // z.members, me % z.members
    order[member] = pay_ref[...]
    for i, ref in enumerate(inside):
        order[member ^ (i + 1)] = ref[...]
    groups[group] = own_group[...]
    for i, ref in enumerate(across):
        groups[group ^ (i + 1)] = ref[...]
    sums = both_ways(z, rates_ref, order, groups, v_ref, u_ref, ends_ref)

    def store(t, value):
        tiles_ref[t] = value

    halos = solve_lines(z, sums, f_ref, v_ref, u_ref, ends_ref, store)
    hand_on(z, halos, tiles_ref, halo_ref, y_refs)


def middle_kernel(z, received, f_ref, v_ref, u_ref, ends_ref, tiles_ref, halo_ref, *y_refs):
    def store(t, value):
        tiles_ref[t] = value

    halos = solve_lines(z, gathered_sums(z, received), f_ref, v_ref, u_ref, ends_ref, store)
    hand_on(z, halos, tiles_ref, halo_ref, y_refs)


def second_kernel(
    z, tiles_ref, base_ref, halo_ref, rates_ref, faces, left_ref, right_ref, inverse_ref, v_ref, u_ref,
    *refs
):
    halos = 1 if z.gy == 2 else 2
    low, high = refs[0], refs[halos - 1]
    pay_ref, f_ref = refs[halos:]
    low_mask, high_mask = inner("gy", z.gy)

    def y_halo(side, row):
        lines = slice(row * z.species, (row + 1) * z.species)
        return high[lines, :] * high_mask if side else low[lines, :] * low_mask

    right_sides(
        z, tiles_ref, base_ref, lambda side, y: halo_ref[side * z.ny + y], y_halo, rates_ref, faces,
        left_ref, right_ref, inverse_ref, f_ref,
    )
    send_sums(z, f_ref, v_ref, u_ref, pay_ref)


def last_kernel(z, received, f_ref, v_ref, u_ref, ends_ref, out_ref):
    def store(t, value):
        out_ref[pl.ds(t, z.species, stride=z.tiles), :] = value

    solve_lines(z, gathered_sums(z, received), f_ref, v_ref, u_ref, ends_ref, store)


def per_device(z, c, k, warm, sigma, frequency, barrier, proportions):
    vmem = pl.BlockSpec(memory_space=pltpu.VMEM)
    smem = pl.BlockSpec(memory_space=pltpu.SMEM)
    params = pltpu.CompilerParams(vmem_limit_bytes=48 * 2**20)

    def shaped(*shape):
        return jax.ShapeDtypeStruct(shape, F32)

    def call(kernel, outs, ins, scratch=(), flops=1000000):
        specs = [spec for spec, _ in ins]
        return pl.pallas_call(
            functools.partial(kernel, z),
            out_shape=outs,
            in_specs=specs,
            out_specs=jax.tree.map(lambda _: vmem, outs),
            scratch_shapes=list(scratch),
            compiler_params=params,
            cost_estimate=pl.CostEstimate(flops=flops, bytes_accessed=1000000, transcendentals=0),
        )(*[value for _, value in ins])

    def shift(value, axis, by):
        count = lax.axis_size(axis)
        return lax.ppermute(value, axis, [(i, (i + by) % count) for i in range(count)])

    def swap(sends):
        return [shift(value, "gy", by) for value, by in zip(sends, (1, -1))]

    def in_vmem(*values):
        return [(vmem, value) for value in values]

    c = c.reshape(z.species * z.tiles, z.nx)
    k = k.reshape(z.tiles, z.nx)
    warm = warm.reshape(z.tiles, z.nx)
    halos = 1 if z.gy == 2 else 2
    block = shaped(z.tiles, *z.tile)
    per_peer = shaped(z.devices, z.lines, z.nx)
    ends_shape = shaped(5 * z.ny, *z.tile)
    current = [block, shaped(2 * z.ny, *z.tile)]
    y_edges = [shaped(z.nz * z.species, z.nx)] * halos

    def exchange(value, count, unit):
        pairs = [[(i, i ^ (k * unit)) for i in range(z.devices)] for k in range(1, count)]
        return [lax.ppermute(value, "gz", p) for p in pairs]

    up, down, *sends = call(
        edges_kernel,
        [shaped(z.edge_rows, z.nx)] * 2 + [shaped(z.nz * (z.species + 1), z.nx)] * halos,
        in_vmem(c, k),
    )
    from_below, from_above = shift(up, "gz", 1), shift(down, "gz", -1)
    received = swap(sends)
    tiles, rates, x_faces, arrhenius, left, right, inverse, base = call(
        setup_kernel,
        [
            block,
            shaped(4, *z.tile),
            shaped(2, z.tiles, z.nx),
            block,
            shaped(z.levels, z.tiles, *z.tile),
            shaped(z.levels, z.tiles, *z.tile),
            block,
            block,
        ],
        in_vmem(c, k, warm)
        + [(smem, sigma), (smem, frequency), (smem, barrier)]
        + in_vmem(proportions),
        [pltpu.VMEM((z.tiles, z.nx), F32)],
    )
    pay, f, faces = call(
        first_kernel,
        [shaped(z.block_rows, z.nx), block, shaped(4, z.tiles, z.nx)],
        in_vmem(k, from_below, from_above, tiles, base, rates, left, right, inverse, *received),
    )
    inside = exchange(pay, z.members, 1)
    group = call(
        merge_kernel,
        shaped(z.group_rows, z.nx),
        in_vmem(rates, pay, *inside),
        [pltpu.VMEM((z.members, z.block_rows, z.nx), F32)],
    )
    across = exchange(group, z.groups_z, z.members)
    tiles, halo, v, u, ends, *sends = call(
        meet_kernel,
        [*current, block, block, ends_shape, *y_edges],
        in_vmem(rates, f, pay, group, *inside, *across),
        [
            pltpu.VMEM((z.members, z.block_rows, z.nx), F32),
            pltpu.VMEM((z.groups_z, z.group_rows, z.nx), F32),
        ],
    )
    for step in range(1, STEPS):
        if step > 1:
            sums = lax.all_to_all(pay, "gz", 0, 0, tiled=True)
            tiles, halo, *sends = call(
                middle_kernel, [*current, *y_edges], in_vmem(sums, f, v, u, ends)
            )
        received = swap(sends)
        base = call(base_kernel, block, in_vmem(tiles, rates, x_faces, arrhenius, proportions))
        pay, f = call(
            second_kernel,
            [per_peer, block],
            in_vmem(tiles, base, halo, rates, faces, left, right, inverse, v, u, *received),
        )
    sums = lax.all_to_all(pay, "gz", 0, 0, tiled=True)
    out = call(last_kernel, shaped(z.species * z.tiles, z.nx), in_vmem(sums, f, v, u, ends))
    return out.reshape(z.species, z.ny, z.nz, z.nx)


def solution(mesh):
    def device_program(starting_densities, *others):
        sizes = Sizes(mesh, starting_densities.shape)
        return per_device(sizes, starting_densities, *others)

    return jax.shard_map(
        device_program,
        mesh=mesh,
        in_specs=(
            P(None, "gy", "gz", None),
            P("gy", "gz", None),
            P("gy", "gz", None),
            P(),
            P(),
            P(),
            P(),
        ),
        out_specs=P(None, "gy", "gz", None),
        check_vma=False,
    )
```

```python
import functools

import jax
import jax.numpy as jnp
from jax import lax
from jax.experimental import pallas as pl
from jax.experimental.pallas import tpu as pltpu
from jax.sharding import PartitionSpec as P

F32 = jnp.float32


class Sizes:
    def __init__(self, mesh, block):
        self.species, self.ny, self.nz, self.nx = block
        self.tiles = self.ny * self.nz
        self.lines = self.ny * self.species
        self.devices = mesh.shape["gz"]
        self.gy = mesh.shape["gy"]
        self.levels = (self.nx - 1).bit_length()
        self.tile = (self.species, self.nx)
        padded = -(-self.ny // 8) * 8
        self.edge_rows = self.lines + padded
        self.members = 1 << (self.devices.bit_length() // 2)
        self.groups_z = self.devices // self.members
        self.faces_at = 2 * self.lines
        self.block_rows = self.faces_at + self.tiles + padded
        self.group_top = self.faces_at + self.members * self.tiles
        self.group_rows = self.group_top + padded

    def groups(self, size):
        for base in range(0, self.tiles, size):
            yield range(base, min(base + size, self.tiles))


def column(ref, z):
    rows = lax.broadcasted_iota(jnp.int32, z.tile, 0)
    value = jnp.zeros(z.tile, F32)
    for s in range(z.species):
        value = jnp.where(rows == s, ref[s], value)
    return value


def spread(ref, row, z):
    return jnp.broadcast_to(ref[pl.ds(row, 1), :], z.tile)


def per_line(z, y):
    return slice(y * z.species, (y + 1) * z.species)


def along_x(v, by, nx):
    return pltpu.roll(v, by % nx, v.ndim - 1)


def flag(condition):
    return jnp.where(condition, 1.0, 0.0).astype(F32)


def inner(axis, count):
    me = lax.axis_index(axis)
    return flag(me > 0), flag(me < count - 1)


def edges_kernel(z, c_hbm, k_hbm, c_ref, k_ref, near_ref, far_ref, *refs):
    *y_refs, sems = refs
    loads = [
        pltpu.make_async_copy(k_hbm, k_ref, sems.at[0]),
        pltpu.make_async_copy(c_hbm, c_ref, sems.at[1]),
    ]
    for load in loads:
        load.start()
    for load in loads:
        load.wait()
    odd = lax.axis_index("gz") % 2
    for ref, row in ((near_ref, (1 - odd) * (z.nz - 1)), (far_ref, odd * (z.nz - 1))):
        for y in range(z.ny):
            at = y * z.nz + row
            ref[per_line(z, y), :] = c_ref[pl.ds(at, z.species, stride=z.tiles), :]
            ref[z.lines + y : z.lines + y + 1, :] = k_ref[pl.ds(at, 1), :]
        ref[z.lines + z.ny :, :] = jnp.zeros((z.edge_rows - z.lines - z.ny, z.nx), F32)
    for ref, y in zip(y_refs, y_picks(z)):
        for i in range(z.nz):
            ref[i * z.species : (i + 1) * z.species, :] = c_ref[
                pl.ds(y * z.nz + i, z.species, stride=z.tiles), :
            ]
        start = y * z.nz if isinstance(y, int) else pl.multiple_of(y * z.nz, z.nz)
        ref[z.nz * z.species :, :] = k_ref[pl.ds(start, z.nz), :]


def y_picks(z):
    if z.gy == 2:
        return [jnp.where(lax.axis_index("gy") == 1, 0, z.ny - 1)]
    return [z.ny - 1, 0]


def setup_kernel(
    z, c_ref, k_ref, warm_ref, sigma_ref, frequency_ref, barrier_ref, proportions_ref,
    tiles_ref, rates_ref, faces, arrhenius_ref, left_ref, right_ref, inverse_ref, base_ref, heat_ref,
):
    sigma = column(sigma_ref, z)
    frequency = column(frequency_ref, z)
    barrier = column(barrier_ref, z)
    rates_ref[0] = 4.0 * sigma
    rates_ref[1] = 0.015 * sigma
    rates_ref[2] = 4096.0 * sigma
    rates_ref[3] = 1.0 / (1024.0 * sigma)
    heat_ref[...] = 1.0 - 1.0 / warm_ref[...]
    k = k_ref[...]
    lanes = lax.broadcasted_iota(jnp.int32, k.shape, 1)
    faces[0] = 0.5 * (k + jnp.where(lanes == 0, 0.0, along_x(k, 1, z.nx)))
    faces[1] = 0.5 * (k + jnp.where(lanes == z.nx - 1, 0.0, along_x(k, -1, z.nx)))
    for t in range(z.tiles):
        tiles_ref[t] = c_ref[pl.ds(t, z.species, stride=z.tiles), :]
        arrhenius_ref[t] = frequency * jnp.exp(barrier * spread(heat_ref, t, z))
    base_sides(z, tiles_ref, rates_ref, faces, arrhenius_ref, proportions_ref, base_ref)

    lanes = lax.broadcasted_iota(jnp.int32, z.tile, 1)
    rho = rates_ref[0]
    for tiles in z.groups(8):
        e, d = [], []
        for t in tiles:
            before = rho * spread(faces.at[0], t, z)
            after = rho * spread(faces.at[1], t, z)
            d.append(1.0 + (before + after))
            e.append(jnp.where(lanes == 0, 0.0, before))
        for level in range(z.levels):
            stride = 1 << level
            for i, t in enumerate(tiles):
                r = 1.0 / d[i]
                above = along_x(e[i], -stride, z.nx)
                left = e[i] * along_x(r, stride, z.nx)
                right = above * along_x(r, -stride, z.nx)
                left_ref[level, t] = left
                right_ref[level, t] = right
                d[i] = d[i] - e[i] * left - above * right
                e[i] = left * along_x(e[i], stride, z.nx)
        for i, t in enumerate(tiles):
            inverse_ref[t] = 1.0 / d[i]


def base_sides(z, tiles_ref, rates_ref, faces, arrhenius_ref, proportions_ref, base_ref):
    lanes = lax.broadcasted_iota(jnp.int32, z.tile, 1)
    rate = rates_ref[0]
    reacting = jnp.concatenate(
        [arrhenius_ref[t] * jnp.tanh(tiles_ref[t]) for t in range(z.tiles)], axis=1
    )
    source = jnp.dot(
        proportions_ref[...],
        reacting,
        precision=lax.Precision.HIGHEST,
        preferred_element_type=F32,
    )
    for t in range(z.tiles):
        v = tiles_ref[t]
        before = jnp.where(lanes == 0, 0.0, along_x(v, 1, z.nx))
        after = jnp.where(lanes == z.nx - 1, 0.0, along_x(v, -1, z.nx))
        lap = rate * (
            spread(faces.at[1], t, z) * (after - v) - spread(faces.at[0], t, z) * (v - before)
        )
        base_ref[t] = v + lap + source[:, t * z.nx : (t + 1) * z.nx]


def base_kernel(z, *refs):
    base_sides(z, *refs)


def right_sides(z, tiles_ref, base_ref, z_halo, y_halo, rates_ref, faces, left, right, inverse, f_ref):
    rate_y, rate_z = rates_ref[1], rates_ref[2]
    for tiles in z.groups(8):
        section, lap = [], []
        for t in tiles:
            y, row = divmod(t, z.nz)
            v = tiles_ref[t]
            z_before = tiles_ref[t - 1] if row else z_halo(0, y)
            z_after = tiles_ref[t + 1] if row < z.nz - 1 else z_halo(1, y)
            y_before = tiles_ref[t - z.nz] if y else y_halo(0, row)
            y_after = tiles_ref[t + z.nz] if y < z.ny - 1 else y_halo(1, row)
            flux = [spread(faces.at[n], t, z) for n in range(4)]
            lap_y = rate_y * (flux[1] * (y_after - v) - flux[0] * (v - y_before))
            lap_z = rate_z * (flux[3] * (z_after - v) - flux[2] * (v - z_before))
            lap.append(lap_z)
            section.append(base_ref[t] + lap_y + lap_z)
        for level in range(z.levels):
            stride = 1 << level
            for i, t in enumerate(tiles):
                section[i] = (
                    section[i]
                    + left[level, t] * along_x(section[i], stride, z.nx)
                    + right[level, t] * along_x(section[i], -stride, z.nx)
                )
        for i, t in enumerate(tiles):
            f_ref[t] = section[i] * inverse[t] - 0.5 * lap[i]


def send_sums(z, f_ref, v_ref, u_ref, pay_ref):
    for y in range(z.ny):
        tiles = range(y * z.nz, (y + 1) * z.nz)
        pay_ref[0, per_line(z, y), :] = functools.reduce(jnp.add, [v_ref[t] * f_ref[t] for t in tiles])
        pay_ref[1, per_line(z, y), :] = functools.reduce(jnp.add, [u_ref[t] * f_ref[t] for t in tiles])


def total_kernel(z, pay_ref, *refs):
    inside = refs[: z.members - 1]
    within_ref, *out_refs = refs[z.members - 1 :]
    me = lax.axis_index("gz")
    group, member = me // z.members, me % z.members
    below = above = jnp.zeros((z.lines, z.nx), F32)
    rising, falling = pay_ref[0], pay_ref[1]
    for i, ref in enumerate(inside):
        lower = (member ^ (i + 1)) < member
        up, down = ref[0], ref[1]
        rising, falling = rising + up, falling + down
        below = below + jnp.where(lower, up, 0.0)
        above = above + jnp.where(lower, 0.0, down)
    within_ref[0] = below
    within_ref[1] = above
    for i, ref in enumerate(out_refs):
        ref[...] = jnp.where((group ^ (i + 1)) > group, rising, falling)


def first_kernel(
    z, k_ref, near_ref, far_ref, tiles_ref, base_ref, rates_ref, left_ref, right_ref, inverse_ref, *refs
):
    halos = 1 if z.gy == 2 else 2
    y_received = refs[:halos]
    pay_ref, f_ref, faces, from_below, from_above = refs[halos:]
    odd = lax.axis_index("gz") % 2 == 1
    from_below[...] = jnp.where(odd, near_ref[...], far_ref[...])
    from_above[...] = jnp.where(odd, far_ref[...], near_ref[...])
    k = k_ref[...]
    low, high = y_received[0], y_received[-1]
    low_mask, high_mask = inner("gy", z.gy)
    k_base = z.nz * z.species
    below = jnp.concatenate([low[k_base:, :] * low_mask, k[: z.tiles - z.nz]], axis=0)
    above = jnp.concatenate([k[z.nz :], high[k_base:, :] * high_mask], axis=0)
    faces[0] = 0.5 * (k + below)
    faces[1] = 0.5 * (k + above)

    z_low, z_high = inner("gz", z.devices)
    rows = lax.broadcasted_iota(jnp.int32, (z.nz, z.nx), 0)
    pay_ref[z.faces_at + z.tiles :, :] = jnp.zeros((z.block_rows - z.faces_at - z.tiles, z.nx), F32)
    for y in range(z.ny):
        own = slice(y * z.nz, (y + 1) * z.nz)
        here = k[own]
        row = z.lines + y
        before = jnp.broadcast_to(from_below[row : row + 1, :] * z_low, here.shape)
        after = jnp.broadcast_to(from_above[row : row + 1, :] * z_high, here.shape)
        before = here + jnp.where(rows == 0, before, pltpu.roll(here, 1, 0))
        after = here + jnp.where(rows == z.nz - 1, after, pltpu.roll(here, z.nz - 1, 0))
        faces[2, own, :] = 0.5 * before
        faces[3, own, :] = 0.5 * after
        pay_ref[z.faces_at + y * z.nz : z.faces_at + (y + 1) * z.nz, :] = 1.0 / before
        top = z.faces_at + z.tiles + y
        pay_ref[top : top + 1, :] = 1.0 / after[z.nz - 1 :, :]

    def z_halo(side, y):
        lines = per_line(z, y)
        return from_above[lines, :] * z_high if side else from_below[lines, :] * z_low

    def y_halo(side, row):
        lines = per_line(z, row)
        return high[lines, :] * high_mask if side else low[lines, :] * low_mask

    right_sides(
        z, tiles_ref, base_ref, z_halo, y_halo, rates_ref, faces, left_ref, right_ref, inverse_ref, f_ref
    )
    ohms = rates_ref[3]
    zero, one = jnp.zeros(z.tile, F32), jnp.ones(z.tile, F32)
    for y in range(z.ny):
        p, q, first, second = (one, zero), (zero, one), zero, zero
        for i in range(z.nz):
            ohm = ohms * spread(pay_ref, z.faces_at + y * z.nz + i, z)
            p, q = advance(p, ohm), advance(q, ohm)
            f = f_ref[y * z.nz + i]
            first = first + p[0] * f
            second = second + q[0] * f
        pay_ref[per_line(z, y), :] = first
        pay_ref[per_line(z, z.ny + y), :] = second


def advance(state, ohm):
    v, w = state
    v = v + w * ohm
    return v, w + v


def merge_kernel(z, rates_ref, pay_ref, *refs):
    *received, group_ref, order = refs
    me = lax.axis_index("gz") % z.members
    order[me] = pay_ref[...]
    for i, ref in enumerate(received):
        order[me ^ (i + 1)] = ref[...]
    ohms = rates_ref[3]
    zero, one = jnp.zeros(z.tile, F32), jnp.ones(z.tile, F32)
    for y in range(z.ny):
        p, q, first, second = (one, zero), (zero, one), zero, zero
        for j in range(z.members):
            s1, s2 = order[j, per_line(z, y), :], order[j, per_line(z, z.ny + y), :]
            first = first + (p[0] * s1 + p[1] * s2)
            second = second + (q[0] * s1 + q[1] * s2)
            if j < z.members - 1:
                for i in range(z.nz):
                    ohm = ohms * spread(order.at[j], z.faces_at + y * z.nz + i, z)
                    p, q = advance(p, ohm), advance(q, ohm)
        group_ref[per_line(z, y), :] = first
        group_ref[per_line(z, z.ny + y), :] = second
    for j in range(z.members):
        start = z.faces_at + j * z.tiles
        group_ref[start : start + z.tiles, :] = order[j, z.faces_at : z.faces_at + z.tiles, :]
    group_ref[z.group_top :, :] = order[z.members - 1, z.faces_at + z.tiles :, :]


def both_ways(z, rates_ref, order, groups, v_ref, u_ref, ends_ref):
    me = lax.axis_index("gz")
    group, member = me // z.members, me % z.members
    ohms = rates_ref[3]
    zero, one = jnp.zeros(z.tile, F32), jnp.ones(z.tile, F32)
    ys = range(z.ny)

    def ohm(ref, row):
        return ohms * spread(ref, row, z)

    def totals(ref, y):
        return ref[per_line(z, y), :], ref[per_line(z, z.ny + y), :]

    def up_rows(ref, start, state):
        state = list(state)
        for i in range(z.nz):
            for y in ys:
                state[3 * y : 3 * y + 2] = advance(
                    state[3 * y : 3 * y + 2], ohm(ref, start + y * z.nz + i)
                )
        return tuple(state)

    def up_add(ref, state):
        state = list(state)
        for y in ys:
            s1, s2 = totals(ref, y)
            state[3 * y + 2] = state[3 * y + 2] + (state[3 * y] * s1 + state[3 * y + 1] * s2)
        return tuple(state)

    def up_group(g, state):
        ref = groups.at[g]
        return lax.fori_loop(
            0,
            z.members,
            lambda j, s: up_rows(ref, z.faces_at + j * z.tiles, s),
            up_add(ref, state),
        )

    def up_block(j, state):
        ref = order.at[j]
        return up_rows(ref, z.faces_at, up_add(ref, state))

    state = (zero, one, zero) * z.ny
    state = lax.fori_loop(0, group, up_group, state)
    state = lax.fori_loop(0, member, up_block, state)
    below, rising = [], []
    mine = order.at[member]
    for y in ys:
        pair = state[3 * y : 3 * y + 2]
        below.append(state[3 * y + 2])
        ends_ref[y] = pair[0]
        for i in range(z.nz):
            pair = advance(pair, ohm(mine, z.faces_at + y * z.nz + i))
            v_ref[y * z.nz + i] = pair[0]
            if i == 0:
                rising.append(pair)
        ends_ref[z.ny + y] = pair[0] + pair[1] * ohm(mine, z.faces_at + z.tiles + y)

    def down_rows(ref, start, state):
        state = list(state)
        for i in reversed(range(z.nz)):
            for y in ys:
                _, u, w, total = state[4 * y : 4 * y + 4]
                w = w + u
                state[4 * y : 4 * y + 4] = [u, u + w * ohm(ref, start + y * z.nz + i), w, total]
        return tuple(state)

    def down_add(ref, state):
        state = list(state)
        for y in ys:
            s1, s2 = totals(ref, y)
            state[4 * y + 3] = state[4 * y + 3] + (state[4 * y + 1] * s1 - state[4 * y + 2] * s2)
        return tuple(state)

    def down_group(i, state):
        ref = groups.at[z.groups_z - 1 - i]
        state = lax.fori_loop(
            0,
            z.members,
            lambda j, s: down_rows(ref, z.faces_at + (z.members - 1 - j) * z.tiles, s),
            state,
        )
        return down_add(ref, state)

    def down_block(i, state):
        ref = order.at[z.members - 1 - i]
        return down_add(ref, down_rows(ref, z.faces_at, state))

    state = ()
    for y in ys:
        state += (zero, ohm(groups.at[z.groups_z - 1], z.group_top + y), one, zero)
    state = lax.fori_loop(0, z.groups_z - 1 - group, down_group, state)
    state = lax.fori_loop(0, z.members - 1 - member, down_block, state)
    above = []
    for y in ys:
        last, u, w, total = state[4 * y : 4 * y + 4]
        above.append(total)
        ends_ref[3 * z.ny + y] = last
        for i in reversed(range(z.nz)):
            u_ref[y * z.nz + i] = u
            if i == 0:
                v, wv = rising[y]
                ends_ref[4 * z.ny + y] = 1.0 / (wv * u + v * w)
            w = w + u
            u = u + w * ohm(mine, z.faces_at + y * z.nz + i)
        ends_ref[2 * z.ny + y] = u
    return below, above


def solve_lines(z, sums, f_ref, v_ref, u_ref, ends_ref, store):
    halos = []
    for y, (below, above) in enumerate(zip(*sums)):
        scale = ends_ref[4 * z.ny + y]
        tiles = range(y * z.nz, (y + 1) * z.nz)
        after = {}
        total = above
        for t in reversed(tiles):
            after[t] = total
            total = total + u_ref[t] * f_ref[t]
        low = scale * (ends_ref[2 * z.ny + y] * below + ends_ref[y] * total)
        total = below
        for t in tiles:
            total = total + v_ref[t] * f_ref[t]
            store(t, scale * (u_ref[t] * total + v_ref[t] * after[t]))
        high = scale * (ends_ref[3 * z.ny + y] * total + ends_ref[z.ny + y] * above)
        halos.append((low, high))
    return halos


def hand_on(z, halos, tiles_ref, halo_ref, y_refs):
    for y, (low, high) in enumerate(halos):
        halo_ref[y] = low
        halo_ref[z.ny + y] = high
    for ref, y in zip(y_refs, y_picks(z)):
        for i in range(z.nz):
            ref[i * z.species : (i + 1) * z.species, :] = tiles_ref[y * z.nz + i]


def meet_kernel(z, rates_ref, f_ref, pay_ref, own_group, *refs):
    inside, across = refs[: z.members - 1], refs[z.members - 1 : z.members + z.groups_z - 2]
    refs = refs[z.members + z.groups_z - 2 :]
    tiles_ref, halo_ref, v_ref, u_ref, ends_ref, *y_refs, order, groups = refs
    me = lax.axis_index("gz")
    group, member = me // z.members, me % z.members
    order[member] = pay_ref[...]
    for i, ref in enumerate(inside):
        order[member ^ (i + 1)] = ref[...]
    groups[group] = own_group[...]
    for i, ref in enumerate(across):
        groups[group ^ (i + 1)] = ref[...]
    sums = both_ways(z, rates_ref, order, groups, v_ref, u_ref, ends_ref)

    def store(t, value):
        tiles_ref[t] = value

    halos = solve_lines(z, sums, f_ref, v_ref, u_ref, ends_ref, store)
    hand_on(z, halos, tiles_ref, halo_ref, y_refs)


def second_kernel(
    z, tiles_ref, base_ref, halo_ref, rates_ref, faces, left_ref, right_ref, inverse_ref, v_ref, u_ref,
    *refs
):
    halos = 1 if z.gy == 2 else 2
    low, high = refs[0], refs[halos - 1]
    pay_ref, f_ref = refs[halos:]
    low_mask, high_mask = inner("gy", z.gy)

    def y_halo(side, row):
        lines = slice(row * z.species, (row + 1) * z.species)
        return high[lines, :] * high_mask if side else low[lines, :] * low_mask

    right_sides(
        z, tiles_ref, base_ref, lambda side, y: halo_ref[side * z.ny + y], y_halo, rates_ref, faces,
        left_ref, right_ref, inverse_ref, f_ref,
    )
    send_sums(z, f_ref, v_ref, u_ref, pay_ref)


def last_kernel(z, within_ref, f_ref, v_ref, u_ref, ends_ref, *refs):
    *across, out_ref = refs
    group = lax.axis_index("gz") // z.members
    below, above = within_ref[0], within_ref[1]
    for i, ref in enumerate(across):
        lower = (group ^ (i + 1)) < group
        value = ref[...]
        below = below + jnp.where(lower, value, 0.0)
        above = above + jnp.where(lower, 0.0, value)
    sums = [[v[per_line(z, y)] for y in range(z.ny)] for v in (below, above)]

    def store(t, value):
        out_ref[pl.ds(t, z.species, stride=z.tiles), :] = value

    solve_lines(z, sums, f_ref, v_ref, u_ref, ends_ref, store)


def per_device(z, c, k, warm, sigma, frequency, barrier, proportions):
    vmem = pl.BlockSpec(memory_space=pltpu.VMEM)
    smem = pl.BlockSpec(memory_space=pltpu.SMEM)
    params = pltpu.CompilerParams(vmem_limit_bytes=48 * 2**20)

    def shaped(*shape):
        return jax.ShapeDtypeStruct(shape, F32)

    def call(kernel, outs, ins, scratch=(), flops=1000000):
        specs = [spec for spec, _ in ins]
        return pl.pallas_call(
            functools.partial(kernel, z),
            out_shape=outs,
            in_specs=specs,
            out_specs=jax.tree.map(lambda _: vmem, outs),
            scratch_shapes=list(scratch),
            compiler_params=params,
            cost_estimate=pl.CostEstimate(flops=flops, bytes_accessed=1000000, transcendentals=0),
        )(*[value for _, value in ins])

    def shift(value, axis, by):
        count = lax.axis_size(axis)
        return lax.ppermute(value, axis, [(i, (i + by) % count) for i in range(count)])

    def swap(sends):
        return [shift(value, "gy", by) for value, by in zip(sends, (1, -1))]

    def in_vmem(*values):
        return [(vmem, value) for value in values]

    c = c.reshape(z.species * z.tiles, z.nx)
    k = k.reshape(z.tiles, z.nx)
    warm = warm.reshape(z.tiles, z.nx)
    halos = 1 if z.gy == 2 else 2
    block = shaped(z.tiles, *z.tile)
    ends_shape = shaped(5 * z.ny, *z.tile)

    def exchange(value, count, unit):
        values = value if isinstance(value, list) else [value] * (count - 1)
        pairs = [[(i, i ^ (k * unit)) for i in range(z.devices)] for k in range(1, count)]
        return [lax.ppermute(v, "gz", p) for v, p in zip(values, pairs)]

    def neighbours(near, far):
        last = z.devices - 1
        links = [(i, i + 1) for i in range(1, last, 2)]
        links = [pair for i, j in links for pair in ((i, j), (j, i))]
        ends = [(i, i) for i in (0, last)]
        far_pairs = [(i * z.gy + n, j * z.gy + n) for i, j in links for n in range(z.gy)]
        far_pairs += [(i * z.gy + n, j * z.gy + (n ^ 1)) for i, j in ends for n in range(z.gy)]
        return exchange(near, 2, 1)[0], lax.ppermute(far, ("gz", "gy"), far_pairs)

    c, k, near, far, *sends = pl.pallas_call(
        functools.partial(edges_kernel, z),
        out_shape=[shaped(z.species * z.tiles, z.nx), shaped(z.tiles, z.nx)]
        + [shaped(z.edge_rows, z.nx)] * 2
        + [shaped(z.nz * (z.species + 1), z.nx)] * halos,
        in_specs=[pl.BlockSpec(memory_space=pl.ANY)] * 2,
        out_specs=[vmem] * (4 + halos),
        scratch_shapes=[pltpu.SemaphoreType.DMA((2,))],
        compiler_params=params,
    )(c, k)
    received = swap(sends)
    near, far = neighbours(near, far)
    tiles, rates, x_faces, arrhenius, left, right, inverse, base = call(
        setup_kernel,
        [
            block,
            shaped(4, *z.tile),
            shaped(2, z.tiles, z.nx),
            block,
            shaped(z.levels, z.tiles, *z.tile),
            shaped(z.levels, z.tiles, *z.tile),
            block,
            block,
        ],
        in_vmem(c, k, warm)
        + [(smem, sigma), (smem, frequency), (smem, barrier)]
        + in_vmem(proportions),
        [pltpu.VMEM((z.tiles, z.nx), F32)],
    )
    pay, f, faces = call(
        first_kernel,
        [shaped(z.block_rows, z.nx), block, shaped(4, z.tiles, z.nx)],
        in_vmem(k, near, far, tiles, base, rates, left, right, inverse, *received),
        [pltpu.VMEM((z.edge_rows, z.nx), F32)] * 2,
    )
    inside = exchange(pay, z.members, 1)
    group = call(
        merge_kernel,
        shaped(z.group_rows, z.nx),
        in_vmem(rates, pay, *inside),
        [pltpu.VMEM((z.members, z.block_rows, z.nx), F32)],
    )
    across = exchange(group, z.groups_z, z.members)
    tiles, halo, v, u, ends, *sends = call(
        meet_kernel,
        [block, shaped(2 * z.ny, *z.tile), block, block, ends_shape]
        + [shaped(z.nz * z.species, z.nx)] * halos,
        in_vmem(rates, f, pay, group, *inside, *across),
        [
            pltpu.VMEM((z.members, z.block_rows, z.nx), F32),
            pltpu.VMEM((z.groups_z, z.group_rows, z.nx), F32),
        ],
    )

    received = swap(sends)
    base = call(base_kernel, block, in_vmem(tiles, rates, x_faces, arrhenius, proportions))
    pay, f = call(
        second_kernel,
        [shaped(2, z.lines, z.nx), block],
        in_vmem(tiles, base, halo, rates, faces, left, right, inverse, v, u, *received),
    )
    inside = exchange(pay, z.members, 1)
    within, *totals = call(
        total_kernel,
        [shaped(2, z.lines, z.nx)] + [shaped(z.lines, z.nx)] * (z.groups_z - 1),
        in_vmem(pay, *inside),
    )
    across = exchange(totals, z.groups_z, z.members)
    out = call(
        last_kernel,
        shaped(z.species * z.tiles, z.nx),
        in_vmem(within, f, v, u, ends, *across),
    )
    return out.reshape(z.species, z.ny, z.nz, z.nx)


def solution(mesh):
    def device_program(starting_densities, *others):
        sizes = Sizes(mesh, starting_densities.shape)
        return per_device(sizes, starting_densities, *others)

    return jax.shard_map(
        device_program,
        mesh=mesh,
        in_specs=(
            P(None, "gy", "gz", None),
            P("gy", "gz", None),
            P("gy", "gz", None),
            P(),
            P(),
            P(),
            P(),
        ),
        out_specs=P(None, "gy", "gz", None),
        check_vma=False,
    )
```

```python
import functools

import jax
import jax.numpy as jnp
from jax import lax
from jax.experimental import pallas as pl
from jax.experimental.pallas import tpu as pltpu
from jax.sharding import PartitionSpec as P

F32 = jnp.float32


class Sizes:
    def __init__(self, mesh, block):
        self.species, self.ny, self.nz, self.nx = block
        self.tiles = self.ny * self.nz
        self.lines = self.ny * self.species
        self.devices = mesh.shape["gz"]
        self.gy = mesh.shape["gy"]
        self.levels = (self.nx - 1).bit_length()
        self.tile = (self.species, self.nx)
        padded = -(-self.ny // 8) * 8
        self.edge_rows = self.lines + padded
        self.members = 1 << (self.devices.bit_length() // 2)
        self.groups_z = self.devices // self.members
        self.faces_at = 2 * self.lines
        self.block_rows = self.faces_at + self.tiles + padded
        self.group_top = self.faces_at + self.members * self.tiles
        self.group_rows = self.group_top + padded

    def conductance(self, arguments):
        start = self.species * self.tiles
        return arguments.at[start : start + self.tiles]

    def warmth(self, arguments):
        start = (self.species + 1) * self.tiles
        return arguments.at[start : start + self.tiles]

    def groups(self, size):
        for base in range(0, self.tiles, size):
            yield range(base, min(base + size, self.tiles))


def column(ref, z):
    square = (z.species, z.species)
    mine = lax.broadcasted_iota(jnp.int32, square, 0) == lax.broadcasted_iota(jnp.int32, square, 1)
    values = jnp.where(mine, jnp.broadcast_to(ref[...], square), 0.0)
    return jnp.broadcast_to(jnp.sum(values, axis=1, keepdims=True), z.tile)


def spread(ref, row, z):
    return jnp.broadcast_to(ref[pl.ds(row, 1), :], z.tile)


def per_line(z, y):
    return slice(y * z.species, (y + 1) * z.species)


def along_x(v, by, nx):
    return pltpu.roll(v, by % nx, v.ndim - 1)


def flag(condition):
    return jnp.where(condition, 1.0, 0.0).astype(F32)


def inner(axis, count):
    me = lax.axis_index(axis)
    return flag(me > 0), flag(me < count - 1)


def edges_kernel(z, c_ref, far_ref, near_ref, *y_refs):
    k_ref = z.conductance(c_ref)
    odd = lax.axis_index("gz") % 2
    for ref, row in ((near_ref, (1 - odd) * (z.nz - 1)), (far_ref, odd * (z.nz - 1))):
        for y in range(z.ny):
            at = y * z.nz + row
            ref[per_line(z, y), :] = c_ref[pl.ds(at, z.species, stride=z.tiles), :]
            ref[z.lines + y : z.lines + y + 1, :] = k_ref[pl.ds(at, 1), :]
        ref[z.lines + z.ny :, :] = jnp.zeros((z.edge_rows - z.lines - z.ny, z.nx), F32)
    for ref, y in zip(y_refs, y_picks(z)):
        for i in range(z.nz):
            ref[i * z.species : (i + 1) * z.species, :] = c_ref[
                pl.ds(y * z.nz + i, z.species, stride=z.tiles), :
            ]
        start = y * z.nz if isinstance(y, int) else pl.multiple_of(y * z.nz, z.nz)
        ref[z.nz * z.species :, :] = k_ref[pl.ds(start, z.nz), :]


def y_picks(z):
    if z.gy == 2:
        return [jnp.where(lax.axis_index("gy") == 1, 0, z.ny - 1)]
    return [z.ny - 1, 0]


def coefficients_kernel(z, arguments, sigma_ref, rates_ref, faces, left_ref, right_ref, inverse_ref):
    sigma = column(sigma_ref, z)
    rho = 4.0 * sigma
    rates_ref[0] = rho
    rates_ref[1] = 0.015 * sigma
    rates_ref[2] = 4096.0 * sigma
    rates_ref[3] = 1.0 / (1024.0 * sigma)
    k = z.conductance(arguments)[...]
    lanes = lax.broadcasted_iota(jnp.int32, k.shape, 1)
    faces[0] = 0.5 * (k + jnp.where(lanes == 0, 0.0, along_x(k, 1, z.nx)))
    faces[1] = 0.5 * (k + jnp.where(lanes == z.nx - 1, 0.0, along_x(k, -1, z.nx)))
    lanes = lax.broadcasted_iota(jnp.int32, z.tile, 1)
    tiles = range(z.tiles)
    e, d = [], []
    for t in tiles:
        before = rho * spread(faces.at[0], t, z)
        after = rho * spread(faces.at[1], t, z)
        d.append(1.0 + (before + after))
        e.append(jnp.where(lanes == 0, 0.0, before))
    for level in range(z.levels):
        stride = 1 << level
        half = 2 * stride == z.nx
        for t in tiles:
            r = 1.0 / d[t]
            above = along_x(e[t], -stride, z.nx)
            r_before = along_x(r, stride, z.nx)
            left = e[t] * r_before
            right = above * (r_before if half else along_x(r, -stride, z.nx))
            left_ref[level, t] = left + right if half else left
            if not half:
                right_ref[level, t] = right
            d[t] = d[t] - e[t] * left - above * right
            if not half:
                e[t] = left * along_x(e[t], stride, z.nx)
    for t in tiles:
        inverse_ref[t] = 1.0 / d[t]


def source_kernel(
    z, c_ref, frequency_ref, barrier_ref, proportions_ref, rates_ref, faces,
    tiles_ref, arrhenius_ref, base_ref, heat_ref,
):
    frequency, barrier = column(frequency_ref, z), column(barrier_ref, z)
    heat_ref[...] = 1.0 - 1.0 / z.warmth(c_ref)[...]
    for t in range(z.tiles):
        tiles_ref[t] = c_ref[pl.ds(t, z.species, stride=z.tiles), :]
        arrhenius_ref[t] = frequency * jnp.exp(barrier * spread(heat_ref, t, z))
    base_sides(z, tiles_ref, rates_ref, faces, arrhenius_ref, proportions_ref, base_ref)


def base_sides(z, tiles_ref, rates_ref, faces, arrhenius_ref, proportions_ref, base_ref):
    lanes = lax.broadcasted_iota(jnp.int32, z.tile, 1)
    rate = rates_ref[0]
    reacting = jnp.concatenate(
        [arrhenius_ref[t] * jnp.tanh(tiles_ref[t]) for t in range(z.tiles)], axis=1
    )
    source = jnp.dot(
        proportions_ref[...],
        reacting,
        precision=lax.Precision.HIGHEST,
        preferred_element_type=F32,
    )
    for t in range(z.tiles):
        v = tiles_ref[t]
        before = jnp.where(lanes == 0, 0.0, along_x(v, 1, z.nx))
        after = jnp.where(lanes == z.nx - 1, 0.0, along_x(v, -1, z.nx))
        lap = rate * (
            spread(faces.at[1], t, z) * (after - v) - spread(faces.at[0], t, z) * (v - before)
        )
        base_ref[t] = v + lap + source[:, t * z.nx : (t + 1) * z.nx]


def right_sides(z, places, tiles_ref, base_ref, z_halo, y_halo, rates_ref, y_faces, z_faces, left, right, inverse, f_ref):
    rate_y, rate_z = rates_ref[1], rates_ref[2]
    section, lap = [], []
    for y, row in places:
        t = y * z.nz + row
        v = tiles_ref[t]
        z_before = tiles_ref[t - 1] if row else z_halo(0, y)
        z_after = tiles_ref[t + 1] if row < z.nz - 1 else z_halo(1, y)
        if isinstance(y, int):
            y_before = tiles_ref[t - z.nz] if y else y_halo(0, row)
            y_after = tiles_ref[t + z.nz] if y < z.ny - 1 else y_halo(1, row)
        else:
            y_before = jnp.where(y > 0, tiles_ref[jnp.maximum(y - 1, 0) * z.nz + row], y_halo(0, row))
            y_after = jnp.where(
                y < z.ny - 1, tiles_ref[jnp.minimum(y + 1, z.ny - 1) * z.nz + row], y_halo(1, row)
            )
        flux = [spread(faces.at[n], t, z) for faces in (y_faces, z_faces) for n in range(2)]
        lap_y = rate_y * (flux[1] * (y_after - v) - flux[0] * (v - y_before))
        lap_z = rate_z * (flux[3] * (z_after - v) - flux[2] * (v - z_before))
        lap.append(lap_z)
        section.append(base_ref[t] + lap_y + lap_z)
    for level in range(z.levels):
        stride = 1 << level
        for i, (y, row) in enumerate(places):
            t = y * z.nz + row
            before = along_x(section[i], stride, z.nx)
            more = left[level, t] * before
            if 2 * stride < z.nx:
                more = more + right[level, t] * along_x(section[i], -stride, z.nx)
            section[i] = section[i] + more
    for i, (y, row) in enumerate(places):
        t = y * z.nz + row
        f_ref[t] = section[i] * inverse[t] - 0.5 * lap[i]


def y_halos(z, received):
    low, high = received[0], received[-1]
    low_mask, high_mask = inner("gy", z.gy)

    def halo(side, row):
        lines = per_line(z, row)
        return high[lines, :] * high_mask if side else low[lines, :] * low_mask

    return halo


def send_sums(z, f_ref, v_ref, u_ref, pay_ref):
    for y in range(z.ny):
        tiles = range(y * z.nz, (y + 1) * z.nz)
        pay_ref[0, per_line(z, y), :] = functools.reduce(jnp.add, [v_ref[t] * f_ref[t] for t in tiles])
        pay_ref[1, per_line(z, y), :] = functools.reduce(jnp.add, [u_ref[t] * f_ref[t] for t in tiles])


def total_kernel(z, pay_ref, *refs):
    inside = refs[: z.members - 1]
    within_ref, *out_refs = refs[z.members - 1 :]
    me = lax.axis_index("gz")
    group, member = me // z.members, me % z.members
    below = above = jnp.zeros((z.lines, z.nx), F32)
    rising, falling = pay_ref[0], pay_ref[1]
    for i, ref in enumerate(inside):
        lower = (member ^ (i + 1)) < member
        up, down = ref[0], ref[1]
        rising, falling = rising + up, falling + down
        below = below + jnp.where(lower, up, 0.0)
        above = above + jnp.where(lower, 0.0, down)
    within_ref[0] = below
    within_ref[1] = above
    for i, ref in enumerate(reversed(out_refs)):
        ref[...] = jnp.where((group ^ (i + 1)) > group, rising, falling)


def z_face_pair(z, k_ref, low, high):
    rows = lax.broadcasted_iota(jnp.int32, (z.nz, z.nx), 0)
    for y in range(z.ny):
        here = k_ref[y * z.nz : (y + 1) * z.nz, :]
        before, after = (jnp.broadcast_to(row, here.shape) for row in (low(y), high(y)))
        yield (
            here + jnp.where(rows == 0, before, pltpu.roll(here, 1, 0)),
            here + jnp.where(rows == z.nz - 1, after, pltpu.roll(here, z.nz - 1, 0)),
        )


def early_kernel(z, arguments, tiles_ref, base_ref, rates_ref, left_ref, right_ref, inverse_ref, *refs):
    halos = 1 if z.gy == 2 else 2
    received = refs[:halos]
    f_ref, y_faces, z_faces = refs[halos:]
    k_ref = z.conductance(arguments)
    k = k_ref[...]
    low, high = received[0], received[-1]
    low_mask, high_mask = inner("gy", z.gy)
    k_base = z.nz * z.species
    below = jnp.concatenate([low[k_base:, :] * low_mask, k[: z.tiles - z.nz]], axis=0)
    above = jnp.concatenate([k[z.nz :], high[k_base:, :] * high_mask], axis=0)
    y_faces[0] = 0.5 * (k + below)
    y_faces[1] = 0.5 * (k + above)
    nothing = jnp.zeros((1, z.nx), F32)
    for y, (before, after) in enumerate(z_face_pair(z, k_ref, lambda y: nothing, lambda y: nothing)):
        own = slice(y * z.nz, (y + 1) * z.nz)
        z_faces[0, own, :] = 0.5 * before
        z_faces[1, own, :] = 0.5 * after
    places = [(y, row) for y in range(z.ny) for row in range(1, z.nz - 1)]
    right_sides(
        z, places, tiles_ref, base_ref, None, y_halos(z, received), rates_ref, y_faces, z_faces,
        left_ref, right_ref, inverse_ref, f_ref,
    )


def first_kernel(
    z, arguments, far_ref, near_ref, tiles_ref, base_ref, rates_ref, left_ref, right_ref, inverse_ref,
    early_ref, y_faces, *refs
):
    halos = 1 if z.gy == 2 else 2
    received = refs[:halos]
    pay_ref, f_ref, z_faces, from_below, from_above = refs[halos:]
    k_ref = z.conductance(arguments)
    odd = lax.axis_index("gz") % 2 == 1
    from_below[...] = jnp.where(odd, near_ref[...], far_ref[...])
    from_above[...] = jnp.where(odd, far_ref[...], near_ref[...])
    z_low, z_high = inner("gz", z.devices)
    pay_ref[z.faces_at + z.tiles :, :] = jnp.zeros((z.block_rows - z.faces_at - z.tiles, z.nx), F32)

    def k_low(y):
        return from_below[z.lines + y : z.lines + y + 1, :] * z_low

    def k_high(y):
        return from_above[z.lines + y : z.lines + y + 1, :] * z_high

    for y, (before, after) in enumerate(z_face_pair(z, k_ref, k_low, k_high)):
        own = slice(y * z.nz, (y + 1) * z.nz)
        z_faces[0, own, :] = 0.5 * before
        z_faces[1, own, :] = 0.5 * after
        pay_ref[z.faces_at + y * z.nz : z.faces_at + (y + 1) * z.nz, :] = 1.0 / before
        top = z.faces_at + z.tiles + y
        pay_ref[top : top + 1, :] = 1.0 / after[z.nz - 1 :, :]

    def z_halo(side, y):
        lines = per_line(z, y)
        return from_above[lines, :] * z_high if side else from_below[lines, :] * z_low

    for y in range(z.ny):
        for row in range(1, z.nz - 1):
            f_ref[y * z.nz + row] = early_ref[y * z.nz + row]
    places = [(y, row) for y in range(z.ny) for row in sorted({0, z.nz - 1})]
    right_sides(
        z, places, tiles_ref, base_ref, z_halo, y_halos(z, received), rates_ref, y_faces, z_faces,
        left_ref, right_ref, inverse_ref, f_ref,
    )
    ohms = rates_ref[3]
    zero, one = jnp.zeros(z.tile, F32), jnp.ones(z.tile, F32)
    for y in range(z.ny):
        p, q, first, second = (one, zero), (zero, one), zero, zero
        for i in range(z.nz):
            ohm = ohms * spread(pay_ref, z.faces_at + y * z.nz + i, z)
            p, q = advance(p, ohm), advance(q, ohm)
            f = f_ref[y * z.nz + i]
            first = first + p[0] * f
            second = second + q[0] * f
        pay_ref[per_line(z, y), :] = first
        pay_ref[per_line(z, z.ny + y), :] = second


def advance(state, ohm):
    v, w = state
    v = v + w * ohm
    return v, w + v


def merge_kernel(z, rates_ref, pay_ref, *refs):
    *received, group_ref, order = refs
    me = lax.axis_index("gz") % z.members
    order[me] = pay_ref[...]
    for i, ref in enumerate(received):
        order[me ^ (i + 1)] = ref[...]
    ohms = rates_ref[3]
    zero, one = jnp.zeros(z.tile, F32), jnp.ones(z.tile, F32)
    for y in range(z.ny):
        p, q, first, second = (one, zero), (zero, one), zero, zero
        for j in range(z.members):
            s1, s2 = order[j, per_line(z, y), :], order[j, per_line(z, z.ny + y), :]
            first = first + (p[0] * s1 + p[1] * s2)
            second = second + (q[0] * s1 + q[1] * s2)
            if j < z.members - 1:
                for i in range(z.nz):
                    ohm = ohms * spread(order.at[j], z.faces_at + y * z.nz + i, z)
                    p, q = advance(p, ohm), advance(q, ohm)
        group_ref[per_line(z, y), :] = first
        group_ref[per_line(z, z.ny + y), :] = second
    for j in range(z.members):
        start = z.faces_at + j * z.tiles
        group_ref[start : start + z.tiles, :] = order[j, z.faces_at : z.faces_at + z.tiles, :]
    group_ref[z.group_top :, :] = order[z.members - 1, z.faces_at + z.tiles :, :]


def both_ways(z, rates_ref, order, groups, v_ref, u_ref, ends_ref):
    me = lax.axis_index("gz")
    group, member = me // z.members, me % z.members
    ohms = rates_ref[3]
    zero, one = jnp.zeros(z.tile, F32), jnp.ones(z.tile, F32)
    ys = range(z.ny)

    def ohm(ref, row):
        return ohms * spread(ref, row, z)

    def totals(ref, y):
        return ref[per_line(z, y), :], ref[per_line(z, z.ny + y), :]

    def up_rows(ref, start, state):
        state = list(state)
        for i in range(z.nz):
            for y in ys:
                state[3 * y : 3 * y + 2] = advance(
                    state[3 * y : 3 * y + 2], ohm(ref, start + y * z.nz + i)
                )
        return tuple(state)

    def up_add(ref, state):
        state = list(state)
        for y in ys:
            s1, s2 = totals(ref, y)
            state[3 * y + 2] = state[3 * y + 2] + (state[3 * y] * s1 + state[3 * y + 1] * s2)
        return tuple(state)

    def up_group(g, state):
        ref = groups.at[g]
        return lax.fori_loop(
            0,
            z.members,
            lambda j, s: up_rows(ref, z.faces_at + j * z.tiles, s),
            up_add(ref, state),
        )

    def up_block(j, state):
        ref = order.at[j]
        return up_rows(ref, z.faces_at, up_add(ref, state))

    state = (zero, one, zero) * z.ny
    state = lax.fori_loop(0, group, up_group, state)
    state = lax.fori_loop(0, member, up_block, state)
    below, rising = [], []
    mine = order.at[member]
    for y in ys:
        pair = state[3 * y : 3 * y + 2]
        below.append(state[3 * y + 2])
        ends_ref[y] = pair[0]
        for i in range(z.nz):
            pair = advance(pair, ohm(mine, z.faces_at + y * z.nz + i))
            v_ref[y * z.nz + i] = pair[0]
            if i == 0:
                rising.append(pair)
        ends_ref[z.ny + y] = pair[0] + pair[1] * ohm(mine, z.faces_at + z.tiles + y)

    def down_rows(ref, start, state):
        state = list(state)
        for i in reversed(range(z.nz)):
            for y in ys:
                _, u, w, total = state[4 * y : 4 * y + 4]
                w = w + u
                state[4 * y : 4 * y + 4] = [u, u + w * ohm(ref, start + y * z.nz + i), w, total]
        return tuple(state)

    def down_add(ref, state):
        state = list(state)
        for y in ys:
            s1, s2 = totals(ref, y)
            state[4 * y + 3] = state[4 * y + 3] + (state[4 * y + 1] * s1 - state[4 * y + 2] * s2)
        return tuple(state)

    def down_group(i, state):
        ref = groups.at[z.groups_z - 1 - i]
        state = lax.fori_loop(
            0,
            z.members,
            lambda j, s: down_rows(ref, z.faces_at + (z.members - 1 - j) * z.tiles, s),
            state,
        )
        return down_add(ref, state)

    def down_block(i, state):
        ref = order.at[z.members - 1 - i]
        return down_add(ref, down_rows(ref, z.faces_at, state))

    state = ()
    for y in ys:
        state += (zero, ohm(groups.at[z.groups_z - 1], z.group_top + y), one, zero)
    state = lax.fori_loop(0, z.groups_z - 1 - group, down_group, state)
    state = lax.fori_loop(0, z.members - 1 - member, down_block, state)
    above = []
    for y in ys:
        last, u, w, total = state[4 * y : 4 * y + 4]
        above.append(total)
        ends_ref[3 * z.ny + y] = last
        for i in reversed(range(z.nz)):
            u_ref[y * z.nz + i] = u
            if i == 0:
                v, wv = rising[y]
                ends_ref[4 * z.ny + y] = 1.0 / (wv * u + v * w)
            w = w + u
            u = u + w * ohm(mine, z.faces_at + y * z.nz + i)
        ends_ref[2 * z.ny + y] = u
    return below, above


def solve_lines(z, sums, f_ref, v_ref, u_ref, ends_ref, store, finish=None):
    halos = []
    for y, (below, above) in enumerate(zip(*sums)):
        scale = ends_ref[4 * z.ny + y]
        tiles = range(y * z.nz, (y + 1) * z.nz)
        after = {}
        total = above
        for t in reversed(tiles):
            after[t] = total
            total = total + u_ref[t] * f_ref[t]
        low = scale * (ends_ref[2 * z.ny + y] * below + ends_ref[y] * total)
        total = below
        for t in tiles:
            total = total + v_ref[t] * f_ref[t]
            store(t, scale * (u_ref[t] * total + v_ref[t] * after[t]))
        if finish:
            finish(y)
        high = scale * (ends_ref[3 * z.ny + y] * total + ends_ref[z.ny + y] * above)
        halos.append((low, high))
    return halos


def hand_on(z, halos, tiles_ref, halo_ref, y_refs):
    for y, (low, high) in enumerate(halos):
        halo_ref[y] = low
        halo_ref[z.ny + y] = high
    for ref, y in zip(y_refs, y_picks(z)):
        for i in range(z.nz):
            ref[i * z.species : (i + 1) * z.species, :] = tiles_ref[y * z.nz + i]


def meet_kernel(z, rates_ref, f_ref, pay_ref, own_group, *refs):
    inside, across = refs[: z.members - 1], refs[z.members - 1 : z.members + z.groups_z - 2]
    refs = refs[z.members + z.groups_z - 2 :]
    tiles_ref, halo_ref, v_ref, u_ref, ends_ref, *y_refs, order, groups = refs
    me = lax.axis_index("gz")
    group, member = me // z.members, me % z.members
    order[member] = pay_ref[...]
    for i, ref in enumerate(inside):
        order[member ^ (i + 1)] = ref[...]
    groups[group] = own_group[...]
    for i, ref in enumerate(across):
        groups[group ^ (i + 1)] = ref[...]
    sums = both_ways(z, rates_ref, order, groups, v_ref, u_ref, ends_ref)

    def store(t, value):
        tiles_ref[t] = value

    halos = solve_lines(z, sums, f_ref, v_ref, u_ref, ends_ref, store)
    hand_on(z, halos, tiles_ref, halo_ref, y_refs)


def halo_rows(z):
    if z.gy == 2:
        core = lax.axis_index("gy")
        return y_picks(z), [core + j for j in range(z.ny - 1)]
    return list(range(z.ny)), []


def places_of(z, ys):
    return [(y, row) for y in ys for row in range(z.nz)]


def inner_kernel(
    z, tiles_ref, halo_ref, rates_ref, x_faces, arrhenius_ref, proportions_ref, y_faces, z_faces,
    left_ref, right_ref, inverse_ref, base_ref, f_ref
):
    base_sides(z, tiles_ref, rates_ref, x_faces, arrhenius_ref, proportions_ref, base_ref)
    _, ys = halo_rows(z)
    zero = jnp.zeros(z.tile, F32)
    if ys:
        right_sides(
            z, places_of(z, ys), tiles_ref, base_ref, lambda side, y: halo_ref[side * z.ny + y],
            lambda side, row: zero, rates_ref, y_faces, z_faces, left_ref, right_ref, inverse_ref, f_ref,
        )


def second_kernel(
    z, tiles_ref, halo_ref, rates_ref, y_faces, z_faces, left_ref, right_ref, inverse_ref, base_ref,
    inner_ref, v_ref, u_ref, *refs
):
    halos = 1 if z.gy == 2 else 2
    received = refs[:halos]
    pay_ref, f_ref = refs[halos:]
    ys, done = halo_rows(z)
    for y, row in places_of(z, done):
        f_ref[y * z.nz + row] = inner_ref[y * z.nz + row]
    right_sides(
        z, places_of(z, ys), tiles_ref, base_ref, lambda side, y: halo_ref[side * z.ny + y],
        y_halos(z, received), rates_ref, y_faces, z_faces, left_ref, right_ref, inverse_ref, f_ref,
    )
    send_sums(z, f_ref, v_ref, u_ref, pay_ref)


def last_kernel(z, within_ref, f_ref, v_ref, u_ref, ends_ref, *refs):
    *across, out_hbm, rows_ref, sems = refs
    group = lax.axis_index("gz") // z.members
    below, above = within_ref[0], within_ref[1]
    for i, ref in enumerate(reversed(across)):
        lower = (group ^ (i + 1)) < group
        value = ref[...]
        below = below + jnp.where(lower, value, 0.0)
        above = above + jnp.where(lower, 0.0, value)
    sums = [[v[per_line(z, y)] for y in range(z.ny)] for v in (below, above)]

    def store(t, value):
        rows_ref[pl.ds(t, z.species, stride=z.tiles), :] = value

    blocks = rows_ref.reshape(z.species, z.ny, z.nz, z.nx)
    copies = []

    def send(y):
        copies.append(pltpu.make_async_copy(blocks.at[:, y], out_hbm.at[:, y], sems.at[y]))
        copies[-1].start()

    solve_lines(z, sums, f_ref, v_ref, u_ref, ends_ref, store, send)
    for copy in copies:
        copy.wait()


def per_device(z, c, k, warm, sigma, frequency, barrier, proportions):
    in_vmem = pl.BlockSpec(memory_space=pltpu.VMEM)
    hbm = pl.BlockSpec(memory_space=pltpu.HBM)

    def shaped(*shape):
        return jax.ShapeDtypeStruct(shape, F32)

    def call(kernel, outs, ins, scratch=(), spec=in_vmem, out_spec=in_vmem, us=0.5):
        return pl.pallas_call(
            functools.partial(kernel, z),
            out_shape=outs,
            in_specs=[spec] * len(ins),
            out_specs=jax.tree.map(lambda _: out_spec, outs),
            scratch_shapes=list(scratch),
            compiler_params=pltpu.CompilerParams(vmem_limit_bytes=48 * 2**20),
            cost_estimate=pl.CostEstimate(
                flops=0, bytes_accessed=int(us * 3.69e6), transcendentals=0
            ),
        )(*ins)

    def shift(value, axis, by):
        count = lax.axis_size(axis)
        return lax.ppermute(value, axis, [(i, (i + by) % count) for i in range(count)])

    def swap(sends):
        return [shift(value, "gy", by) for value, by in zip(sends, (1, -1))]

    arguments = jnp.concatenate([v.reshape(-1, z.nx) for v in (c, k, warm)])
    halos = 1 if z.gy == 2 else 2
    block = shaped(z.tiles, *z.tile)
    ends_shape = shaped(5 * z.ny, *z.tile)

    def exchange(value, count, unit):
        values = value if isinstance(value, list) else [value] * (count - 1)
        pairs = [[(i, i ^ (k * unit)) for i in range(z.devices)] for k in range(1, count)]
        if isinstance(value, list):
            return [lax.ppermute(v, "gz", p) for v, p in zip(values[::-1], pairs[::-1])][::-1]
        return [lax.ppermute(v, "gz", p) for v, p in zip(values, pairs)]

    def neighbours(near, far):
        last = z.devices - 1
        links = [(i, i + 1) for i in range(1, last, 2)]
        links = [pair for i, j in links for pair in ((i, j), (j, i))]
        ends = [(i, i) for i in (0, last)]
        far_pairs = [(i * z.gy + n, j * z.gy + n) for i, j in links for n in range(z.gy)]
        far_pairs += [(i * z.gy + n, j * z.gy + (n ^ 1)) for i, j in ends for n in range(z.gy)]
        far = lax.ppermute(far, ("gz", "gy"), far_pairs)
        return exchange(near, 2, 1)[0], far

    far, near, *sends = call(
        edges_kernel,
        [shaped(z.edge_rows, z.nx)] * 2 + [shaped(z.nz * (z.species + 1), z.nx)] * halos,
        [arguments],
    )
    near, far = neighbours(near, far)
    received = swap(sends)
    levels = shaped(z.levels, z.tiles, *z.tile)
    faces = shaped(2, z.tiles, z.nx)
    rates, x_faces, left, right, inverse = call(
        coefficients_kernel,
        [shaped(4, *z.tile), faces, levels, levels, block],
        [arguments, sigma.reshape(1, -1)],
        us=1.0,
    )
    tiles, arrhenius, base = call(
        source_kernel,
        [block] * 3,
        [arguments, frequency.reshape(1, -1), barrier.reshape(1, -1), proportions, rates, x_faces],
        [pltpu.VMEM((z.tiles, z.nx), F32)],
    )
    x_solve = [left, right, inverse]
    early, y_faces = call(
        early_kernel,
        [block, faces],
        [arguments, tiles, base, rates, *x_solve, *received],
        [pltpu.VMEM((2, z.tiles, z.nx), F32)],
    )
    pay, f, z_faces = call(
        first_kernel,
        [shaped(z.block_rows, z.nx), block, faces],
        [arguments, far, near, tiles, base, rates, *x_solve, early, y_faces, *received],
        [pltpu.VMEM((z.edge_rows, z.nx), F32)] * 2,
    )
    inside = exchange(pay, z.members, 1)
    group = call(
        merge_kernel,
        shaped(z.group_rows, z.nx),
        [rates, pay, *inside],
        [pltpu.VMEM((z.members, z.block_rows, z.nx), F32)],
    )
    across = exchange(group, z.groups_z, z.members)
    tiles, halo, v, u, ends, *sends = call(
        meet_kernel,
        [block, shaped(2 * z.ny, *z.tile), block, block, ends_shape]
        + [shaped(z.nz * z.species, z.nx)] * halos,
        [rates, f, pay, group, *inside, *across],
        [
            pltpu.VMEM((z.members, z.block_rows, z.nx), F32),
            pltpu.VMEM((z.groups_z, z.group_rows, z.nx), F32),
        ],
    )

    received = swap(sends)
    base, f = call(
        inner_kernel,
        [block, block],
        [tiles, halo, rates, x_faces, arrhenius, proportions, y_faces, z_faces, *x_solve],
    )
    pay, f = call(
        second_kernel,
        [shaped(2, z.lines, z.nx), block],
        [tiles, halo, rates, y_faces, z_faces, *x_solve, base, f, v, u, *received],
    )
    inside = exchange(pay, z.members, 1)
    within, *totals = call(
        total_kernel,
        [shaped(2, z.lines, z.nx)] + [shaped(z.lines, z.nx)] * (z.groups_z - 1),
        [pay, *inside],
    )
    across = exchange(totals[::-1], z.groups_z, z.members)
    return call(
        last_kernel,
        shaped(z.species, z.ny, z.nz, z.nx),
        [within, f, v, u, ends, *across[::-1]],
        [pltpu.VMEM((z.species * z.tiles, z.nx), F32), pltpu.SemaphoreType.DMA((z.ny,))],
        out_spec=hbm,
    )


def solution(mesh):
    def device_program(starting_densities, *others):
        sizes = Sizes(mesh, starting_densities.shape)
        return per_device(sizes, starting_densities, *others)

    return jax.shard_map(
        device_program,
        mesh=mesh,
        in_specs=(
            P(None, "gy", "gz", None),
            P("gy", "gz", None),
            P("gy", "gz", None),
            P(),
            P(),
            P(),
            P(),
        ),
        out_specs=P(None, "gy", "gz", None),
        check_vma=False,
    )
```

```python
import functools

import jax
import jax.numpy as jnp
from jax import lax
from jax.experimental import pallas as pl
from jax.experimental.pallas import tpu as pltpu
from jax.sharding import PartitionSpec as P

F32 = jnp.float32


class Sizes:
    def __init__(self, mesh, block):
        self.species, self.ny, self.nz, self.nx = block
        self.tiles = self.ny * self.nz
        self.lines = self.ny * self.species
        self.devices = mesh.shape["gz"]
        self.gy = mesh.shape["gy"]
        self.levels = (self.nx - 1).bit_length()
        self.tile = (self.species, self.nx)
        padded = -(-self.ny // 8) * 8
        self.edge_rows = self.lines + padded
        self.members = 1 << (self.devices.bit_length() // 2)
        self.groups_z = self.devices // self.members
        self.faces_at = 2 * self.lines
        self.block_rows = self.faces_at + self.tiles + padded
        self.group_top = self.faces_at + self.members * self.tiles
        self.group_rows = self.group_top + padded

    def conductance(self, arguments):
        start = self.species * self.tiles
        return arguments.at[start : start + self.tiles]

    def warmth(self, arguments):
        start = (self.species + 1) * self.tiles
        return arguments.at[start : start + self.tiles]

    def groups(self, size):
        for base in range(0, self.tiles, size):
            yield range(base, min(base + size, self.tiles))


def column(ref, z):
    square = (z.species, z.species)
    mine = lax.broadcasted_iota(jnp.int32, square, 0) == lax.broadcasted_iota(jnp.int32, square, 1)
    values = jnp.where(mine, jnp.broadcast_to(ref[...], square), 0.0)
    return jnp.broadcast_to(jnp.sum(values, axis=1, keepdims=True), z.tile)


def spread(ref, row, z):
    return jnp.broadcast_to(ref[pl.ds(row, 1), :], z.tile)


def per_line(z, y):
    return slice(y * z.species, (y + 1) * z.species)


def along_x(v, by, nx):
    return pltpu.roll(v, by % nx, v.ndim - 1)


def flag(condition):
    return jnp.where(condition, 1.0, 0.0).astype(F32)


def inner(axis, count):
    me = lax.axis_index(axis)
    return flag(me > 0), flag(me < count - 1)


def edges_kernel(z, c_ref, far_ref, near_ref, *y_refs):
    k_ref = z.conductance(c_ref)
    odd = lax.axis_index("gz") % 2
    for ref, row in ((near_ref, (1 - odd) * (z.nz - 1)), (far_ref, odd * (z.nz - 1))):
        for y in range(z.ny):
            at = y * z.nz + row
            ref[per_line(z, y), :] = c_ref[pl.ds(at, z.species, stride=z.tiles), :]
            ref[z.lines + y : z.lines + y + 1, :] = k_ref[pl.ds(at, 1), :]
        ref[z.lines + z.ny :, :] = jnp.zeros((z.edge_rows - z.lines - z.ny, z.nx), F32)
    for ref, y in zip(y_refs, y_picks(z)):
        for i in range(z.nz):
            ref[i * z.species : (i + 1) * z.species, :] = c_ref[
                pl.ds(y * z.nz + i, z.species, stride=z.tiles), :
            ]
        start = y * z.nz if isinstance(y, int) else pl.multiple_of(y * z.nz, z.nz)
        ref[z.nz * z.species :, :] = k_ref[pl.ds(start, z.nz), :]


def y_picks(z):
    if z.gy == 2:
        return [jnp.where(lax.axis_index("gy") == 1, 0, z.ny - 1)]
    return [z.ny - 1, 0]


def coefficients_kernel(z, arguments, sigma_ref, rates_ref, faces, left_ref, right_ref, inverse_ref):
    sigma = column(sigma_ref, z)
    rho = 4.0 * sigma
    rates_ref[0] = rho
    rates_ref[1] = 0.015 * sigma
    rates_ref[2] = 4096.0 * sigma
    rates_ref[3] = 1.0 / (1024.0 * sigma)
    k = z.conductance(arguments)[...]
    lanes = lax.broadcasted_iota(jnp.int32, k.shape, 1)
    faces[0] = 0.5 * (k + jnp.where(lanes == 0, 0.0, along_x(k, 1, z.nx)))
    faces[1] = 0.5 * (k + jnp.where(lanes == z.nx - 1, 0.0, along_x(k, -1, z.nx)))
    lanes = lax.broadcasted_iota(jnp.int32, z.tile, 1)
    tiles = range(z.tiles)
    e, d = [], []
    for t in tiles:
        before = rho * spread(faces.at[0], t, z)
        after = rho * spread(faces.at[1], t, z)
        d.append(1.0 + (before + after))
        e.append(jnp.where(lanes == 0, 0.0, before))
    for level in range(z.levels):
        stride = 1 << level
        half = 2 * stride == z.nx
        for t in tiles:
            r = 1.0 / d[t]
            above = along_x(e[t], -stride, z.nx)
            r_before = along_x(r, stride, z.nx)
            left = e[t] * r_before
            right = above * (r_before if half else along_x(r, -stride, z.nx))
            left_ref[level, t] = left + right if half else left
            if not half:
                right_ref[level, t] = right
            d[t] = d[t] - e[t] * left - above * right
            if not half:
                e[t] = left * along_x(e[t], stride, z.nx)
    for t in tiles:
        inverse_ref[t] = 1.0 / d[t]


def source_kernel(
    z, c_ref, frequency_ref, barrier_ref, proportions_ref, rates_ref, faces,
    tiles_ref, arrhenius_ref, base_ref, heat_ref,
):
    frequency, barrier = column(frequency_ref, z), column(barrier_ref, z)
    heat_ref[...] = 1.0 - 1.0 / z.warmth(c_ref)[...]
    for t in range(z.tiles):
        tiles_ref[t] = c_ref[pl.ds(t, z.species, stride=z.tiles), :]
        arrhenius_ref[t] = frequency * jnp.exp(barrier * spread(heat_ref, t, z))
    base_sides(z, tiles_ref, rates_ref, faces, arrhenius_ref, proportions_ref, base_ref)


def base_sides(z, tiles_ref, rates_ref, faces, arrhenius_ref, proportions_ref, base_ref):
    lanes = lax.broadcasted_iota(jnp.int32, z.tile, 1)
    rate = rates_ref[0]
    reacting = jnp.concatenate(
        [arrhenius_ref[t] * jnp.tanh(tiles_ref[t]) for t in range(z.tiles)], axis=1
    )
    source = jnp.dot(
        proportions_ref[...],
        reacting,
        precision=lax.Precision.HIGHEST,
        preferred_element_type=F32,
    )
    for t in range(z.tiles):
        v = tiles_ref[t]
        before = jnp.where(lanes == 0, 0.0, along_x(v, 1, z.nx))
        after = jnp.where(lanes == z.nx - 1, 0.0, along_x(v, -1, z.nx))
        lap = rate * (
            spread(faces.at[1], t, z) * (after - v) - spread(faces.at[0], t, z) * (v - before)
        )
        base_ref[t] = v + lap + source[:, t * z.nx : (t + 1) * z.nx]


def right_sides(z, places, tiles_ref, base_ref, z_halo, y_halo, rates_ref, y_faces, z_faces, left, right, inverse, f_ref):
    rate_y, rate_z = rates_ref[1], rates_ref[2]
    section, lap = [], []
    for y, row in places:
        t = y * z.nz + row
        v = tiles_ref[t]
        z_before = tiles_ref[t - 1] if row else z_halo(0, y)
        z_after = tiles_ref[t + 1] if row < z.nz - 1 else z_halo(1, y)
        if isinstance(y, int):
            y_before = tiles_ref[t - z.nz] if y else y_halo(0, row)
            y_after = tiles_ref[t + z.nz] if y < z.ny - 1 else y_halo(1, row)
        else:
            y_before = jnp.where(y > 0, tiles_ref[jnp.maximum(y - 1, 0) * z.nz + row], y_halo(0, row))
            y_after = jnp.where(
                y < z.ny - 1, tiles_ref[jnp.minimum(y + 1, z.ny - 1) * z.nz + row], y_halo(1, row)
            )
        flux = [spread(faces.at[n], t, z) for faces in (y_faces, z_faces) for n in range(2)]
        lap_y = rate_y * (flux[1] * (y_after - v) - flux[0] * (v - y_before))
        lap_z = rate_z * (flux[3] * (z_after - v) - flux[2] * (v - z_before))
        lap.append(lap_z)
        section.append(base_ref[t] + lap_y + lap_z)
    for level in range(z.levels):
        stride = 1 << level
        for i, (y, row) in enumerate(places):
            t = y * z.nz + row
            before = along_x(section[i], stride, z.nx)
            more = left[level, t] * before
            if 2 * stride < z.nx:
                more = more + right[level, t] * along_x(section[i], -stride, z.nx)
            section[i] = section[i] + more
    for i, (y, row) in enumerate(places):
        t = y * z.nz + row
        f_ref[t] = section[i] * inverse[t] - 0.5 * lap[i]


def y_halos(z, received):
    low, high = received[0], received[-1]
    low_mask, high_mask = inner("gy", z.gy)

    def halo(side, row):
        lines = per_line(z, row)
        return high[lines, :] * high_mask if side else low[lines, :] * low_mask

    return halo


def send_sums(z, f_ref, v_ref, u_ref, pay_ref):
    for y in range(z.ny):
        tiles = range(y * z.nz, (y + 1) * z.nz)
        pay_ref[0, per_line(z, y), :] = functools.reduce(jnp.add, [v_ref[t] * f_ref[t] for t in tiles])
        pay_ref[1, per_line(z, y), :] = functools.reduce(jnp.add, [u_ref[t] * f_ref[t] for t in tiles])


def total_kernel(z, pay_ref, *refs):
    inside = refs[: z.members - 1]
    within_ref, *out_refs = refs[z.members - 1 :]
    me = lax.axis_index("gz")
    group, member = me // z.members, me % z.members
    below = above = jnp.zeros((z.lines, z.nx), F32)
    rising, falling = pay_ref[0], pay_ref[1]
    for i, ref in enumerate(inside):
        lower = (member ^ (i + 1)) < member
        up, down = ref[0], ref[1]
        rising, falling = rising + up, falling + down
        below = below + jnp.where(lower, up, 0.0)
        above = above + jnp.where(lower, 0.0, down)
    within_ref[0] = below
    within_ref[1] = above
    for i, ref in enumerate(reversed(out_refs)):
        ref[...] = jnp.where((group ^ (i + 1)) > group, rising, falling)


def z_face_pair(z, k_ref, low, high):
    rows = lax.broadcasted_iota(jnp.int32, (z.nz, z.nx), 0)
    for y in range(z.ny):
        here = k_ref[y * z.nz : (y + 1) * z.nz, :]
        before, after = (jnp.broadcast_to(row, here.shape) for row in (low(y), high(y)))
        yield (
            here + jnp.where(rows == 0, before, pltpu.roll(here, 1, 0)),
            here + jnp.where(rows == z.nz - 1, after, pltpu.roll(here, z.nz - 1, 0)),
        )


def early_kernel(z, arguments, tiles_ref, base_ref, rates_ref, left_ref, right_ref, inverse_ref, *refs):
    halos = 1 if z.gy == 2 else 2
    received = refs[:halos]
    f_ref, y_faces, z_faces = refs[halos:]
    k_ref = z.conductance(arguments)
    k = k_ref[...]
    low, high = received[0], received[-1]
    low_mask, high_mask = inner("gy", z.gy)
    k_base = z.nz * z.species
    below = jnp.concatenate([low[k_base:, :] * low_mask, k[: z.tiles - z.nz]], axis=0)
    above = jnp.concatenate([k[z.nz :], high[k_base:, :] * high_mask], axis=0)
    y_faces[0] = 0.5 * (k + below)
    y_faces[1] = 0.5 * (k + above)
    nothing = jnp.zeros((1, z.nx), F32)
    for y, (before, after) in enumerate(z_face_pair(z, k_ref, lambda y: nothing, lambda y: nothing)):
        own = slice(y * z.nz, (y + 1) * z.nz)
        z_faces[0, own, :] = 0.5 * before
        z_faces[1, own, :] = 0.5 * after
    places = [(y, row) for y in range(z.ny) for row in range(1, z.nz - 1)]
    right_sides(
        z, places, tiles_ref, base_ref, None, y_halos(z, received), rates_ref, y_faces, z_faces,
        left_ref, right_ref, inverse_ref, f_ref,
    )


def first_kernel(
    z, arguments, far_ref, near_ref, tiles_ref, base_ref, rates_ref, left_ref, right_ref, inverse_ref,
    early_ref, y_faces, *refs
):
    halos = 1 if z.gy == 2 else 2
    received = refs[:halos]
    pay_ref, f_ref, z_faces, from_below, from_above = refs[halos:]
    k_ref = z.conductance(arguments)
    odd = lax.axis_index("gz") % 2 == 1
    from_below[...] = jnp.where(odd, near_ref[...], far_ref[...])
    from_above[...] = jnp.where(odd, far_ref[...], near_ref[...])
    z_low, z_high = inner("gz", z.devices)
    pay_ref[z.faces_at + z.tiles :, :] = jnp.zeros((z.block_rows - z.faces_at - z.tiles, z.nx), F32)

    def k_low(y):
        return from_below[z.lines + y : z.lines + y + 1, :] * z_low

    def k_high(y):
        return from_above[z.lines + y : z.lines + y + 1, :] * z_high

    for y, (before, after) in enumerate(z_face_pair(z, k_ref, k_low, k_high)):
        own = slice(y * z.nz, (y + 1) * z.nz)
        z_faces[0, own, :] = 0.5 * before
        z_faces[1, own, :] = 0.5 * after
        pay_ref[z.faces_at + y * z.nz : z.faces_at + (y + 1) * z.nz, :] = 1.0 / before
        top = z.faces_at + z.tiles + y
        pay_ref[top : top + 1, :] = 1.0 / after[z.nz - 1 :, :]

    def z_halo(side, y):
        lines = per_line(z, y)
        return from_above[lines, :] * z_high if side else from_below[lines, :] * z_low

    for y in range(z.ny):
        for row in range(1, z.nz - 1):
            f_ref[y * z.nz + row] = early_ref[y * z.nz + row]
    places = [(y, row) for y in range(z.ny) for row in sorted({0, z.nz - 1})]
    right_sides(
        z, places, tiles_ref, base_ref, z_halo, y_halos(z, received), rates_ref, y_faces, z_faces,
        left_ref, right_ref, inverse_ref, f_ref,
    )
    ohms = rates_ref[3]
    zero, one = jnp.zeros(z.tile, F32), jnp.ones(z.tile, F32)
    for y in range(z.ny):
        p, q, first, second = (one, zero), (zero, one), zero, zero
        for i in range(z.nz):
            ohm = ohms * spread(pay_ref, z.faces_at + y * z.nz + i, z)
            p, q = advance(p, ohm), advance(q, ohm)
            f = f_ref[y * z.nz + i]
            first = first + p[0] * f
            second = second + q[0] * f
        pay_ref[per_line(z, y), :] = first
        pay_ref[per_line(z, z.ny + y), :] = second


def advance(state, ohm):
    v, w = state
    v = v + w * ohm
    return v, w + v


def merge_kernel(z, rates_ref, pay_ref, *refs):
    *received, group_ref, order = refs
    me = lax.axis_index("gz") % z.members
    order[me] = pay_ref[...]
    for i, ref in enumerate(received):
        order[me ^ (i + 1)] = ref[...]
    ohms = rates_ref[3]
    zero, one = jnp.zeros(z.tile, F32), jnp.ones(z.tile, F32)
    for y in range(z.ny):
        p, q, first, second = (one, zero), (zero, one), zero, zero
        for j in range(z.members):
            s1, s2 = order[j, per_line(z, y), :], order[j, per_line(z, z.ny + y), :]
            first = first + (p[0] * s1 + p[1] * s2)
            second = second + (q[0] * s1 + q[1] * s2)
            if j < z.members - 1:
                for i in range(z.nz):
                    ohm = ohms * spread(order.at[j], z.faces_at + y * z.nz + i, z)
                    p, q = advance(p, ohm), advance(q, ohm)
        group_ref[per_line(z, y), :] = first
        group_ref[per_line(z, z.ny + y), :] = second
    for j in range(z.members):
        start = z.faces_at + j * z.tiles
        group_ref[start : start + z.tiles, :] = order[j, z.faces_at : z.faces_at + z.tiles, :]
    group_ref[z.group_top :, :] = order[z.members - 1, z.faces_at + z.tiles :, :]


def transfers(z, rates_ref, refs, blocks):
    ohms = rates_ref[3]
    zero, one = jnp.zeros(z.tile, F32), jnp.ones(z.tile, F32)

    def block(j, state):
        state = list(state)
        start = z.faces_at + j * z.tiles
        for i in range(z.nz):
            for n, ref in enumerate(refs):
                for y in range(z.ny):
                    ohm = ohms * spread(ref, start + y * z.nz + i, z)
                    at = 4 * (n * z.ny + y)
                    state[at : at + 2] = advance(state[at : at + 2], ohm)
                    state[at + 2 : at + 4] = advance(state[at + 2 : at + 4], ohm)
        return tuple(state)

    state = (one, zero, zero, one) * (z.ny * len(refs))
    state = lax.fori_loop(0, blocks, block, state) if blocks > 1 else block(0, state)
    return [state[4 * z.ny * n : 4 * z.ny * (n + 1)] for n in range(len(refs))]


def inside_kernel(z, rates_ref, *refs):
    *blocks, sums_ref, transfers_ref = refs
    me = lax.axis_index("gz") % z.members
    for i, matrix in enumerate(transfers(z, rates_ref, blocks, 1)):
        sums_ref[me ^ i] = blocks[i][: 2 * z.lines, :]
        for n, value in enumerate(matrix):
            transfers_ref[me ^ i, n] = value


def far_kernel(z, rates_ref, group_ref, out_ref):
    (matrix,) = transfers(z, rates_ref, [group_ref], z.members)
    for n, value in enumerate(matrix):
        out_ref[n] = value


def both_ways(z, rates_ref, own_ref, blocks, groups, top_ref, v_ref, u_ref, ends_ref, sums_ref):
    me = lax.axis_index("gz")
    group, member = me // z.members, me % z.members
    ohms = rates_ref[3]
    zero, one = jnp.zeros(z.tile, F32), jnp.ones(z.tile, F32)
    ys = range(z.ny)

    def ohm(ref, row):
        return ohms * spread(ref, row, z)

    def totals(sums, j, y):
        return sums[j, per_line(z, y), :], sums[j, per_line(z, z.ny + y), :]

    def up(refs, j, state):
        sums, matrices = refs
        out = []
        for y in ys:
            v, w, total = state[3 * y : 3 * y + 3]
            s1, s2 = totals(sums, j, y)
            pv, pw, qv, qw = (matrices[j, 4 * y + n] for n in range(4))
            out += [pv * v + qv * w, pw * v + qw * w, total + (v * s1 + w * s2)]
        return tuple(out)

    def down(refs, j, state):
        sums, matrices = refs
        out = []
        for y in ys:
            u, w, total = state[3 * y : 3 * y + 3]
            s1, s2 = totals(sums, j, y)
            pv, pw, qv, qw = (matrices[j, 4 * y + n] for n in range(4))
            u, w = qw * u + qv * w, pw * u + pv * w
            out += [u, w, total + (u * s1 - w * s2)]
        return tuple(out)

    state = (zero, one, zero) * z.ny
    state = lax.fori_loop(0, group, lambda j, s: up(groups, j, s), state)
    state = lax.fori_loop(0, member, lambda j, s: up(blocks, j, s), state)
    rising = []
    for y in ys:
        pair = state[3 * y : 3 * y + 2]
        sums_ref[y] = state[3 * y + 2]
        ends_ref[y] = pair[0]
        for i in range(z.nz):
            pair = advance(pair, ohm(own_ref, z.faces_at + y * z.nz + i))
            v_ref[y * z.nz + i] = pair[0]
            if i == 0:
                rising.append(pair)
        ends_ref[z.ny + y] = pair[0] + pair[1] * ohm(own_ref, z.faces_at + z.tiles + y)

    state = ()
    for y in ys:
        state += (ohm(top_ref, y), one, zero)
    last = z.groups_z - 1
    state = lax.fori_loop(0, last - group, lambda i, s: down(groups, last - i, s), state)
    last = z.members - 1
    state = lax.fori_loop(0, last - member, lambda i, s: down(blocks, last - i, s), state)
    for y in ys:
        u, w, total = state[3 * y : 3 * y + 3]
        sums_ref[z.ny + y] = total
        ends_ref[3 * z.ny + y] = u - w * ohm(own_ref, z.faces_at + z.tiles + y)
        for i in reversed(range(z.nz)):
            u_ref[y * z.nz + i] = u
            if i == 0:
                v, wv = rising[y]
                ends_ref[4 * z.ny + y] = 1.0 / (wv * u + v * w)
            w = w + u
            u = u + w * ohm(own_ref, z.faces_at + y * z.nz + i)
        ends_ref[2 * z.ny + y] = u


def solve_row(z, y, sums, f_ref, v_ref, u_ref, ends_ref, store):
    below, above = sums
    scale = ends_ref[4 * z.ny + y]
    after = [None] * z.nz
    total = above
    for i in reversed(range(z.nz)):
        t = y * z.nz + i
        after[i] = total
        total = total + u_ref[t] * f_ref[t]
    low = scale * (ends_ref[2 * z.ny + y] * below + ends_ref[y] * total)
    total = below
    for i in range(z.nz):
        t = y * z.nz + i
        total = total + v_ref[t] * f_ref[t]
        store(i, scale * (u_ref[t] * total + v_ref[t] * after[i]))
    high = scale * (ends_ref[3 * z.ny + y] * total + ends_ref[z.ny + y] * above)
    return low, high


def meet_kernel(z, rates_ref, f_ref, pay_ref, own_group, block_sums, block_transfers, far_transfer, *refs):
    across, refs = refs[: z.groups_z - 1], refs[z.groups_z - 1 :]
    v_ref, u_ref, ends_ref, sums_ref, *y_refs, group_sums, group_transfers, tops = refs
    group = lax.axis_index("gz") // z.members
    near = transfers(z, rates_ref, across[:-1], z.members)
    for i, ref in enumerate((own_group, *across)):
        group_sums[group ^ i] = ref[: 2 * z.lines, :]
        tops[group ^ i] = ref[z.group_top :, :]
    for i, matrix in enumerate(near):
        for n, value in enumerate(matrix):
            group_transfers[group ^ (i + 1), n] = value
    group_transfers[group ^ len(across)] = far_transfer[...]
    both_ways(
        z, rates_ref, pay_ref, (block_sums, block_transfers), (group_sums, group_transfers),
        tops.at[z.groups_z - 1], v_ref, u_ref, ends_ref, sums_ref,
    )
    for ref, y in zip(y_refs, y_picks(z)):

        def store(i, value):
            ref[i * z.species : (i + 1) * z.species, :] = value

        solve_row(z, y, (sums_ref[y], sums_ref[z.ny + y]), f_ref, v_ref, u_ref, ends_ref, store)


def rows_kernel(z, f_ref, v_ref, u_ref, ends_ref, sums_ref, tiles_ref, halo_ref):
    for y in range(z.ny):

        def store(i, value):
            tiles_ref[y * z.nz + i] = value

        low, high = solve_row(
            z, y, (sums_ref[y], sums_ref[z.ny + y]), f_ref, v_ref, u_ref, ends_ref, store
        )
        halo_ref[y] = low
        halo_ref[z.ny + y] = high


def halo_rows(z):
    if z.gy == 2:
        core = lax.axis_index("gy")
        return y_picks(z), [core + j for j in range(z.ny - 1)]
    return list(range(z.ny)), []


def places_of(z, ys):
    return [(y, row) for y in ys for row in range(z.nz)]


def inner_kernel(
    z, tiles_ref, halo_ref, rates_ref, x_faces, arrhenius_ref, proportions_ref, y_faces, z_faces,
    left_ref, right_ref, inverse_ref, base_ref, f_ref
):
    base_sides(z, tiles_ref, rates_ref, x_faces, arrhenius_ref, proportions_ref, base_ref)
    _, ys = halo_rows(z)
    zero = jnp.zeros(z.tile, F32)
    if ys:
        right_sides(
            z, places_of(z, ys), tiles_ref, base_ref, lambda side, y: halo_ref[side * z.ny + y],
            lambda side, row: zero, rates_ref, y_faces, z_faces, left_ref, right_ref, inverse_ref, f_ref,
        )


def second_kernel(
    z, tiles_ref, halo_ref, rates_ref, y_faces, z_faces, left_ref, right_ref, inverse_ref, base_ref,
    inner_ref, v_ref, u_ref, *refs
):
    halos = 1 if z.gy == 2 else 2
    received = refs[:halos]
    pay_ref, f_ref = refs[halos:]
    ys, done = halo_rows(z)
    for y, row in places_of(z, done):
        f_ref[y * z.nz + row] = inner_ref[y * z.nz + row]
    right_sides(
        z, places_of(z, ys), tiles_ref, base_ref, lambda side, y: halo_ref[side * z.ny + y],
        y_halos(z, received), rates_ref, y_faces, z_faces, left_ref, right_ref, inverse_ref, f_ref,
    )
    send_sums(z, f_ref, v_ref, u_ref, pay_ref)


def last_kernel(z, within_ref, f_ref, v_ref, u_ref, ends_ref, *refs):
    *across, out_hbm, rows_ref, sems = refs
    group = lax.axis_index("gz") // z.members
    below, above = within_ref[0], within_ref[1]
    for i, ref in enumerate(reversed(across)):
        lower = (group ^ (i + 1)) < group
        value = ref[...]
        below = below + jnp.where(lower, value, 0.0)
        above = above + jnp.where(lower, 0.0, value)
    blocks = rows_ref.reshape(z.species, z.ny, z.nz, z.nx)
    copies = []
    for y in range(z.ny):

        def store(i, value):
            rows_ref[pl.ds(y * z.nz + i, z.species, stride=z.tiles), :] = value

        sums = below[per_line(z, y)], above[per_line(z, y)]
        solve_row(z, y, sums, f_ref, v_ref, u_ref, ends_ref, store)
        copies.append(pltpu.make_async_copy(blocks.at[:, y], out_hbm.at[:, y], sems.at[y]))
        copies[-1].start()
    for copy in copies:
        copy.wait()


def per_device(z, c, k, warm, sigma, frequency, barrier, proportions):
    in_vmem = pl.BlockSpec(memory_space=pltpu.VMEM)
    hbm = pl.BlockSpec(memory_space=pltpu.HBM)

    def shaped(*shape):
        return jax.ShapeDtypeStruct(shape, F32)

    def call(kernel, outs, ins, scratch=(), spec=in_vmem, out_spec=in_vmem, us=0.5):
        return pl.pallas_call(
            functools.partial(kernel, z),
            out_shape=outs,
            in_specs=[spec] * len(ins),
            out_specs=jax.tree.map(lambda _: out_spec, outs),
            scratch_shapes=list(scratch),
            compiler_params=pltpu.CompilerParams(vmem_limit_bytes=48 * 2**20),
            cost_estimate=pl.CostEstimate(
                flops=0, bytes_accessed=int(us * 3.69e6), transcendentals=0
            ),
        )(*ins)

    def shift(value, axis, by):
        count = lax.axis_size(axis)
        return lax.ppermute(value, axis, [(i, (i + by) % count) for i in range(count)])

    def swap(sends):
        return [shift(value, "gy", by) for value, by in zip(sends, (1, -1))]

    arguments = jnp.concatenate([v.reshape(-1, z.nx) for v in (c, k, warm)])
    halos = 1 if z.gy == 2 else 2
    block = shaped(z.tiles, *z.tile)
    ends_shape = shaped(5 * z.ny, *z.tile)

    def exchange(value, count, unit):
        values = value if isinstance(value, list) else [value] * (count - 1)
        pairs = [[(i, i ^ (k * unit)) for i in range(z.devices)] for k in range(1, count)]
        if isinstance(value, list):
            return [lax.ppermute(v, "gz", p) for v, p in zip(values[::-1], pairs[::-1])][::-1]
        return [lax.ppermute(v, "gz", p) for v, p in zip(values, pairs)]

    def neighbours(near, far):
        last = z.devices - 1
        links = [(i, i + 1) for i in range(1, last, 2)]
        links = [pair for i, j in links for pair in ((i, j), (j, i))]
        ends = [(i, i) for i in (0, last)]
        far_pairs = [(i * z.gy + n, j * z.gy + n) for i, j in links for n in range(z.gy)]
        far_pairs += [(i * z.gy + n, j * z.gy + (n ^ 1)) for i, j in ends for n in range(z.gy)]
        far = lax.ppermute(far, ("gz", "gy"), far_pairs)
        return exchange(near, 2, 1)[0], far

    far, near, *sends = call(
        edges_kernel,
        [shaped(z.edge_rows, z.nx)] * 2 + [shaped(z.nz * (z.species + 1), z.nx)] * halos,
        [arguments],
    )
    near, far = neighbours(near, far)
    received = swap(sends)
    levels = shaped(z.levels, z.tiles, *z.tile)
    faces = shaped(2, z.tiles, z.nx)
    rates, x_faces, left, right, inverse = call(
        coefficients_kernel,
        [shaped(4, *z.tile), faces, levels, levels, block],
        [arguments, sigma.reshape(1, -1)],
        us=1.0,
    )
    tiles, arrhenius, base = call(
        source_kernel,
        [block] * 3,
        [arguments, frequency.reshape(1, -1), barrier.reshape(1, -1), proportions, rates, x_faces],
        [pltpu.VMEM((z.tiles, z.nx), F32)],
    )
    x_solve = [left, right, inverse]
    early, y_faces = call(
        early_kernel,
        [block, faces],
        [arguments, tiles, base, rates, *x_solve, *received],
        [pltpu.VMEM((2, z.tiles, z.nx), F32)],
    )
    pay, f, z_faces = call(
        first_kernel,
        [shaped(z.block_rows, z.nx), block, faces],
        [arguments, far, near, tiles, base, rates, *x_solve, early, y_faces, *received],
        [pltpu.VMEM((z.edge_rows, z.nx), F32)] * 2,
    )
    inside = exchange(pay, z.members, 1)
    group = call(
        merge_kernel,
        shaped(z.group_rows, z.nx),
        [rates, pay, *inside],
        [pltpu.VMEM((z.members, z.block_rows, z.nx), F32)],
    )
    across = exchange(group, z.groups_z, z.members)
    matrices = shaped(4 * z.ny, *z.tile)
    block_sums, block_transfers = call(
        inside_kernel,
        [shaped(z.members, 2 * z.lines, z.nx), shaped(z.members, *matrices.shape)],
        [rates, pay, *inside],
    )
    far_transfer = call(far_kernel, matrices, [rates, across[-1]])
    v, u, ends, sums, *sends = call(
        meet_kernel,
        [block, block, ends_shape, shaped(2 * z.ny, *z.tile)]
        + [shaped(z.nz * z.species, z.nx)] * halos,
        [rates, f, pay, group, block_sums, block_transfers, far_transfer, *across],
        [
            pltpu.VMEM((z.groups_z, 2 * z.lines, z.nx), F32),
            pltpu.VMEM((z.groups_z, *matrices.shape), F32),
            pltpu.VMEM((z.groups_z, z.group_rows - z.group_top, z.nx), F32),
        ],
    )

    received = swap(sends)
    tiles, halo = call(rows_kernel, [block, shaped(2 * z.ny, *z.tile)], [f, v, u, ends, sums])
    base, f = call(
        inner_kernel,
        [block, block],
        [tiles, halo, rates, x_faces, arrhenius, proportions, y_faces, z_faces, *x_solve],
    )
    pay, f = call(
        second_kernel,
        [shaped(2, z.lines, z.nx), block],
        [tiles, halo, rates, y_faces, z_faces, *x_solve, base, f, v, u, *received],
    )
    inside = exchange(pay, z.members, 1)
    within, *totals = call(
        total_kernel,
        [shaped(2, z.lines, z.nx)] + [shaped(z.lines, z.nx)] * (z.groups_z - 1),
        [pay, *inside],
    )
    across = exchange(totals[::-1], z.groups_z, z.members)
    return call(
        last_kernel,
        shaped(z.species, z.ny, z.nz, z.nx),
        [within, f, v, u, ends, *across[::-1]],
        [pltpu.VMEM((z.species * z.tiles, z.nx), F32), pltpu.SemaphoreType.DMA((z.ny,))],
        out_spec=hbm,
    )


def solution(mesh):
    def device_program(starting_densities, *others):
        sizes = Sizes(mesh, starting_densities.shape)
        return per_device(sizes, starting_densities, *others)

    return jax.shard_map(
        device_program,
        mesh=mesh,
        in_specs=(
            P(None, "gy", "gz", None),
            P("gy", "gz", None),
            P("gy", "gz", None),
            P(),
            P(),
            P(),
            P(),
        ),
        out_specs=P(None, "gy", "gz", None),
        check_vma=False,
    )
```

```python
import functools

import jax
import jax.numpy as jnp
from jax import lax
from jax.experimental import pallas as pl
from jax.experimental.pallas import tpu as pltpu
from jax.sharding import PartitionSpec as P

F32 = jnp.float32


class Sizes:
    def __init__(self, mesh, block):
        self.species, self.ny, self.nz, self.nx = block
        self.tiles = self.ny * self.nz
        self.lines = self.ny * self.species
        self.devices = mesh.shape["gz"]
        self.gy = mesh.shape["gy"]
        self.levels = (self.nx - 1).bit_length()
        self.tile = (self.species, self.nx)
        padded = -(-self.ny // 8) * 8
        self.edge_rows = self.lines + padded
        self.members = 1 << (self.devices.bit_length() // 2)
        self.groups_z = self.devices // self.members
        self.faces_at = 2 * self.lines
        self.block_rows = self.faces_at + self.tiles + padded
        self.group_top = self.faces_at + self.members * self.tiles
        self.group_rows = self.group_top + padded

    def conductance(self, arguments):
        start = self.species * self.tiles
        return arguments.at[start : start + self.tiles]

    def warmth(self, arguments):
        start = (self.species + 1) * self.tiles
        return arguments.at[start : start + self.tiles]

    def groups(self, size):
        for base in range(0, self.tiles, size):
            yield range(base, min(base + size, self.tiles))


def column(ref, z):
    square = (z.species, z.species)
    mine = lax.broadcasted_iota(jnp.int32, square, 0) == lax.broadcasted_iota(jnp.int32, square, 1)
    values = jnp.where(mine, jnp.broadcast_to(ref[...], square), 0.0)
    return jnp.broadcast_to(jnp.sum(values, axis=1, keepdims=True), z.tile)


def spread(ref, row, z):
    return jnp.broadcast_to(ref[pl.ds(row, 1), :], z.tile)


def per_line(z, y):
    return slice(y * z.species, (y + 1) * z.species)


def along_x(v, by, nx):
    return pltpu.roll(v, by % nx, v.ndim - 1)


def flag(condition):
    return jnp.where(condition, 1.0, 0.0).astype(F32)


def inner(axis, count):
    me = lax.axis_index(axis)
    return flag(me > 0), flag(me < count - 1)


def edges_kernel(z, c_ref, far_ref, near_ref, *y_refs):
    k_ref = z.conductance(c_ref)
    odd = lax.axis_index("gz") % 2
    for ref, row in ((near_ref, (1 - odd) * (z.nz - 1)), (far_ref, odd * (z.nz - 1))):
        for y in range(z.ny):
            at = y * z.nz + row
            ref[per_line(z, y), :] = c_ref[pl.ds(at, z.species, stride=z.tiles), :]
            ref[z.lines + y : z.lines + y + 1, :] = k_ref[pl.ds(at, 1), :]
        ref[z.lines + z.ny :, :] = jnp.zeros((z.edge_rows - z.lines - z.ny, z.nx), F32)
    for ref, y in zip(y_refs, y_picks(z)):
        for i in range(z.nz):
            ref[i * z.species : (i + 1) * z.species, :] = c_ref[
                pl.ds(y * z.nz + i, z.species, stride=z.tiles), :
            ]
        start = y * z.nz if isinstance(y, int) else pl.multiple_of(y * z.nz, z.nz)
        ref[z.nz * z.species :, :] = k_ref[pl.ds(start, z.nz), :]


def y_picks(z):
    if z.gy == 2:
        return [jnp.where(lax.axis_index("gy") == 1, 0, z.ny - 1)]
    return [z.ny - 1, 0]


def coefficients_kernel(z, arguments, sigma_ref, rates_ref, faces, left_ref, right_ref, inverse_ref):
    sigma = column(sigma_ref, z)
    rho = 4.0 * sigma
    rates_ref[0] = rho
    rates_ref[1] = 0.015 * sigma
    rates_ref[2] = 4096.0 * sigma
    rates_ref[3] = 1.0 / (1024.0 * sigma)
    k = z.conductance(arguments)[...]
    lanes = lax.broadcasted_iota(jnp.int32, k.shape, 1)
    faces[0] = 0.5 * (k + jnp.where(lanes == 0, 0.0, along_x(k, 1, z.nx)))
    faces[1] = 0.5 * (k + jnp.where(lanes == z.nx - 1, 0.0, along_x(k, -1, z.nx)))
    lanes = lax.broadcasted_iota(jnp.int32, z.tile, 1)
    tiles = range(z.tiles)
    e, d = [], []
    for t in tiles:
        before = rho * spread(faces.at[0], t, z)
        after = rho * spread(faces.at[1], t, z)
        d.append(1.0 + (before + after))
        e.append(jnp.where(lanes == 0, 0.0, before))
    for level in range(z.levels):
        stride = 1 << level
        half = 2 * stride == z.nx
        for t in tiles:
            r = 1.0 / d[t]
            above = along_x(e[t], -stride, z.nx)
            r_before = along_x(r, stride, z.nx)
            left = e[t] * r_before
            right = above * (r_before if half else along_x(r, -stride, z.nx))
            left_ref[level, t] = left + right if half else left
            if not half:
                right_ref[level, t] = right
            d[t] = d[t] - e[t] * left - above * right
            if not half:
                e[t] = left * along_x(e[t], stride, z.nx)
    for t in tiles:
        inverse_ref[t] = 1.0 / d[t]


def source_kernel(
    z, c_ref, frequency_ref, barrier_ref, proportions_ref, rates_ref, faces,
    tiles_ref, arrhenius_ref, base_ref, heat_ref,
):
    frequency, barrier = column(frequency_ref, z), column(barrier_ref, z)
    heat_ref[...] = 1.0 - 1.0 / z.warmth(c_ref)[...]
    for t in range(z.tiles):
        tiles_ref[t] = c_ref[pl.ds(t, z.species, stride=z.tiles), :]
        arrhenius_ref[t] = frequency * jnp.exp(barrier * spread(heat_ref, t, z))
    base_sides(z, tiles_ref, rates_ref, faces, arrhenius_ref, proportions_ref, base_ref)


def base_sides(z, tiles_ref, rates_ref, faces, arrhenius_ref, proportions_ref, base_ref):
    lanes = lax.broadcasted_iota(jnp.int32, z.tile, 1)
    rate = rates_ref[0]
    reacting = jnp.concatenate(
        [arrhenius_ref[t] * jnp.tanh(tiles_ref[t]) for t in range(z.tiles)], axis=1
    )
    source = jnp.dot(
        proportions_ref[...],
        reacting,
        precision=lax.Precision.HIGHEST,
        preferred_element_type=F32,
    )
    for t in range(z.tiles):
        v = tiles_ref[t]
        before = jnp.where(lanes == 0, 0.0, along_x(v, 1, z.nx))
        after = jnp.where(lanes == z.nx - 1, 0.0, along_x(v, -1, z.nx))
        lap = rate * (
            spread(faces.at[1], t, z) * (after - v) - spread(faces.at[0], t, z) * (v - before)
        )
        base_ref[t] = v + lap + source[:, t * z.nx : (t + 1) * z.nx]


def right_sides(z, places, tiles_ref, base_ref, z_halo, y_halo, rates_ref, y_faces, z_faces, left, right, inverse, f_ref):
    rate_y, rate_z = rates_ref[1], rates_ref[2]
    section, lap = [], []
    for y, row in places:
        t = y * z.nz + row
        v = tiles_ref[t]
        z_before = tiles_ref[t - 1] if row else z_halo(0, y)
        z_after = tiles_ref[t + 1] if row < z.nz - 1 else z_halo(1, y)
        if isinstance(y, int):
            y_before = tiles_ref[t - z.nz] if y else y_halo(0, row)
            y_after = tiles_ref[t + z.nz] if y < z.ny - 1 else y_halo(1, row)
        else:
            y_before = jnp.where(y > 0, tiles_ref[jnp.maximum(y - 1, 0) * z.nz + row], y_halo(0, row))
            y_after = jnp.where(
                y < z.ny - 1, tiles_ref[jnp.minimum(y + 1, z.ny - 1) * z.nz + row], y_halo(1, row)
            )
        flux = [spread(faces.at[n], t, z) for faces in (y_faces, z_faces) for n in range(2)]
        lap_y = rate_y * (flux[1] * (y_after - v) - flux[0] * (v - y_before))
        lap_z = rate_z * (flux[3] * (z_after - v) - flux[2] * (v - z_before))
        lap.append(lap_z)
        section.append(base_ref[t] + lap_y + lap_z)
    for level in range(z.levels):
        stride = 1 << level
        for i, (y, row) in enumerate(places):
            t = y * z.nz + row
            before = along_x(section[i], stride, z.nx)
            more = left[level, t] * before
            if 2 * stride < z.nx:
                more = more + right[level, t] * along_x(section[i], -stride, z.nx)
            section[i] = section[i] + more
    for i, (y, row) in enumerate(places):
        t = y * z.nz + row
        f_ref[t] = section[i] * inverse[t] - 0.5 * lap[i]


def y_halos(z, received):
    low, high = received[0], received[-1]
    low_mask, high_mask = inner("gy", z.gy)

    def halo(side, row):
        lines = per_line(z, row)
        return high[lines, :] * high_mask if side else low[lines, :] * low_mask

    return halo


def send_sums(z, f_ref, v_ref, u_ref, pay_ref):
    for y in range(z.ny):
        tiles = range(y * z.nz, (y + 1) * z.nz)
        pay_ref[0, per_line(z, y), :] = functools.reduce(jnp.add, [v_ref[t] * f_ref[t] for t in tiles])
        pay_ref[1, per_line(z, y), :] = functools.reduce(jnp.add, [u_ref[t] * f_ref[t] for t in tiles])


def total_kernel(z, pay_ref, *refs):
    inside = refs[: z.members - 1]
    within_ref, *out_refs = refs[z.members - 1 :]
    me = lax.axis_index("gz")
    group, member = me // z.members, me % z.members
    below = above = jnp.zeros((z.lines, z.nx), F32)
    rising, falling = pay_ref[0], pay_ref[1]
    for i, ref in enumerate(inside):
        lower = (member ^ (i + 1)) < member
        up, down = ref[0], ref[1]
        rising, falling = rising + up, falling + down
        below = below + jnp.where(lower, up, 0.0)
        above = above + jnp.where(lower, 0.0, down)
    within_ref[0] = below
    within_ref[1] = above
    for i, ref in enumerate(reversed(out_refs)):
        ref[...] = jnp.where((group ^ (i + 1)) > group, rising, falling)


def z_face_pair(z, k_ref, low, high):
    rows = lax.broadcasted_iota(jnp.int32, (z.nz, z.nx), 0)
    for y in range(z.ny):
        here = k_ref[y * z.nz : (y + 1) * z.nz, :]
        before, after = (jnp.broadcast_to(row, here.shape) for row in (low(y), high(y)))
        yield (
            here + jnp.where(rows == 0, before, pltpu.roll(here, 1, 0)),
            here + jnp.where(rows == z.nz - 1, after, pltpu.roll(here, z.nz - 1, 0)),
        )


def early_kernel(z, arguments, tiles_ref, base_ref, rates_ref, left_ref, right_ref, inverse_ref, *refs):
    halos = 1 if z.gy == 2 else 2
    received = refs[:halos]
    f_ref, y_faces, z_faces = refs[halos:]
    k_ref = z.conductance(arguments)
    k = k_ref[...]
    low, high = received[0], received[-1]
    low_mask, high_mask = inner("gy", z.gy)
    k_base = z.nz * z.species
    below = jnp.concatenate([low[k_base:, :] * low_mask, k[: z.tiles - z.nz]], axis=0)
    above = jnp.concatenate([k[z.nz :], high[k_base:, :] * high_mask], axis=0)
    y_faces[0] = 0.5 * (k + below)
    y_faces[1] = 0.5 * (k + above)
    nothing = jnp.zeros((1, z.nx), F32)
    for y, (before, after) in enumerate(z_face_pair(z, k_ref, lambda y: nothing, lambda y: nothing)):
        own = slice(y * z.nz, (y + 1) * z.nz)
        z_faces[0, own, :] = 0.5 * before
        z_faces[1, own, :] = 0.5 * after
    places = [(y, row) for y in range(z.ny) for row in range(1, z.nz - 1)]
    right_sides(
        z, places, tiles_ref, base_ref, None, y_halos(z, received), rates_ref, y_faces, z_faces,
        left_ref, right_ref, inverse_ref, f_ref,
    )


def first_kernel(
    z, arguments, far_ref, near_ref, tiles_ref, base_ref, rates_ref, left_ref, right_ref, inverse_ref,
    early_ref, y_faces, *refs
):
    halos = 1 if z.gy == 2 else 2
    received = refs[:halos]
    pay_ref, f_ref, z_faces, from_below, from_above = refs[halos:]
    k_ref = z.conductance(arguments)
    odd = lax.axis_index("gz") % 2 == 1
    from_below[...] = jnp.where(odd, near_ref[...], far_ref[...])
    from_above[...] = jnp.where(odd, far_ref[...], near_ref[...])
    z_low, z_high = inner("gz", z.devices)
    pay_ref[z.faces_at + z.tiles :, :] = jnp.zeros((z.block_rows - z.faces_at - z.tiles, z.nx), F32)

    def k_low(y):
        return from_below[z.lines + y : z.lines + y + 1, :] * z_low

    def k_high(y):
        return from_above[z.lines + y : z.lines + y + 1, :] * z_high

    for y, (before, after) in enumerate(z_face_pair(z, k_ref, k_low, k_high)):
        own = slice(y * z.nz, (y + 1) * z.nz)
        z_faces[0, own, :] = 0.5 * before
        z_faces[1, own, :] = 0.5 * after
        pay_ref[z.faces_at + y * z.nz : z.faces_at + (y + 1) * z.nz, :] = 1.0 / before
        top = z.faces_at + z.tiles + y
        pay_ref[top : top + 1, :] = 1.0 / after[z.nz - 1 :, :]

    def z_halo(side, y):
        lines = per_line(z, y)
        return from_above[lines, :] * z_high if side else from_below[lines, :] * z_low

    for y in range(z.ny):
        for row in range(1, z.nz - 1):
            f_ref[y * z.nz + row] = early_ref[y * z.nz + row]
    places = [(y, row) for y in range(z.ny) for row in sorted({0, z.nz - 1})]
    right_sides(
        z, places, tiles_ref, base_ref, z_halo, y_halos(z, received), rates_ref, y_faces, z_faces,
        left_ref, right_ref, inverse_ref, f_ref,
    )
    ohms = rates_ref[3]
    zero, one = jnp.zeros(z.tile, F32), jnp.ones(z.tile, F32)
    for y in range(z.ny):
        p, q, first, second = (one, zero), (zero, one), zero, zero
        for i in range(z.nz):
            ohm = ohms * spread(pay_ref, z.faces_at + y * z.nz + i, z)
            p, q = advance(p, ohm), advance(q, ohm)
            f = f_ref[y * z.nz + i]
            first = first + p[0] * f
            second = second + q[0] * f
        pay_ref[per_line(z, y), :] = first
        pay_ref[per_line(z, z.ny + y), :] = second


def advance(state, ohm):
    v, w = state
    v = v + w * ohm
    return v, w + v


def merge_kernel(z, rates_ref, pay_ref, *refs):
    *received, group_ref, order = refs
    me = lax.axis_index("gz") % z.members
    order[me] = pay_ref[...]
    for i, ref in enumerate(received):
        order[me ^ (i + 1)] = ref[...]
    ohms = rates_ref[3]
    zero, one = jnp.zeros(z.tile, F32), jnp.ones(z.tile, F32)
    for y in range(z.ny):
        p, q, first, second = (one, zero), (zero, one), zero, zero
        for j in range(z.members):
            s1, s2 = order[j, per_line(z, y), :], order[j, per_line(z, z.ny + y), :]
            first = first + (p[0] * s1 + p[1] * s2)
            second = second + (q[0] * s1 + q[1] * s2)
            if j < z.members - 1:
                for i in range(z.nz):
                    ohm = ohms * spread(order.at[j], z.faces_at + y * z.nz + i, z)
                    p, q = advance(p, ohm), advance(q, ohm)
        group_ref[per_line(z, y), :] = first
        group_ref[per_line(z, z.ny + y), :] = second
    for j in range(z.members):
        start = z.faces_at + j * z.tiles
        group_ref[start : start + z.tiles, :] = order[j, z.faces_at : z.faces_at + z.tiles, :]
    group_ref[z.group_top :, :] = order[z.members - 1, z.faces_at + z.tiles :, :]


def transfers(z, rates_ref, refs, blocks):
    ohms = rates_ref[3]
    zero, one = jnp.zeros(z.tile, F32), jnp.ones(z.tile, F32)

    def block(j, state):
        state = list(state)
        start = z.faces_at + j * z.tiles
        for i in range(z.nz):
            for n, ref in enumerate(refs):
                for y in range(z.ny):
                    ohm = ohms * spread(ref, start + y * z.nz + i, z)
                    at = 4 * (n * z.ny + y)
                    state[at : at + 2] = advance(state[at : at + 2], ohm)
                    state[at + 2 : at + 4] = advance(state[at + 2 : at + 4], ohm)
        return tuple(state)

    state = (one, zero, zero, one) * (z.ny * len(refs))
    state = lax.fori_loop(0, blocks, block, state) if blocks > 1 else block(0, state)
    return [state[4 * z.ny * n : 4 * z.ny * (n + 1)] for n in range(len(refs))]


def inside_kernel(z, rates_ref, *refs):
    *blocks, sums_ref, transfers_ref = refs
    me = lax.axis_index("gz") % z.members
    for i, matrix in enumerate(transfers(z, rates_ref, blocks, 1)):
        sums_ref[me ^ i] = blocks[i][: 2 * z.lines, :]
        for n, value in enumerate(matrix):
            transfers_ref[me ^ i, n] = value


def far_kernel(z, rates_ref, group_ref, out_ref):
    (matrix,) = transfers(z, rates_ref, [group_ref], z.members)
    for n, value in enumerate(matrix):
        out_ref[n] = value


def both_ways(z, rates_ref, own_ref, blocks, groups, top_ref, v_ref, u_ref, ends_ref, sums_ref):
    me = lax.axis_index("gz")
    group, member = me // z.members, me % z.members
    ohms = rates_ref[3]
    zero, one = jnp.zeros(z.tile, F32), jnp.ones(z.tile, F32)
    ys = range(z.ny)

    def ohm(ref, row):
        return ohms * spread(ref, row, z)

    def totals(sums, j, y):
        return sums[j, per_line(z, y), :], sums[j, per_line(z, z.ny + y), :]

    def up(refs, j, state):
        sums, matrices = refs
        out = []
        for y in ys:
            v, w, total = state[3 * y : 3 * y + 3]
            s1, s2 = totals(sums, j, y)
            pv, pw, qv, qw = (matrices[j, 4 * y + n] for n in range(4))
            out += [pv * v + qv * w, pw * v + qw * w, total + (v * s1 + w * s2)]
        return tuple(out)

    def down(refs, j, state):
        sums, matrices = refs
        out = []
        for y in ys:
            u, w, total = state[3 * y : 3 * y + 3]
            s1, s2 = totals(sums, j, y)
            pv, pw, qv, qw = (matrices[j, 4 * y + n] for n in range(4))
            u, w = qw * u + qv * w, pw * u + pv * w
            out += [u, w, total + (u * s1 - w * s2)]
        return tuple(out)

    state = (zero, one, zero) * z.ny
    state = lax.fori_loop(0, group, lambda j, s: up(groups, j, s), state)
    state = lax.fori_loop(0, member, lambda j, s: up(blocks, j, s), state)
    rising = []
    for y in ys:
        pair = state[3 * y : 3 * y + 2]
        sums_ref[y] = state[3 * y + 2]
        ends_ref[y] = pair[0]
        for i in range(z.nz):
            pair = advance(pair, ohm(own_ref, z.faces_at + y * z.nz + i))
            v_ref[y * z.nz + i] = pair[0]
            if i == 0:
                rising.append(pair)
        ends_ref[z.ny + y] = pair[0] + pair[1] * ohm(own_ref, z.faces_at + z.tiles + y)

    state = ()
    for y in ys:
        state += (ohm(top_ref, y), one, zero)
    last = z.groups_z - 1
    state = lax.fori_loop(0, last - group, lambda i, s: down(groups, last - i, s), state)
    last = z.members - 1
    state = lax.fori_loop(0, last - member, lambda i, s: down(blocks, last - i, s), state)
    for y in ys:
        u, w, total = state[3 * y : 3 * y + 3]
        sums_ref[z.ny + y] = total
        ends_ref[3 * z.ny + y] = u - w * ohm(own_ref, z.faces_at + z.tiles + y)
        for i in reversed(range(z.nz)):
            u_ref[y * z.nz + i] = u
            if i == 0:
                v, wv = rising[y]
                ends_ref[4 * z.ny + y] = 1.0 / (wv * u + v * w)
            w = w + u
            u = u + w * ohm(own_ref, z.faces_at + y * z.nz + i)
        ends_ref[2 * z.ny + y] = u


def solve_row(z, y, sums, f_ref, v_ref, u_ref, ends_ref, store):
    below, above = sums
    scale = ends_ref[4 * z.ny + y]
    after = [None] * z.nz
    total = above
    for i in reversed(range(z.nz)):
        t = y * z.nz + i
        after[i] = total
        total = total + u_ref[t] * f_ref[t]
    low = scale * (ends_ref[2 * z.ny + y] * below + ends_ref[y] * total)
    total = below
    for i in range(z.nz):
        t = y * z.nz + i
        total = total + v_ref[t] * f_ref[t]
        store(i, scale * (u_ref[t] * total + v_ref[t] * after[i]))
    high = scale * (ends_ref[3 * z.ny + y] * total + ends_ref[z.ny + y] * above)
    return low, high


def meet_kernel(z, rates_ref, f_ref, pay_ref, own_group, block_sums, block_transfers, far_transfer, *refs):
    across, refs = refs[: z.groups_z - 1], refs[z.groups_z - 1 :]
    v_ref, u_ref, ends_ref, sums_ref, *y_refs, group_sums, group_transfers, tops = refs
    group = lax.axis_index("gz") // z.members
    near = transfers(z, rates_ref, across[:-1], z.members)
    for i, ref in enumerate((own_group, *across)):
        group_sums[group ^ i] = ref[: 2 * z.lines, :]
        tops[group ^ i] = ref[z.group_top :, :]
    for i, matrix in enumerate(near):
        for n, value in enumerate(matrix):
            group_transfers[group ^ (i + 1), n] = value
    group_transfers[group ^ len(across)] = far_transfer[...]
    both_ways(
        z, rates_ref, pay_ref, (block_sums, block_transfers), (group_sums, group_transfers),
        tops.at[z.groups_z - 1], v_ref, u_ref, ends_ref, sums_ref,
    )
    for ref, y in zip(y_refs, y_picks(z)):

        def store(i, value):
            ref[i * z.species : (i + 1) * z.species, :] = value

        solve_row(z, y, (sums_ref[y], sums_ref[z.ny + y]), f_ref, v_ref, u_ref, ends_ref, store)


def rows_kernel(z, f_ref, v_ref, u_ref, ends_ref, sums_ref, tiles_ref, halo_ref):
    for y in range(z.ny):

        def store(i, value):
            tiles_ref[y * z.nz + i] = value

        low, high = solve_row(
            z, y, (sums_ref[y], sums_ref[z.ny + y]), f_ref, v_ref, u_ref, ends_ref, store
        )
        halo_ref[y] = low
        halo_ref[z.ny + y] = high


def halo_rows(z):
    if z.gy == 2:
        core = lax.axis_index("gy")
        return y_picks(z), [core + j for j in range(z.ny - 1)]
    return list(range(z.ny)), []


def places_of(z, ys):
    return [(y, row) for y in ys for row in range(z.nz)]


def inner_kernel(
    z, tiles_ref, halo_ref, rates_ref, x_faces, arrhenius_ref, proportions_ref, y_faces, z_faces,
    left_ref, right_ref, inverse_ref, base_ref, f_ref
):
    base_sides(z, tiles_ref, rates_ref, x_faces, arrhenius_ref, proportions_ref, base_ref)
    _, ys = halo_rows(z)
    zero = jnp.zeros(z.tile, F32)
    if ys:
        right_sides(
            z, places_of(z, ys), tiles_ref, base_ref, lambda side, y: halo_ref[side * z.ny + y],
            lambda side, row: zero, rates_ref, y_faces, z_faces, left_ref, right_ref, inverse_ref, f_ref,
        )


def second_kernel(
    z, tiles_ref, halo_ref, rates_ref, y_faces, z_faces, left_ref, right_ref, inverse_ref, base_ref,
    inner_ref, v_ref, u_ref, *refs
):
    halos = 1 if z.gy == 2 else 2
    received = refs[:halos]
    pay_ref, f_ref = refs[halos:]
    ys, done = halo_rows(z)
    for y, row in places_of(z, done):
        f_ref[y * z.nz + row] = inner_ref[y * z.nz + row]
    right_sides(
        z, places_of(z, ys), tiles_ref, base_ref, lambda side, y: halo_ref[side * z.ny + y],
        y_halos(z, received), rates_ref, y_faces, z_faces, left_ref, right_ref, inverse_ref, f_ref,
    )
    send_sums(z, f_ref, v_ref, u_ref, pay_ref)


def last_kernel(z, within_ref, f_ref, v_ref, u_ref, ends_ref, *refs):
    *across, out_hbm, rows_ref, sems = refs
    group = lax.axis_index("gz") // z.members
    below, above = within_ref[0], within_ref[1]
    for i, ref in enumerate(reversed(across)):
        lower = (group ^ (i + 1)) < group
        value = ref[...]
        below = below + jnp.where(lower, value, 0.0)
        above = above + jnp.where(lower, 0.0, value)
    blocks = rows_ref.reshape(z.species, z.ny, z.nz, z.nx)
    copies = []
    for y in range(z.ny):

        def store(i, value):
            rows_ref[pl.ds(y * z.nz + i, z.species, stride=z.tiles), :] = value

        sums = below[per_line(z, y)], above[per_line(z, y)]
        solve_row(z, y, sums, f_ref, v_ref, u_ref, ends_ref, store)
        copies.append(pltpu.make_async_copy(blocks.at[:, y], out_hbm.at[:, y], sems.at[y]))
        copies[-1].start()
    for copy in copies:
        copy.wait()


def per_device(z, c, k, warm, sigma, frequency, barrier, proportions):
    in_vmem = pl.BlockSpec(memory_space=pltpu.VMEM)
    hbm = pl.BlockSpec(memory_space=pltpu.HBM)

    def shaped(*shape):
        return jax.ShapeDtypeStruct(shape, F32)

    def call(kernel, outs, ins, scratch=(), spec=in_vmem, out_spec=in_vmem, us=0.5):
        return pl.pallas_call(
            functools.partial(kernel, z),
            out_shape=outs,
            in_specs=[spec] * len(ins),
            out_specs=jax.tree.map(lambda _: out_spec, outs),
            scratch_shapes=list(scratch),
            compiler_params=pltpu.CompilerParams(vmem_limit_bytes=48 * 2**20),
            cost_estimate=pl.CostEstimate(
                flops=0, bytes_accessed=int(us * 3.69e6), transcendentals=0
            ),
        )(*ins)

    def shift(value, axis, by):
        count = lax.axis_size(axis)
        return lax.ppermute(value, axis, [(i, (i + by) % count) for i in range(count)])

    def swap(sends):
        return [shift(value, "gy", by) for value, by in zip(sends, (1, -1))]

    arguments = jnp.concatenate([v.reshape(-1, z.nx) for v in (c, k, warm)])
    halos = 1 if z.gy == 2 else 2
    block = shaped(z.tiles, *z.tile)
    ends_shape = shaped(5 * z.ny, *z.tile)

    def exchange(value, count, unit):
        values = value if isinstance(value, list) else [value] * (count - 1)
        pairs = [[(i, i ^ (k * unit)) for i in range(z.devices)] for k in range(1, count)]
        if isinstance(value, list):
            return [lax.ppermute(v, "gz", p) for v, p in zip(values[::-1], pairs[::-1])][::-1]
        return [lax.ppermute(v, "gz", p) for v, p in zip(values, pairs)]

    def neighbours(near, far):
        last = z.devices - 1
        links = [(i, i + 1) for i in range(1, last, 2)]
        links = [pair for i, j in links for pair in ((i, j), (j, i))]
        ends = [(i, i) for i in (0, last)]
        far_pairs = [(i * z.gy + n, j * z.gy + n) for i, j in links for n in range(z.gy)]
        far_pairs += [(i * z.gy + n, j * z.gy + (n ^ 1)) for i, j in ends for n in range(z.gy)]
        far = lax.ppermute(far, ("gz", "gy"), far_pairs)
        return exchange(near, 2, 1)[0], far

    far, near, *sends = call(
        edges_kernel,
        [shaped(z.edge_rows, z.nx)] * 2 + [shaped(z.nz * (z.species + 1), z.nx)] * halos,
        [arguments],
    )
    near, far = neighbours(near, far)
    received = swap(sends)
    levels = shaped(z.levels, z.tiles, *z.tile)
    faces = shaped(2, z.tiles, z.nx)
    rates, x_faces, left, right, inverse = call(
        coefficients_kernel,
        [shaped(4, *z.tile), faces, levels, levels, block],
        [arguments, sigma.reshape(1, -1)],
        us=1.0,
    )
    vectors = [shift(v, "gy", 1).reshape(1, -1) for v in (frequency, barrier)]
    tiles, arrhenius, base = call(
        source_kernel,
        [block] * 3,
        [arguments, *vectors, proportions, rates, x_faces],
        [pltpu.VMEM((z.tiles, z.nx), F32)],
    )
    x_solve = [left, right, inverse]
    early, y_faces = call(
        early_kernel,
        [block, faces],
        [arguments, tiles, base, rates, *x_solve, *received],
        [pltpu.VMEM((2, z.tiles, z.nx), F32)],
    )
    pay, f, z_faces = call(
        first_kernel,
        [shaped(z.block_rows, z.nx), block, faces],
        [arguments, far, near, tiles, base, rates, *x_solve, early, y_faces, *received],
        [pltpu.VMEM((z.edge_rows, z.nx), F32)] * 2,
    )
    inside = exchange(pay, z.members, 1)
    group = call(
        merge_kernel,
        shaped(z.group_rows, z.nx),
        [rates, pay, *inside],
        [pltpu.VMEM((z.members, z.block_rows, z.nx), F32)],
    )
    across = exchange(group, z.groups_z, z.members)
    matrices = shaped(4 * z.ny, *z.tile)
    block_sums, block_transfers = call(
        inside_kernel,
        [shaped(z.members, 2 * z.lines, z.nx), shaped(z.members, *matrices.shape)],
        [rates, pay, *inside],
    )
    far_transfer = call(far_kernel, matrices, [rates, across[-1]])
    v, u, ends, sums, *sends = call(
        meet_kernel,
        [block, block, ends_shape, shaped(2 * z.ny, *z.tile)]
        + [shaped(z.nz * z.species, z.nx)] * halos,
        [rates, f, pay, group, block_sums, block_transfers, far_transfer, *across],
        [
            pltpu.VMEM((z.groups_z, 2 * z.lines, z.nx), F32),
            pltpu.VMEM((z.groups_z, *matrices.shape), F32),
            pltpu.VMEM((z.groups_z, z.group_rows - z.group_top, z.nx), F32),
        ],
    )

    received = swap(sends)
    tiles, halo = call(rows_kernel, [block, shaped(2 * z.ny, *z.tile)], [f, v, u, ends, sums])
    base, f = call(
        inner_kernel,
        [block, block],
        [tiles, halo, rates, x_faces, arrhenius, proportions, y_faces, z_faces, *x_solve],
    )
    pay, f = call(
        second_kernel,
        [shaped(2, z.lines, z.nx), block],
        [tiles, halo, rates, y_faces, z_faces, *x_solve, base, f, v, u, *received],
    )
    inside = exchange(pay, z.members, 1)
    within, *totals = call(
        total_kernel,
        [shaped(2, z.lines, z.nx)] + [shaped(z.lines, z.nx)] * (z.groups_z - 1),
        [pay, *inside],
    )
    across = exchange(totals[::-1], z.groups_z, z.members)
    return call(
        last_kernel,
        shaped(z.species, z.ny, z.nz, z.nx),
        [within, f, v, u, ends, *across[::-1]],
        [pltpu.VMEM((z.species * z.tiles, z.nx), F32), pltpu.SemaphoreType.DMA((z.ny,))],
        out_spec=hbm,
    )


def solution(mesh):
    def device_program(starting_densities, *others):
        sizes = Sizes(mesh, starting_densities.shape)
        return per_device(sizes, starting_densities, *others)

    return jax.shard_map(
        device_program,
        mesh=mesh,
        in_specs=(
            P(None, "gy", "gz", None),
            P("gy", "gz", None),
            P("gy", "gz", None),
            P(),
            P(),
            P(),
            P(),
        ),
        out_specs=P(None, "gy", "gz", None),
        check_vma=False,
    )
```

```python
import functools

import jax
import jax.numpy as jnp
from jax import lax
from jax.experimental import pallas as pl
from jax.experimental.pallas import tpu as pltpu
from jax.sharding import PartitionSpec as P

F32 = jnp.float32


class Sizes:
    def __init__(self, mesh, block):
        self.species, self.ny, self.nz, self.nx = block
        self.tiles = self.ny * self.nz
        self.lines = self.ny * self.species
        self.devices = mesh.shape["gz"]
        self.gy = mesh.shape["gy"]
        self.levels = (self.nx - 1).bit_length()
        self.pairs = (self.levels - 1) // 2
        self.tile = (self.species, self.nx)
        padded = -(-self.ny // 8) * 8
        self.edge_rows = self.lines + padded
        self.members = 1 << (self.devices.bit_length() // 2)
        self.groups_z = self.devices // self.members
        self.faces_at = 2 * self.lines
        self.block_rows = self.faces_at + self.tiles + padded
        self.group_top = self.faces_at + self.members * self.tiles
        self.group_rows = self.group_top + padded

    def conductance(self, arguments):
        start = self.species * self.tiles
        return arguments.at[start : start + self.tiles]

    def warmth(self, arguments):
        start = (self.species + 1) * self.tiles
        return arguments.at[start : start + self.tiles]

    def groups(self, size):
        for base in range(0, self.tiles, size):
            yield range(base, min(base + size, self.tiles))


def column(ref, z):
    square = (z.species, z.species)
    mine = lax.broadcasted_iota(jnp.int32, square, 0) == lax.broadcasted_iota(jnp.int32, square, 1)
    values = jnp.where(mine, jnp.broadcast_to(ref[...], square), 0.0)
    return jnp.broadcast_to(jnp.sum(values, axis=1, keepdims=True), z.tile)


def spread(ref, row, z):
    return jnp.broadcast_to(ref[pl.ds(row, 1), :], z.tile)


def per_line(z, y):
    return slice(y * z.species, (y + 1) * z.species)


def along_x(v, by, nx):
    return pltpu.roll(v, by % nx, v.ndim - 1)


def flag(condition):
    return jnp.where(condition, 1.0, 0.0).astype(F32)


def inner(axis, count):
    me = lax.axis_index(axis)
    return flag(me > 0), flag(me < count - 1)


def edges_kernel(z, c_ref, far_ref, near_ref, *y_refs):
    k_ref = z.conductance(c_ref)
    odd = lax.axis_index("gz") % 2
    for ref, row in ((near_ref, (1 - odd) * (z.nz - 1)), (far_ref, odd * (z.nz - 1))):
        for y in range(z.ny):
            at = y * z.nz + row
            ref[per_line(z, y), :] = c_ref[pl.ds(at, z.species, stride=z.tiles), :]
            ref[z.lines + y : z.lines + y + 1, :] = k_ref[pl.ds(at, 1), :]
        ref[z.lines + z.ny :, :] = jnp.zeros((z.edge_rows - z.lines - z.ny, z.nx), F32)
    for ref, y in zip(y_refs, y_picks(z)):
        for i in range(z.nz):
            ref[i * z.species : (i + 1) * z.species, :] = c_ref[
                pl.ds(y * z.nz + i, z.species, stride=z.tiles), :
            ]
        start = y * z.nz if isinstance(y, int) else pl.multiple_of(y * z.nz, z.nz)
        ref[z.nz * z.species :, :] = k_ref[pl.ds(start, z.nz), :]


def y_picks(z):
    if z.gy == 2:
        return [jnp.where(lax.axis_index("gy") == 1, 0, z.ny - 1)]
    return [z.ny - 1, 0]


def coefficients_kernel(z, arguments, sigma_ref, rates_ref, faces, left_ref, right_ref, inverse_ref):
    sigma = column(sigma_ref, z)
    rho = 4.0 * sigma
    rates_ref[0] = rho
    rates_ref[1] = 0.015 * sigma
    rates_ref[2] = 4096.0 * sigma
    rates_ref[3] = 1.0 / (1024.0 * sigma)
    k = z.conductance(arguments)[...]
    lanes = lax.broadcasted_iota(jnp.int32, k.shape, 1)
    faces[0] = 0.5 * (k + jnp.where(lanes == 0, 0.0, along_x(k, 1, z.nx)))
    faces[1] = 0.5 * (k + jnp.where(lanes == z.nx - 1, 0.0, along_x(k, -1, z.nx)))
    lanes = lax.broadcasted_iota(jnp.int32, z.tile, 1)
    tiles = range(z.tiles)
    e, d = [], []
    for t in tiles:
        before = rho * spread(faces.at[0], t, z)
        after = rho * spread(faces.at[1], t, z)
        d.append(1.0 + (before + after))
        e.append(jnp.where(lanes == 0, 0.0, before))
    for level in range(z.levels):
        stride = 1 << level
        half = 2 * stride == z.nx
        for t in tiles:
            r = 1.0 / d[t]
            above = along_x(e[t], -stride, z.nx)
            r_before = along_x(r, stride, z.nx)
            left = e[t] * r_before
            right = above * (r_before if half else along_x(r, -stride, z.nx))
            left_ref[level, t] = left + right if half else left
            if not half:
                right_ref[level, t] = right
            d[t] = d[t] - e[t] * left - above * right
            if not half:
                e[t] = left * along_x(e[t], stride, z.nx)
    for t in tiles:
        inverse_ref[t] = 1.0 / d[t]


def source_kernel(
    z, c_ref, frequency_ref, barrier_ref, proportions_ref, rates_ref, faces,
    tiles_ref, arrhenius_ref, base_ref, heat_ref,
):
    frequency, barrier = column(frequency_ref, z), column(barrier_ref, z)
    heat_ref[...] = 1.0 - 1.0 / z.warmth(c_ref)[...]
    for t in range(z.tiles):
        tiles_ref[t] = c_ref[pl.ds(t, z.species, stride=z.tiles), :]
        arrhenius_ref[t] = frequency * jnp.exp(barrier * spread(heat_ref, t, z))
    base_sides(z, tiles_ref, rates_ref, faces, arrhenius_ref, proportions_ref, base_ref)


def base_sides(z, tiles_ref, rates_ref, faces, arrhenius_ref, proportions_ref, base_ref):
    lanes = lax.broadcasted_iota(jnp.int32, z.tile, 1)
    rate = rates_ref[0]
    reacting = jnp.concatenate(
        [arrhenius_ref[t] * jnp.tanh(tiles_ref[t]) for t in range(z.tiles)], axis=1
    )
    source = jnp.dot(
        proportions_ref[...],
        reacting,
        precision=lax.Precision.HIGHEST,
        preferred_element_type=F32,
    )
    for t in range(z.tiles):
        v = tiles_ref[t]
        before = jnp.where(lanes == 0, 0.0, along_x(v, 1, z.nx))
        after = jnp.where(lanes == z.nx - 1, 0.0, along_x(v, -1, z.nx))
        lap = rate * (
            spread(faces.at[1], t, z) * (after - v) - spread(faces.at[0], t, z) * (v - before)
        )
        base_ref[t] = v + lap + source[:, t * z.nx : (t + 1) * z.nx]


def edge_places(z):
    return [(y, row) for y in range(z.ny) for row in sorted({0, z.nz - 1})]


def join_levels(z, t, left, right, joined, at):
    for pair in range(z.pairs):
        stride = 4**pair
        l1, r1, l2, r2 = (ref[2 * pair + n, t] for n in range(2) for ref in (left, right))
        factors = (
            l1 + l2 * along_x(r1, 2 * stride, z.nx),
            r1 + r2 * along_x(l1, -2 * stride, z.nx),
            l2 * along_x(l1, 2 * stride, z.nx),
            r2 * along_x(r1, -2 * stride, z.nx),
        )
        for n, factor in enumerate(factors):
            joined[4 * pair + n, at] = factor


def right_sides(
    z, places, tiles_ref, base_ref, z_halo, y_halo, rates_ref, y_faces, z_faces, left, right, inverse, f_ref,
    joined=None,
):
    rate_y, rate_z = rates_ref[1], rates_ref[2]
    section, lap = [], []
    for y, row in places:
        t = y * z.nz + row
        v = tiles_ref[t]
        z_before = tiles_ref[t - 1] if row else z_halo(0, y)
        z_after = tiles_ref[t + 1] if row < z.nz - 1 else z_halo(1, y)
        if isinstance(y, int):
            y_before = tiles_ref[t - z.nz] if y else y_halo(0, row)
            y_after = tiles_ref[t + z.nz] if y < z.ny - 1 else y_halo(1, row)
        else:
            y_before = jnp.where(y > 0, tiles_ref[jnp.maximum(y - 1, 0) * z.nz + row], y_halo(0, row))
            y_after = jnp.where(
                y < z.ny - 1, tiles_ref[jnp.minimum(y + 1, z.ny - 1) * z.nz + row], y_halo(1, row)
            )
        flux = [spread(faces.at[n], t, z) for faces in (y_faces, z_faces) for n in range(2)]
        lap_y = rate_y * (flux[1] * (y_after - v) - flux[0] * (v - y_before))
        lap_z = rate_z * (flux[3] * (z_after - v) - flux[2] * (v - z_before))
        lap.append(lap_z)
        section.append(base_ref[t] + lap_y + lap_z)
    pairs = z.pairs if joined else 0
    for pair in range(pairs):
        stride = 4**pair
        for i, (y, row) in enumerate(places):
            t = y * z.nz + row
            factors = [joined(4 * pair + n, i) for n in range(4)]
            factors[2:2] = left[2 * pair + 1, t], right[2 * pair + 1, t]
            terms = []
            for factor, by in zip(factors, (1, -1, 2, -2, 3, -3)):
                terms.append(factor * along_x(section[i], by * stride, z.nx))
            section[i] = section[i] + ((terms[0] + terms[1]) + (terms[2] + terms[3])) + (terms[4] + terms[5])
    for level in range(2 * pairs, z.levels):
        stride = 1 << level
        for i, (y, row) in enumerate(places):
            t = y * z.nz + row
            before = along_x(section[i], stride, z.nx)
            more = left[level, t] * before
            if 2 * stride < z.nx:
                more = more + right[level, t] * along_x(section[i], -stride, z.nx)
            section[i] = section[i] + more
    for i, (y, row) in enumerate(places):
        t = y * z.nz + row
        f_ref[t] = section[i] * inverse[t] - 0.5 * lap[i]


def y_halos(z, received):
    low, high = received[0], received[-1]
    low_mask, high_mask = inner("gy", z.gy)

    def halo(side, row):
        lines = per_line(z, row)
        return high[lines, :] * high_mask if side else low[lines, :] * low_mask

    return halo


def send_sums(z, f_ref, v_ref, u_ref, pay_ref):
    for y in range(z.ny):
        tiles = range(y * z.nz, (y + 1) * z.nz)
        pay_ref[0, per_line(z, y), :] = functools.reduce(jnp.add, [v_ref[t] * f_ref[t] for t in tiles])
        pay_ref[1, per_line(z, y), :] = functools.reduce(jnp.add, [u_ref[t] * f_ref[t] for t in tiles])


def total_kernel(z, pay_ref, *refs):
    inside = refs[: z.members - 1]
    within_ref, *out_refs = refs[z.members - 1 :]
    me = lax.axis_index("gz")
    group, member = me // z.members, me % z.members
    below = above = jnp.zeros((z.lines, z.nx), F32)
    rising, falling = pay_ref[0], pay_ref[1]
    for i, ref in enumerate(inside):
        lower = (member ^ (i + 1)) < member
        up, down = ref[0], ref[1]
        rising, falling = rising + up, falling + down
        below = below + jnp.where(lower, up, 0.0)
        above = above + jnp.where(lower, 0.0, down)
    within_ref[0] = below
    within_ref[1] = above
    for i, ref in enumerate(reversed(out_refs)):
        ref[...] = jnp.where((group ^ (i + 1)) > group, rising, falling)


def z_face_pair(z, k_ref, low, high):
    rows = lax.broadcasted_iota(jnp.int32, (z.nz, z.nx), 0)
    for y in range(z.ny):
        here = k_ref[y * z.nz : (y + 1) * z.nz, :]
        before, after = (jnp.broadcast_to(row, here.shape) for row in (low(y), high(y)))
        yield (
            here + jnp.where(rows == 0, before, pltpu.roll(here, 1, 0)),
            here + jnp.where(rows == z.nz - 1, after, pltpu.roll(here, z.nz - 1, 0)),
        )


def early_kernel(z, arguments, tiles_ref, base_ref, rates_ref, left_ref, right_ref, inverse_ref, *refs):
    halos = 1 if z.gy == 2 else 2
    received = refs[:halos]
    f_ref, y_faces, joined_ref, z_faces = refs[halos:]
    for i, (y, row) in enumerate(edge_places(z)):
        join_levels(z, y * z.nz + row, left_ref, right_ref, joined_ref, i)
    k_ref = z.conductance(arguments)
    k = k_ref[...]
    low, high = received[0], received[-1]
    low_mask, high_mask = inner("gy", z.gy)
    k_base = z.nz * z.species
    below = jnp.concatenate([low[k_base:, :] * low_mask, k[: z.tiles - z.nz]], axis=0)
    above = jnp.concatenate([k[z.nz :], high[k_base:, :] * high_mask], axis=0)
    y_faces[0] = 0.5 * (k + below)
    y_faces[1] = 0.5 * (k + above)
    nothing = jnp.zeros((1, z.nx), F32)
    for y, (before, after) in enumerate(z_face_pair(z, k_ref, lambda y: nothing, lambda y: nothing)):
        own = slice(y * z.nz, (y + 1) * z.nz)
        z_faces[0, own, :] = 0.5 * before
        z_faces[1, own, :] = 0.5 * after
    places = [(y, row) for y in range(z.ny) for row in range(1, z.nz - 1)]
    right_sides(
        z, places, tiles_ref, base_ref, None, y_halos(z, received), rates_ref, y_faces, z_faces,
        left_ref, right_ref, inverse_ref, f_ref,
    )


def first_kernel(
    z, arguments, far_ref, near_ref, tiles_ref, base_ref, rates_ref, left_ref, right_ref, inverse_ref,
    early_ref, y_faces, joined_ref, *refs
):
    halos = 1 if z.gy == 2 else 2
    received = refs[:halos]
    pay_ref, f_ref, z_faces, from_below, from_above = refs[halos:]
    k_ref = z.conductance(arguments)
    odd = lax.axis_index("gz") % 2 == 1
    from_below[...] = jnp.where(odd, near_ref[...], far_ref[...])
    from_above[...] = jnp.where(odd, far_ref[...], near_ref[...])
    z_low, z_high = inner("gz", z.devices)
    pay_ref[z.faces_at + z.tiles :, :] = jnp.zeros((z.block_rows - z.faces_at - z.tiles, z.nx), F32)

    def k_low(y):
        return from_below[z.lines + y : z.lines + y + 1, :] * z_low

    def k_high(y):
        return from_above[z.lines + y : z.lines + y + 1, :] * z_high

    for y, (before, after) in enumerate(z_face_pair(z, k_ref, k_low, k_high)):
        own = slice(y * z.nz, (y + 1) * z.nz)
        z_faces[0, own, :] = 0.5 * before
        z_faces[1, own, :] = 0.5 * after
        pay_ref[z.faces_at + y * z.nz : z.faces_at + (y + 1) * z.nz, :] = 1.0 / before
        top = z.faces_at + z.tiles + y
        pay_ref[top : top + 1, :] = 1.0 / after[z.nz - 1 :, :]

    def z_halo(side, y):
        lines = per_line(z, y)
        return from_above[lines, :] * z_high if side else from_below[lines, :] * z_low

    for y in range(z.ny):
        for row in range(1, z.nz - 1):
            f_ref[y * z.nz + row] = early_ref[y * z.nz + row]
    right_sides(
        z, edge_places(z), tiles_ref, base_ref, z_halo, y_halos(z, received), rates_ref, y_faces, z_faces,
        left_ref, right_ref, inverse_ref, f_ref, lambda n, i: joined_ref[n, i],
    )
    ohms = rates_ref[3]
    zero, one = jnp.zeros(z.tile, F32), jnp.ones(z.tile, F32)
    for y in range(z.ny):
        p, q, first, second = (one, zero), (zero, one), zero, zero
        for i in range(z.nz):
            ohm = ohms * spread(pay_ref, z.faces_at + y * z.nz + i, z)
            p, q = advance(p, ohm), advance(q, ohm)
            f = f_ref[y * z.nz + i]
            first = first + p[0] * f
            second = second + q[0] * f
        pay_ref[per_line(z, y), :] = first
        pay_ref[per_line(z, z.ny + y), :] = second


def advance(state, ohm):
    v, w = state
    v = v + w * ohm
    return v, w + v


def merge_kernel(z, rates_ref, pay_ref, *refs):
    *received, group_ref, order = refs
    me = lax.axis_index("gz") % z.members
    order[me] = pay_ref[...]
    for i, ref in enumerate(received):
        order[me ^ (i + 1)] = ref[...]
    ohms = rates_ref[3]
    zero, one = jnp.zeros(z.tile, F32), jnp.ones(z.tile, F32)
    for y in range(z.ny):
        p, q, first, second = (one, zero), (zero, one), zero, zero
        for j in range(z.members):
            s1, s2 = order[j, per_line(z, y), :], order[j, per_line(z, z.ny + y), :]
            first = first + (p[0] * s1 + p[1] * s2)
            second = second + (q[0] * s1 + q[1] * s2)
            if j < z.members - 1:
                for i in range(z.nz):
                    ohm = ohms * spread(order.at[j], z.faces_at + y * z.nz + i, z)
                    p, q = advance(p, ohm), advance(q, ohm)
        group_ref[per_line(z, y), :] = first
        group_ref[per_line(z, z.ny + y), :] = second
    for j in range(z.members):
        start = z.faces_at + j * z.tiles
        group_ref[start : start + z.tiles, :] = order[j, z.faces_at : z.faces_at + z.tiles, :]
    group_ref[z.group_top :, :] = order[z.members - 1, z.faces_at + z.tiles :, :]


def transfers(z, rates_ref, refs, blocks):
    ohms = rates_ref[3]
    zero, one = jnp.zeros(z.tile, F32), jnp.ones(z.tile, F32)

    def block(j, state):
        state = list(state)
        start = z.faces_at + j * z.tiles
        for i in range(z.nz):
            for n, ref in enumerate(refs):
                for y in range(z.ny):
                    ohm = ohms * spread(ref, start + y * z.nz + i, z)
                    at = 4 * (n * z.ny + y)
                    state[at : at + 2] = advance(state[at : at + 2], ohm)
                    state[at + 2 : at + 4] = advance(state[at + 2 : at + 4], ohm)
        return tuple(state)

    state = (one, zero, zero, one) * (z.ny * len(refs))
    state = lax.fori_loop(0, blocks, block, state) if blocks > 1 else block(0, state)
    return [state[4 * z.ny * n : 4 * z.ny * (n + 1)] for n in range(len(refs))]


def inside_kernel(z, rates_ref, *refs):
    *blocks, sums_ref, transfers_ref = refs
    me = lax.axis_index("gz") % z.members
    for i, matrix in enumerate(transfers(z, rates_ref, blocks, 1)):
        sums_ref[me ^ i] = blocks[i][: 2 * z.lines, :]
        for n, value in enumerate(matrix):
            transfers_ref[me ^ i, n] = value


def far_kernel(z, rates_ref, group_ref, out_ref):
    (matrix,) = transfers(z, rates_ref, [group_ref], z.members)
    for n, value in enumerate(matrix):
        out_ref[n] = value


def both_ways(z, rates_ref, own_ref, blocks, groups, top_ref, v_ref, u_ref, ends_ref, sums_ref):
    me = lax.axis_index("gz")
    group, member = me // z.members, me % z.members
    ohms = rates_ref[3]
    zero, one = jnp.zeros(z.tile, F32), jnp.ones(z.tile, F32)
    ys = range(z.ny)

    def ohm(ref, row):
        return ohms * spread(ref, row, z)

    def totals(sums, j, y):
        return sums[j, per_line(z, y), :], sums[j, per_line(z, z.ny + y), :]

    def up(refs, j, state):
        sums, matrices = refs
        out = []
        for y in ys:
            v, w, total = state[3 * y : 3 * y + 3]
            s1, s2 = totals(sums, j, y)
            pv, pw, qv, qw = (matrices[j, 4 * y + n] for n in range(4))
            out += [pv * v + qv * w, pw * v + qw * w, total + (v * s1 + w * s2)]
        return tuple(out)

    def down(refs, j, state):
        sums, matrices = refs
        out = []
        for y in ys:
            u, w, total = state[3 * y : 3 * y + 3]
            s1, s2 = totals(sums, j, y)
            pv, pw, qv, qw = (matrices[j, 4 * y + n] for n in range(4))
            u, w = qw * u + qv * w, pw * u + pv * w
            out += [u, w, total + (u * s1 - w * s2)]
        return tuple(out)

    state = (zero, one, zero) * z.ny
    state = lax.fori_loop(0, group, lambda j, s: up(groups, j, s), state)
    state = lax.fori_loop(0, member, lambda j, s: up(blocks, j, s), state)
    rising = []
    for y in ys:
        pair = state[3 * y : 3 * y + 2]
        sums_ref[y] = state[3 * y + 2]
        ends_ref[y] = pair[0]
        for i in range(z.nz):
            pair = advance(pair, ohm(own_ref, z.faces_at + y * z.nz + i))
            v_ref[y * z.nz + i] = pair[0]
            if i == 0:
                rising.append(pair)
        ends_ref[z.ny + y] = pair[0] + pair[1] * ohm(own_ref, z.faces_at + z.tiles + y)

    state = ()
    for y in ys:
        state += (ohm(top_ref, y), one, zero)
    last = z.groups_z - 1
    state = lax.fori_loop(0, last - group, lambda i, s: down(groups, last - i, s), state)
    last = z.members - 1
    state = lax.fori_loop(0, last - member, lambda i, s: down(blocks, last - i, s), state)
    for y in ys:
        u, w, total = state[3 * y : 3 * y + 3]
        sums_ref[z.ny + y] = total
        ends_ref[3 * z.ny + y] = u - w * ohm(own_ref, z.faces_at + z.tiles + y)
        for i in reversed(range(z.nz)):
            u_ref[y * z.nz + i] = u
            if i == 0:
                v, wv = rising[y]
                ends_ref[4 * z.ny + y] = 1.0 / (wv * u + v * w)
            w = w + u
            u = u + w * ohm(own_ref, z.faces_at + y * z.nz + i)
        ends_ref[2 * z.ny + y] = u


def solve_row(z, y, sums, f_ref, v_ref, u_ref, ends_ref, store):
    below, above = sums
    scale = ends_ref[4 * z.ny + y]
    after = [None] * z.nz
    total = above
    for i in reversed(range(z.nz)):
        t = y * z.nz + i
        after[i] = total
        total = total + u_ref[t] * f_ref[t]
    low = scale * (ends_ref[2 * z.ny + y] * below + ends_ref[y] * total)
    total = below
    for i in range(z.nz):
        t = y * z.nz + i
        total = total + v_ref[t] * f_ref[t]
        store(i, scale * (u_ref[t] * total + v_ref[t] * after[i]))
    high = scale * (ends_ref[3 * z.ny + y] * total + ends_ref[z.ny + y] * above)
    return low, high


def meet_kernel(z, rates_ref, f_ref, pay_ref, own_group, block_sums, block_transfers, far_transfer, *refs):
    across, refs = refs[: z.groups_z - 1], refs[z.groups_z - 1 :]
    v_ref, u_ref, ends_ref, sums_ref, *y_refs, group_sums, group_transfers, tops = refs
    group = lax.axis_index("gz") // z.members
    near = transfers(z, rates_ref, across[:-1], z.members)
    for i, ref in enumerate((own_group, *across)):
        group_sums[group ^ i] = ref[: 2 * z.lines, :]
        tops[group ^ i] = ref[z.group_top :, :]
    for i, matrix in enumerate(near):
        for n, value in enumerate(matrix):
            group_transfers[group ^ (i + 1), n] = value
    group_transfers[group ^ len(across)] = far_transfer[...]
    both_ways(
        z, rates_ref, pay_ref, (block_sums, block_transfers), (group_sums, group_transfers),
        tops.at[z.groups_z - 1], v_ref, u_ref, ends_ref, sums_ref,
    )
    for ref, y in zip(y_refs, y_picks(z)):

        def store(i, value):
            ref[i * z.species : (i + 1) * z.species, :] = value

        solve_row(z, y, (sums_ref[y], sums_ref[z.ny + y]), f_ref, v_ref, u_ref, ends_ref, store)


def rows_kernel(z, f_ref, v_ref, u_ref, ends_ref, sums_ref, tiles_ref, halo_ref):
    for y in range(z.ny):

        def store(i, value):
            tiles_ref[y * z.nz + i] = value

        low, high = solve_row(
            z, y, (sums_ref[y], sums_ref[z.ny + y]), f_ref, v_ref, u_ref, ends_ref, store
        )
        halo_ref[y] = low
        halo_ref[z.ny + y] = high


def halo_rows(z):
    if z.gy == 2:
        core = lax.axis_index("gy")
        return y_picks(z), [core + j for j in range(z.ny - 1)]
    return list(range(z.ny)), []


def places_of(z, ys):
    return [(y, row) for y in ys for row in range(z.nz)]


def inner_kernel(
    z, tiles_ref, halo_ref, rates_ref, x_faces, arrhenius_ref, proportions_ref, y_faces, z_faces,
    left_ref, right_ref, inverse_ref, base_ref, f_ref, joined_ref
):
    ys, _ = halo_rows(z)
    for i, (y, row) in enumerate(places_of(z, ys)):
        join_levels(z, y * z.nz + row, left_ref, right_ref, joined_ref, i)
    base_sides(z, tiles_ref, rates_ref, x_faces, arrhenius_ref, proportions_ref, base_ref)
    _, ys = halo_rows(z)
    zero = jnp.zeros(z.tile, F32)
    if ys:
        right_sides(
            z, places_of(z, ys), tiles_ref, base_ref, lambda side, y: halo_ref[side * z.ny + y],
            lambda side, row: zero, rates_ref, y_faces, z_faces, left_ref, right_ref, inverse_ref, f_ref,
        )


def second_kernel(
    z, tiles_ref, halo_ref, rates_ref, y_faces, z_faces, left_ref, right_ref, inverse_ref, base_ref,
    inner_ref, joined_ref, v_ref, u_ref, *refs
):
    halos = 1 if z.gy == 2 else 2
    received = refs[:halos]
    pay_ref, f_ref = refs[halos:]
    ys, done = halo_rows(z)
    for y, row in places_of(z, done):
        f_ref[y * z.nz + row] = inner_ref[y * z.nz + row]
    right_sides(
        z, places_of(z, ys), tiles_ref, base_ref, lambda side, y: halo_ref[side * z.ny + y],
        y_halos(z, received), rates_ref, y_faces, z_faces, left_ref, right_ref, inverse_ref, f_ref,
        lambda n, i: joined_ref[n, i],
    )
    send_sums(z, f_ref, v_ref, u_ref, pay_ref)


def last_kernel(z, within_ref, f_ref, v_ref, u_ref, ends_ref, *refs):
    *across, out_hbm, rows_ref, sems = refs
    group = lax.axis_index("gz") // z.members
    below, above = within_ref[0], within_ref[1]
    for i, ref in enumerate(reversed(across)):
        lower = (group ^ (i + 1)) < group
        value = ref[...]
        below = below + jnp.where(lower, value, 0.0)
        above = above + jnp.where(lower, 0.0, value)
    blocks = rows_ref.reshape(z.species, z.ny, z.nz, z.nx)
    copies = []
    for y in range(z.ny):

        def store(i, value):
            rows_ref[pl.ds(y * z.nz + i, z.species, stride=z.tiles), :] = value

        sums = below[per_line(z, y)], above[per_line(z, y)]
        solve_row(z, y, sums, f_ref, v_ref, u_ref, ends_ref, store)
        copies.append(pltpu.make_async_copy(blocks.at[:, y], out_hbm.at[:, y], sems.at[y]))
        copies[-1].start()
    for copy in copies:
        copy.wait()


def per_device(z, c, k, warm, sigma, frequency, barrier, proportions):
    in_vmem = pl.BlockSpec(memory_space=pltpu.VMEM)
    hbm = pl.BlockSpec(memory_space=pltpu.HBM)

    def shaped(*shape):
        return jax.ShapeDtypeStruct(shape, F32)

    def call(kernel, outs, ins, scratch=(), spec=in_vmem, out_spec=in_vmem, us=0.5):
        return pl.pallas_call(
            functools.partial(kernel, z),
            out_shape=outs,
            in_specs=[spec] * len(ins),
            out_specs=jax.tree.map(lambda _: out_spec, outs),
            scratch_shapes=list(scratch),
            compiler_params=pltpu.CompilerParams(vmem_limit_bytes=48 * 2**20),
            cost_estimate=pl.CostEstimate(
                flops=0, bytes_accessed=int(us * 3.69e6), transcendentals=0
            ),
        )(*ins)

    def shift(value, axis, by):
        count = lax.axis_size(axis)
        return lax.ppermute(value, axis, [(i, (i + by) % count) for i in range(count)])

    def swap(sends):
        return [shift(value, "gy", by) for value, by in zip(sends, (1, -1))]

    arguments = jnp.concatenate([v.reshape(-1, z.nx) for v in (c, k, warm)])
    halos = 1 if z.gy == 2 else 2
    block = shaped(z.tiles, *z.tile)
    ends_shape = shaped(5 * z.ny, *z.tile)

    def exchange(value, count, unit):
        values = value if isinstance(value, list) else [value] * (count - 1)
        pairs = [[(i, i ^ (k * unit)) for i in range(z.devices)] for k in range(1, count)]
        if isinstance(value, list):
            return [lax.ppermute(v, "gz", p) for v, p in zip(values[::-1], pairs[::-1])][::-1]
        return [lax.ppermute(v, "gz", p) for v, p in zip(values, pairs)]

    def neighbours(near, far):
        last = z.devices - 1
        links = [(i, i + 1) for i in range(1, last, 2)]
        links = [pair for i, j in links for pair in ((i, j), (j, i))]
        ends = [(i, i) for i in (0, last)]
        far_pairs = [(i * z.gy + n, j * z.gy + n) for i, j in links for n in range(z.gy)]
        far_pairs += [(i * z.gy + n, j * z.gy + (n ^ 1)) for i, j in ends for n in range(z.gy)]
        far = lax.ppermute(far, ("gz", "gy"), far_pairs)
        return exchange(near, 2, 1)[0], far

    far, near, *sends = call(
        edges_kernel,
        [shaped(z.edge_rows, z.nx)] * 2 + [shaped(z.nz * (z.species + 1), z.nx)] * halos,
        [arguments],
    )
    near, far = neighbours(near, far)
    received = swap(sends)
    levels = shaped(z.levels, z.tiles, *z.tile)
    faces = shaped(2, z.tiles, z.nx)
    rates, x_faces, left, right, inverse = call(
        coefficients_kernel,
        [shaped(4, *z.tile), faces, levels, levels, block],
        [arguments, sigma.reshape(1, -1)],
        us=1.0,
    )
    vectors = [shift(v, "gy", 1).reshape(1, -1) for v in (frequency, barrier)]
    tiles, arrhenius, base = call(
        source_kernel,
        [block] * 3,
        [arguments, *vectors, proportions, rates, x_faces],
        [pltpu.VMEM((z.tiles, z.nx), F32)],
    )
    x_solve = [left, right, inverse]
    early, y_faces, edge_joined = call(
        early_kernel,
        [block, faces, shaped(4 * z.pairs, len(edge_places(z)), *z.tile)],
        [arguments, tiles, base, rates, *x_solve, *received],
        [pltpu.VMEM((2, z.tiles, z.nx), F32)],
    )
    pay, f, z_faces = call(
        first_kernel,
        [shaped(z.block_rows, z.nx), block, faces],
        [arguments, far, near, tiles, base, rates, *x_solve, early, y_faces, edge_joined, *received],
        [pltpu.VMEM((z.edge_rows, z.nx), F32)] * 2,
    )
    inside = exchange(pay, z.members, 1)
    group = call(
        merge_kernel,
        shaped(z.group_rows, z.nx),
        [rates, pay, *inside],
        [pltpu.VMEM((z.members, z.block_rows, z.nx), F32)],
    )
    across = exchange(group, z.groups_z, z.members)
    matrices = shaped(4 * z.ny, *z.tile)
    block_sums, block_transfers = call(
        inside_kernel,
        [shaped(z.members, 2 * z.lines, z.nx), shaped(z.members, *matrices.shape)],
        [rates, pay, *inside],
    )
    far_transfer = call(far_kernel, matrices, [rates, across[-1]])
    v, u, ends, sums, *sends = call(
        meet_kernel,
        [block, block, ends_shape, shaped(2 * z.ny, *z.tile)]
        + [shaped(z.nz * z.species, z.nx)] * halos,
        [rates, f, pay, group, block_sums, block_transfers, far_transfer, *across],
        [
            pltpu.VMEM((z.groups_z, 2 * z.lines, z.nx), F32),
            pltpu.VMEM((z.groups_z, *matrices.shape), F32),
            pltpu.VMEM((z.groups_z, z.group_rows - z.group_top, z.nx), F32),
        ],
    )

    received = swap(sends)
    tiles, halo = call(rows_kernel, [block, shaped(2 * z.ny, *z.tile)], [f, v, u, ends, sums])
    rows_with_halo = 1 if z.gy == 2 else z.ny
    base, f, joined = call(
        inner_kernel,
        [block, block, shaped(4 * z.pairs, rows_with_halo * z.nz, *z.tile)],
        [tiles, halo, rates, x_faces, arrhenius, proportions, y_faces, z_faces, *x_solve],
    )
    pay, f = call(
        second_kernel,
        [shaped(2, z.lines, z.nx), block],
        [tiles, halo, rates, y_faces, z_faces, *x_solve, base, f, joined, v, u, *received],
    )
    inside = exchange(pay, z.members, 1)
    within, *totals = call(
        total_kernel,
        [shaped(2, z.lines, z.nx)] + [shaped(z.lines, z.nx)] * (z.groups_z - 1),
        [pay, *inside],
    )
    across = exchange(totals[::-1], z.groups_z, z.members)
    return call(
        last_kernel,
        shaped(z.species, z.ny, z.nz, z.nx),
        [within, f, v, u, ends, *across[::-1]],
        [pltpu.VMEM((z.species * z.tiles, z.nx), F32), pltpu.SemaphoreType.DMA((z.ny,))],
        out_spec=hbm,
    )


def solution(mesh):
    def device_program(starting_densities, *others):
        sizes = Sizes(mesh, starting_densities.shape)
        return per_device(sizes, starting_densities, *others)

    return jax.shard_map(
        device_program,
        mesh=mesh,
        in_specs=(
            P(None, "gy", "gz", None),
            P("gy", "gz", None),
            P("gy", "gz", None),
            P(),
            P(),
            P(),
            P(),
        ),
        out_specs=P(None, "gy", "gz", None),
        check_vma=False,
    )
```

```python
import functools

import jax
import jax.numpy as jnp
from jax import lax
from jax.experimental import pallas as pl
from jax.experimental.pallas import tpu as pltpu
from jax.sharding import PartitionSpec as P

F32 = jnp.float32


class Sizes:
    def __init__(self, mesh, block):
        self.species, self.ny, self.nz, self.nx = block
        self.tiles = self.ny * self.nz
        self.lines = self.ny * self.species
        self.devices = mesh.shape["gz"]
        self.gy = mesh.shape["gy"]
        self.levels = (self.nx - 1).bit_length()
        self.pairs = (self.levels - 1) // 2
        self.tile = (self.species, self.nx)
        padded = -(-self.ny // 8) * 8
        self.edge_rows = self.lines + padded
        self.members = 1 << (self.devices.bit_length() // 2)
        self.groups_z = self.devices // self.members
        self.partners = (1, 3, 2) if self.members == 4 else tuple(range(1, self.members))
        self.faces_at = 2 * self.lines
        self.block_rows = self.faces_at + self.tiles + padded
        self.group_top = self.faces_at + self.members * self.tiles
        self.group_rows = self.group_top + padded

    def conductance(self, arguments):
        start = self.species * self.tiles
        return arguments.at[start : start + self.tiles]

    def warmth(self, arguments):
        start = (self.species + 1) * self.tiles
        return arguments.at[start : start + self.tiles]

    def groups(self, size):
        for base in range(0, self.tiles, size):
            yield range(base, min(base + size, self.tiles))


def column(ref, z):
    square = (z.species, z.species)
    mine = lax.broadcasted_iota(jnp.int32, square, 0) == lax.broadcasted_iota(jnp.int32, square, 1)
    values = jnp.where(mine, jnp.broadcast_to(ref[...], square), 0.0)
    return jnp.broadcast_to(jnp.sum(values, axis=1, keepdims=True), z.tile)


def spread(ref, row, z):
    return jnp.broadcast_to(ref[pl.ds(row, 1), :], z.tile)


def per_line(z, y):
    return slice(y * z.species, (y + 1) * z.species)


def along_x(v, by, nx):
    return pltpu.roll(v, by % nx, v.ndim - 1)


def flag(condition):
    return jnp.where(condition, 1.0, 0.0).astype(F32)


def inner(axis, count):
    me = lax.axis_index(axis)
    return flag(me > 0), flag(me < count - 1)


def edges_kernel(z, c_ref, far_ref, near_ref, *y_refs):
    k_ref = z.conductance(c_ref)
    odd = lax.axis_index("gz") % 2
    for ref, row in ((near_ref, (1 - odd) * (z.nz - 1)), (far_ref, odd * (z.nz - 1))):
        for y in range(z.ny):
            at = y * z.nz + row
            ref[per_line(z, y), :] = c_ref[pl.ds(at, z.species, stride=z.tiles), :]
            ref[z.lines + y : z.lines + y + 1, :] = k_ref[pl.ds(at, 1), :]
        ref[z.lines + z.ny :, :] = jnp.zeros((z.edge_rows - z.lines - z.ny, z.nx), F32)
    for ref, y in zip(y_refs, y_picks(z)):
        for i in range(z.nz):
            ref[i * z.species : (i + 1) * z.species, :] = c_ref[
                pl.ds(y * z.nz + i, z.species, stride=z.tiles), :
            ]
        start = y * z.nz if isinstance(y, int) else pl.multiple_of(y * z.nz, z.nz)
        ref[z.nz * z.species :, :] = k_ref[pl.ds(start, z.nz), :]


def y_picks(z):
    if z.gy == 2:
        return [jnp.where(lax.axis_index("gy") == 1, 0, z.ny - 1)]
    return [z.ny - 1, 0]


def coefficients_kernel(z, arguments, sigma_ref, rates_ref, faces, left_ref, right_ref, inverse_ref):
    sigma = column(sigma_ref, z)
    rho = 4.0 * sigma
    rates_ref[0] = rho
    rates_ref[1] = 0.015 * sigma
    rates_ref[2] = 4096.0 * sigma
    rates_ref[3] = 1.0 / (1024.0 * sigma)
    k = z.conductance(arguments)[...]
    lanes = lax.broadcasted_iota(jnp.int32, k.shape, 1)
    faces[0] = 0.5 * (k + jnp.where(lanes == 0, 0.0, along_x(k, 1, z.nx)))
    faces[1] = 0.5 * (k + jnp.where(lanes == z.nx - 1, 0.0, along_x(k, -1, z.nx)))
    lanes = lax.broadcasted_iota(jnp.int32, z.tile, 1)
    tiles = range(z.tiles)
    e, d = [], []
    for t in tiles:
        before = rho * spread(faces.at[0], t, z)
        after = rho * spread(faces.at[1], t, z)
        d.append(1.0 + (before + after))
        e.append(jnp.where(lanes == 0, 0.0, before))
    for level in range(z.levels):
        stride = 1 << level
        half = 2 * stride == z.nx
        for t in tiles:
            r = 1.0 / d[t]
            above = along_x(e[t], -stride, z.nx)
            r_before = along_x(r, stride, z.nx)
            left = e[t] * r_before
            right = above * (r_before if half else along_x(r, -stride, z.nx))
            left_ref[level, t] = left + right if half else left
            if not half:
                right_ref[level, t] = right
            d[t] = d[t] - e[t] * left - above * right
            if not half:
                e[t] = left * along_x(e[t], stride, z.nx)
    for t in tiles:
        inverse_ref[t] = 1.0 / d[t]


def source_kernel(
    z, c_ref, frequency_ref, barrier_ref, proportions_ref, rates_ref, faces,
    tiles_ref, arrhenius_ref, base_ref, heat_ref,
):
    frequency, barrier = column(frequency_ref, z), column(barrier_ref, z)
    heat_ref[...] = 1.0 - 1.0 / z.warmth(c_ref)[...]
    for t in range(z.tiles):
        tiles_ref[t] = c_ref[pl.ds(t, z.species, stride=z.tiles), :]
        arrhenius_ref[t] = frequency * jnp.exp(barrier * spread(heat_ref, t, z))
    base_sides(z, tiles_ref, rates_ref, faces, arrhenius_ref, proportions_ref, base_ref)


def base_sides(z, tiles_ref, rates_ref, faces, arrhenius_ref, proportions_ref, base_ref):
    lanes = lax.broadcasted_iota(jnp.int32, z.tile, 1)
    rate = rates_ref[0]
    reacting = jnp.concatenate(
        [arrhenius_ref[t] * jnp.tanh(tiles_ref[t]) for t in range(z.tiles)], axis=1
    )
    source = jnp.dot(
        proportions_ref[...],
        reacting,
        precision=lax.Precision.HIGHEST,
        preferred_element_type=F32,
    )
    for t in range(z.tiles):
        v = tiles_ref[t]
        before = jnp.where(lanes == 0, 0.0, along_x(v, 1, z.nx))
        after = jnp.where(lanes == z.nx - 1, 0.0, along_x(v, -1, z.nx))
        lap = rate * (
            spread(faces.at[1], t, z) * (after - v) - spread(faces.at[0], t, z) * (v - before)
        )
        base_ref[t] = v + lap + source[:, t * z.nx : (t + 1) * z.nx]


def edge_places(z):
    return [(y, row) for y in range(z.ny) for row in sorted({0, z.nz - 1})]


def join_levels(z, t, left, right, joined, at):
    for pair in range(z.pairs):
        stride = 4**pair
        l1, r1, l2, r2 = (ref[2 * pair + n, t] for n in range(2) for ref in (left, right))
        factors = (
            l1 + l2 * along_x(r1, 2 * stride, z.nx),
            r1 + r2 * along_x(l1, -2 * stride, z.nx),
            l2 * along_x(l1, 2 * stride, z.nx),
            r2 * along_x(r1, -2 * stride, z.nx),
        )
        for n, factor in enumerate(factors):
            joined[4 * pair + n, at] = factor


def right_sides(
    z, places, tiles_ref, base_ref, z_halo, y_halo, rates_ref, y_faces, z_faces, left, right, inverse, f_ref,
    joined=None,
):
    rate_y, rate_z = rates_ref[1], rates_ref[2]
    section, lap = [], []
    for y, row in places:
        t = y * z.nz + row
        v = tiles_ref[t]
        z_before = tiles_ref[t - 1] if row else z_halo(0, y)
        z_after = tiles_ref[t + 1] if row < z.nz - 1 else z_halo(1, y)
        if isinstance(y, int):
            y_before = tiles_ref[t - z.nz] if y else y_halo(0, row)
            y_after = tiles_ref[t + z.nz] if y < z.ny - 1 else y_halo(1, row)
        else:
            y_before = jnp.where(y > 0, tiles_ref[jnp.maximum(y - 1, 0) * z.nz + row], y_halo(0, row))
            y_after = jnp.where(
                y < z.ny - 1, tiles_ref[jnp.minimum(y + 1, z.ny - 1) * z.nz + row], y_halo(1, row)
            )
        flux = [spread(faces.at[n], t, z) for faces in (y_faces, z_faces) for n in range(2)]
        lap_y = rate_y * (flux[1] * (y_after - v) - flux[0] * (v - y_before))
        lap_z = rate_z * (flux[3] * (z_after - v) - flux[2] * (v - z_before))
        lap.append(lap_z)
        section.append(base_ref[t] + lap_y + lap_z)
    pairs = z.pairs if joined else 0
    for pair in range(pairs):
        stride = 4**pair
        for i, (y, row) in enumerate(places):
            t = y * z.nz + row
            factors = [joined(4 * pair + n, i) for n in range(4)]
            factors[2:2] = left[2 * pair + 1, t], right[2 * pair + 1, t]
            terms = []
            for factor, by in zip(factors, (1, -1, 2, -2, 3, -3)):
                terms.append(factor * along_x(section[i], by * stride, z.nx))
            section[i] = section[i] + ((terms[0] + terms[1]) + (terms[2] + terms[3])) + (terms[4] + terms[5])
    for level in range(2 * pairs, z.levels):
        stride = 1 << level
        for i, (y, row) in enumerate(places):
            t = y * z.nz + row
            before = along_x(section[i], stride, z.nx)
            more = left[level, t] * before
            if 2 * stride < z.nx:
                more = more + right[level, t] * along_x(section[i], -stride, z.nx)
            section[i] = section[i] + more
    for i, (y, row) in enumerate(places):
        t = y * z.nz + row
        f_ref[t] = section[i] * inverse[t] - 0.5 * lap[i]


def y_halos(z, received):
    low, high = received[0], received[-1]
    low_mask, high_mask = inner("gy", z.gy)

    def halo(side, row):
        lines = per_line(z, row)
        return high[lines, :] * high_mask if side else low[lines, :] * low_mask

    return halo


def send_sums(z, f_ref, v_ref, u_ref, pay_ref):
    for y in range(z.ny):
        tiles = range(y * z.nz, (y + 1) * z.nz)
        pay_ref[0, per_line(z, y), :] = functools.reduce(jnp.add, [v_ref[t] * f_ref[t] for t in tiles])
        pay_ref[1, per_line(z, y), :] = functools.reduce(jnp.add, [u_ref[t] * f_ref[t] for t in tiles])


def total_kernel(z, pay_ref, *refs):
    inside = refs[: z.members - 1]
    within_ref, *out_refs = refs[z.members - 1 :]
    me = lax.axis_index("gz")
    group, member = me // z.members, me % z.members
    below = above = jnp.zeros((z.lines, z.nx), F32)
    rising, falling = pay_ref[0], pay_ref[1]
    for k, ref in zip(z.partners, inside):
        lower = (member ^ k) < member
        up, down = ref[0], ref[1]
        rising, falling = rising + up, falling + down
        below = below + jnp.where(lower, up, 0.0)
        above = above + jnp.where(lower, 0.0, down)
    within_ref[0] = below
    within_ref[1] = above
    for i, ref in enumerate(reversed(out_refs)):
        ref[...] = jnp.where((group ^ (i + 1)) > group, rising, falling)


def z_face_pair(z, k_ref, low, high):
    rows = lax.broadcasted_iota(jnp.int32, (z.nz, z.nx), 0)
    for y in range(z.ny):
        here = k_ref[y * z.nz : (y + 1) * z.nz, :]
        before, after = (jnp.broadcast_to(row, here.shape) for row in (low(y), high(y)))
        yield (
            here + jnp.where(rows == 0, before, pltpu.roll(here, 1, 0)),
            here + jnp.where(rows == z.nz - 1, after, pltpu.roll(here, z.nz - 1, 0)),
        )


def early_kernel(z, arguments, tiles_ref, base_ref, rates_ref, left_ref, right_ref, inverse_ref, *refs):
    halos = 1 if z.gy == 2 else 2
    received = refs[:halos]
    f_ref, y_faces, joined_ref, z_faces = refs[halos:]
    for i, (y, row) in enumerate(edge_places(z)):
        join_levels(z, y * z.nz + row, left_ref, right_ref, joined_ref, i)
    k_ref = z.conductance(arguments)
    k = k_ref[...]
    low, high = received[0], received[-1]
    low_mask, high_mask = inner("gy", z.gy)
    k_base = z.nz * z.species
    below = jnp.concatenate([low[k_base:, :] * low_mask, k[: z.tiles - z.nz]], axis=0)
    above = jnp.concatenate([k[z.nz :], high[k_base:, :] * high_mask], axis=0)
    y_faces[0] = 0.5 * (k + below)
    y_faces[1] = 0.5 * (k + above)
    nothing = jnp.zeros((1, z.nx), F32)
    for y, (before, after) in enumerate(z_face_pair(z, k_ref, lambda y: nothing, lambda y: nothing)):
        own = slice(y * z.nz, (y + 1) * z.nz)
        z_faces[0, own, :] = 0.5 * before
        z_faces[1, own, :] = 0.5 * after
    places = [(y, row) for y in range(z.ny) for row in range(1, z.nz - 1)]
    right_sides(
        z, places, tiles_ref, base_ref, None, y_halos(z, received), rates_ref, y_faces, z_faces,
        left_ref, right_ref, inverse_ref, f_ref,
    )


def first_kernel(
    z, arguments, far_ref, near_ref, tiles_ref, base_ref, rates_ref, left_ref, right_ref, inverse_ref,
    early_ref, y_faces, joined_ref, *refs
):
    halos = 1 if z.gy == 2 else 2
    received = refs[:halos]
    pay_ref, f_ref, z_faces, from_below, from_above = refs[halos:]
    k_ref = z.conductance(arguments)
    odd = lax.axis_index("gz") % 2 == 1
    from_below[...] = jnp.where(odd, near_ref[...], far_ref[...])
    from_above[...] = jnp.where(odd, far_ref[...], near_ref[...])
    z_low, z_high = inner("gz", z.devices)
    pay_ref[z.faces_at + z.tiles :, :] = jnp.zeros((z.block_rows - z.faces_at - z.tiles, z.nx), F32)

    def k_low(y):
        return from_below[z.lines + y : z.lines + y + 1, :] * z_low

    def k_high(y):
        return from_above[z.lines + y : z.lines + y + 1, :] * z_high

    for y, (before, after) in enumerate(z_face_pair(z, k_ref, k_low, k_high)):
        own = slice(y * z.nz, (y + 1) * z.nz)
        z_faces[0, own, :] = 0.5 * before
        z_faces[1, own, :] = 0.5 * after
        pay_ref[z.faces_at + y * z.nz : z.faces_at + (y + 1) * z.nz, :] = 1.0 / before
        top = z.faces_at + z.tiles + y
        pay_ref[top : top + 1, :] = 1.0 / after[z.nz - 1 :, :]

    def z_halo(side, y):
        lines = per_line(z, y)
        return from_above[lines, :] * z_high if side else from_below[lines, :] * z_low

    for y in range(z.ny):
        for row in range(1, z.nz - 1):
            f_ref[y * z.nz + row] = early_ref[y * z.nz + row]
    right_sides(
        z, edge_places(z), tiles_ref, base_ref, z_halo, y_halos(z, received), rates_ref, y_faces, z_faces,
        left_ref, right_ref, inverse_ref, f_ref, lambda n, i: joined_ref[n, i],
    )
    ohms = rates_ref[3]
    zero, one = jnp.zeros(z.tile, F32), jnp.ones(z.tile, F32)
    for y in range(z.ny):
        p, q, first, second = (one, zero), (zero, one), zero, zero
        for i in range(z.nz):
            ohm = ohms * spread(pay_ref, z.faces_at + y * z.nz + i, z)
            p, q = advance(p, ohm), advance(q, ohm)
            f = f_ref[y * z.nz + i]
            first = first + p[0] * f
            second = second + q[0] * f
        pay_ref[per_line(z, y), :] = first
        pay_ref[per_line(z, z.ny + y), :] = second


def advance(state, ohm):
    v, w = state
    v = v + w * ohm
    return v, w + v


def merge_kernel(z, rates_ref, pay_ref, *refs):
    *received, group_ref, order = refs
    me = lax.axis_index("gz") % z.members
    order[me] = pay_ref[...]
    for k, ref in zip(z.partners, received):
        order[me ^ k] = ref[...]
    ohms = rates_ref[3]
    zero, one = jnp.zeros(z.tile, F32), jnp.ones(z.tile, F32)
    for y in range(z.ny):
        p, q, first, second = (one, zero), (zero, one), zero, zero
        for j in range(z.members):
            s1, s2 = order[j, per_line(z, y), :], order[j, per_line(z, z.ny + y), :]
            first = first + (p[0] * s1 + p[1] * s2)
            second = second + (q[0] * s1 + q[1] * s2)
            if j < z.members - 1:
                for i in range(z.nz):
                    ohm = ohms * spread(order.at[j], z.faces_at + y * z.nz + i, z)
                    p, q = advance(p, ohm), advance(q, ohm)
        group_ref[per_line(z, y), :] = first
        group_ref[per_line(z, z.ny + y), :] = second
    for j in range(z.members):
        start = z.faces_at + j * z.tiles
        group_ref[start : start + z.tiles, :] = order[j, z.faces_at : z.faces_at + z.tiles, :]
    group_ref[z.group_top :, :] = order[z.members - 1, z.faces_at + z.tiles :, :]


def transfers(z, rates_ref, refs, blocks):
    ohms = rates_ref[3]
    zero, one = jnp.zeros(z.tile, F32), jnp.ones(z.tile, F32)

    def block(j, state):
        state = list(state)
        start = z.faces_at + j * z.tiles
        for i in range(z.nz):
            for n, ref in enumerate(refs):
                for y in range(z.ny):
                    ohm = ohms * spread(ref, start + y * z.nz + i, z)
                    at = 4 * (n * z.ny + y)
                    state[at : at + 2] = advance(state[at : at + 2], ohm)
                    state[at + 2 : at + 4] = advance(state[at + 2 : at + 4], ohm)
        return tuple(state)

    state = (one, zero, zero, one) * (z.ny * len(refs))
    state = lax.fori_loop(0, blocks, block, state) if blocks > 1 else block(0, state)
    return [state[4 * z.ny * n : 4 * z.ny * (n + 1)] for n in range(len(refs))]


def inside_kernel(z, rates_ref, *refs):
    *blocks, sums_ref, transfers_ref = refs
    me = lax.axis_index("gz") % z.members
    for k, ref, matrix in zip((0, *z.partners), blocks, transfers(z, rates_ref, blocks, 1)):
        sums_ref[me ^ k] = ref[: 2 * z.lines, :]
        for n, value in enumerate(matrix):
            transfers_ref[me ^ k, n] = value


def far_kernel(z, rates_ref, group_ref, out_ref):
    (matrix,) = transfers(z, rates_ref, [group_ref], z.members)
    for n, value in enumerate(matrix):
        out_ref[n] = value


def both_ways(z, rates_ref, own_ref, blocks, groups, top_ref, v_ref, u_ref, ends_ref, sums_ref):
    me = lax.axis_index("gz")
    group, member = me // z.members, me % z.members
    ohms = rates_ref[3]
    zero, one = jnp.zeros(z.tile, F32), jnp.ones(z.tile, F32)
    ys = range(z.ny)

    def ohm(ref, row):
        return ohms * spread(ref, row, z)

    def totals(sums, j, y):
        return sums[j, per_line(z, y), :], sums[j, per_line(z, z.ny + y), :]

    def up(refs, j, state):
        sums, matrices = refs
        out = []
        for y in ys:
            v, w, total = state[3 * y : 3 * y + 3]
            s1, s2 = totals(sums, j, y)
            pv, pw, qv, qw = (matrices[j, 4 * y + n] for n in range(4))
            out += [pv * v + qv * w, pw * v + qw * w, total + (v * s1 + w * s2)]
        return tuple(out)

    def down(refs, j, state):
        sums, matrices = refs
        out = []
        for y in ys:
            u, w, total = state[3 * y : 3 * y + 3]
            s1, s2 = totals(sums, j, y)
            pv, pw, qv, qw = (matrices[j, 4 * y + n] for n in range(4))
            u, w = qw * u + qv * w, pw * u + pv * w
            out += [u, w, total + (u * s1 - w * s2)]
        return tuple(out)

    state = (zero, one, zero) * z.ny
    state = lax.fori_loop(0, group, lambda j, s: up(groups, j, s), state)
    state = lax.fori_loop(0, member, lambda j, s: up(blocks, j, s), state)
    rising = []
    for y in ys:
        pair = state[3 * y : 3 * y + 2]
        sums_ref[y] = state[3 * y + 2]
        ends_ref[y] = pair[0]
        for i in range(z.nz):
            pair = advance(pair, ohm(own_ref, z.faces_at + y * z.nz + i))
            v_ref[y * z.nz + i] = pair[0]
            if i == 0:
                rising.append(pair)
        ends_ref[z.ny + y] = pair[0] + pair[1] * ohm(own_ref, z.faces_at + z.tiles + y)

    state = ()
    for y in ys:
        state += (ohm(top_ref, y), one, zero)
    last = z.groups_z - 1
    state = lax.fori_loop(0, last - group, lambda i, s: down(groups, last - i, s), state)
    last = z.members - 1
    state = lax.fori_loop(0, last - member, lambda i, s: down(blocks, last - i, s), state)
    for y in ys:
        u, w, total = state[3 * y : 3 * y + 3]
        sums_ref[z.ny + y] = total
        ends_ref[3 * z.ny + y] = u - w * ohm(own_ref, z.faces_at + z.tiles + y)
        for i in reversed(range(z.nz)):
            u_ref[y * z.nz + i] = u
            if i == 0:
                v, wv = rising[y]
                ends_ref[4 * z.ny + y] = 1.0 / (wv * u + v * w)
            w = w + u
            u = u + w * ohm(own_ref, z.faces_at + y * z.nz + i)
        ends_ref[2 * z.ny + y] = u


def solve_row(z, y, sums, f_ref, v_ref, u_ref, ends_ref, store):
    below, above = sums
    scale = ends_ref[4 * z.ny + y]
    after = [None] * z.nz
    total = above
    for i in reversed(range(z.nz)):
        t = y * z.nz + i
        after[i] = total
        total = total + u_ref[t] * f_ref[t]
    low = scale * (ends_ref[2 * z.ny + y] * below + ends_ref[y] * total)
    total = below
    for i in range(z.nz):
        t = y * z.nz + i
        total = total + v_ref[t] * f_ref[t]
        store(i, scale * (u_ref[t] * total + v_ref[t] * after[i]))
    high = scale * (ends_ref[3 * z.ny + y] * total + ends_ref[z.ny + y] * above)
    return low, high


def meet_kernel(z, rates_ref, f_ref, pay_ref, own_group, block_sums, block_transfers, far_transfer, *refs):
    across, refs = refs[: z.groups_z - 1], refs[z.groups_z - 1 :]
    v_ref, u_ref, ends_ref, sums_ref, *y_refs, group_sums, group_transfers, tops = refs
    group = lax.axis_index("gz") // z.members
    near = transfers(z, rates_ref, across[:-1], z.members)
    for i, ref in enumerate((own_group, *across)):
        group_sums[group ^ i] = ref[: 2 * z.lines, :]
        tops[group ^ i] = ref[z.group_top :, :]
    for i, matrix in enumerate(near):
        for n, value in enumerate(matrix):
            group_transfers[group ^ (i + 1), n] = value
    group_transfers[group ^ len(across)] = far_transfer[...]
    both_ways(
        z, rates_ref, pay_ref, (block_sums, block_transfers), (group_sums, group_transfers),
        tops.at[z.groups_z - 1], v_ref, u_ref, ends_ref, sums_ref,
    )
    for ref, y in zip(y_refs, y_picks(z)):

        def store(i, value):
            ref[i * z.species : (i + 1) * z.species, :] = value

        solve_row(z, y, (sums_ref[y], sums_ref[z.ny + y]), f_ref, v_ref, u_ref, ends_ref, store)


def rows_kernel(z, f_ref, v_ref, u_ref, ends_ref, sums_ref, tiles_ref, halo_ref):
    for y in range(z.ny):

        def store(i, value):
            tiles_ref[y * z.nz + i] = value

        low, high = solve_row(
            z, y, (sums_ref[y], sums_ref[z.ny + y]), f_ref, v_ref, u_ref, ends_ref, store
        )
        halo_ref[y] = low
        halo_ref[z.ny + y] = high


def halo_rows(z):
    if z.gy == 2:
        core = lax.axis_index("gy")
        return y_picks(z), [core + j for j in range(z.ny - 1)]
    return list(range(z.ny)), []


def places_of(z, ys):
    return [(y, row) for y in ys for row in range(z.nz)]


def inner_kernel(
    z, tiles_ref, halo_ref, rates_ref, x_faces, arrhenius_ref, proportions_ref, y_faces, z_faces,
    left_ref, right_ref, inverse_ref, base_ref, f_ref, joined_ref
):
    ys, _ = halo_rows(z)
    for i, (y, row) in enumerate(places_of(z, ys)):
        join_levels(z, y * z.nz + row, left_ref, right_ref, joined_ref, i)
    base_sides(z, tiles_ref, rates_ref, x_faces, arrhenius_ref, proportions_ref, base_ref)
    _, ys = halo_rows(z)
    zero = jnp.zeros(z.tile, F32)
    if ys:
        right_sides(
            z, places_of(z, ys), tiles_ref, base_ref, lambda side, y: halo_ref[side * z.ny + y],
            lambda side, row: zero, rates_ref, y_faces, z_faces, left_ref, right_ref, inverse_ref, f_ref,
        )


def second_kernel(
    z, tiles_ref, halo_ref, rates_ref, y_faces, z_faces, left_ref, right_ref, inverse_ref, base_ref,
    inner_ref, joined_ref, v_ref, u_ref, *refs
):
    halos = 1 if z.gy == 2 else 2
    received = refs[:halos]
    pay_ref, f_ref = refs[halos:]
    ys, done = halo_rows(z)
    for y, row in places_of(z, done):
        f_ref[y * z.nz + row] = inner_ref[y * z.nz + row]
    right_sides(
        z, places_of(z, ys), tiles_ref, base_ref, lambda side, y: halo_ref[side * z.ny + y],
        y_halos(z, received), rates_ref, y_faces, z_faces, left_ref, right_ref, inverse_ref, f_ref,
        lambda n, i: joined_ref[n, i],
    )
    send_sums(z, f_ref, v_ref, u_ref, pay_ref)


def last_kernel(z, within_ref, f_ref, v_ref, u_ref, ends_ref, *refs):
    *across, out_hbm, rows_ref, sems = refs
    group = lax.axis_index("gz") // z.members
    below, above = within_ref[0], within_ref[1]
    for i, ref in enumerate(reversed(across)):
        lower = (group ^ (i + 1)) < group
        value = ref[...]
        below = below + jnp.where(lower, value, 0.0)
        above = above + jnp.where(lower, 0.0, value)
    blocks = rows_ref.reshape(z.species, z.ny, z.nz, z.nx)
    copies = []
    for y in range(z.ny):

        def store(i, value):
            rows_ref[pl.ds(y * z.nz + i, z.species, stride=z.tiles), :] = value

        sums = below[per_line(z, y)], above[per_line(z, y)]
        solve_row(z, y, sums, f_ref, v_ref, u_ref, ends_ref, store)
        copies.append(pltpu.make_async_copy(blocks.at[:, y], out_hbm.at[:, y], sems.at[y]))
        copies[-1].start()
    for copy in copies:
        copy.wait()


def per_device(z, c, k, warm, sigma, frequency, barrier, proportions):
    in_vmem = pl.BlockSpec(memory_space=pltpu.VMEM)
    hbm = pl.BlockSpec(memory_space=pltpu.HBM)

    def shaped(*shape):
        return jax.ShapeDtypeStruct(shape, F32)

    def call(kernel, outs, ins, scratch=(), spec=in_vmem, out_spec=in_vmem, us=0.5):
        return pl.pallas_call(
            functools.partial(kernel, z),
            out_shape=outs,
            in_specs=[spec] * len(ins),
            out_specs=jax.tree.map(lambda _: out_spec, outs),
            scratch_shapes=list(scratch),
            compiler_params=pltpu.CompilerParams(vmem_limit_bytes=48 * 2**20),
            cost_estimate=pl.CostEstimate(
                flops=0, bytes_accessed=int(us * 3.69e6), transcendentals=0
            ),
        )(*ins)

    def shift(value, axis, by):
        count = lax.axis_size(axis)
        return lax.ppermute(value, axis, [(i, (i + by) % count) for i in range(count)])

    def swap(sends):
        return [shift(value, "gy", by) for value, by in zip(sends, (1, -1))]

    arguments = jnp.concatenate([v.reshape(-1, z.nx) for v in (c, k, warm)])
    halos = 1 if z.gy == 2 else 2
    block = shaped(z.tiles, *z.tile)
    ends_shape = shaped(5 * z.ny, *z.tile)

    def exchange(value, count, unit):
        values = value if isinstance(value, list) else [value] * (count - 1)
        pairs = [[(i, i ^ (k * unit)) for i in range(z.devices)] for k in range(1, count)]
        if isinstance(value, list):
            return [lax.ppermute(v, "gz", p) for v, p in zip(values[::-1], pairs[::-1])][::-1]
        return [lax.ppermute(v, "gz", p) for v, p in zip(values, pairs)]

    def exchange_inside(value):
        received = exchange(value, z.members, 1)
        return [received[k - 1] for k in z.partners]

    def neighbours(near, far):
        last = z.devices - 1
        links = [(i, i + 1) for i in range(1, last, 2)]
        links = [pair for i, j in links for pair in ((i, j), (j, i))]
        ends = [(i, i) for i in (0, last)]
        far_pairs = [(i * z.gy + n, j * z.gy + n) for i, j in links for n in range(z.gy)]
        far_pairs += [(i * z.gy + n, j * z.gy + (n ^ 1)) for i, j in ends for n in range(z.gy)]
        far = lax.ppermute(far, ("gz", "gy"), far_pairs)
        return exchange(near, 2, 1)[0], far

    far, near, *sends = call(
        edges_kernel,
        [shaped(z.edge_rows, z.nx)] * 2 + [shaped(z.nz * (z.species + 1), z.nx)] * halos,
        [arguments],
    )
    near, far = neighbours(near, far)
    received = swap(sends)
    levels = shaped(z.levels, z.tiles, *z.tile)
    faces = shaped(2, z.tiles, z.nx)
    rates, x_faces, left, right, inverse = call(
        coefficients_kernel,
        [shaped(4, *z.tile), faces, levels, levels, block],
        [arguments, sigma.reshape(1, -1)],
        us=1.0,
    )
    vectors = [shift(v, "gy", 1).reshape(1, -1) for v in (frequency, barrier)]
    tiles, arrhenius, base = call(
        source_kernel,
        [block] * 3,
        [arguments, *vectors, proportions, rates, x_faces],
        [pltpu.VMEM((z.tiles, z.nx), F32)],
    )
    x_solve = [left, right, inverse]
    early, y_faces, edge_joined = call(
        early_kernel,
        [block, faces, shaped(4 * z.pairs, len(edge_places(z)), *z.tile)],
        [arguments, tiles, base, rates, *x_solve, *received],
        [pltpu.VMEM((2, z.tiles, z.nx), F32)],
    )
    pay, f, z_faces = call(
        first_kernel,
        [shaped(z.block_rows, z.nx), block, faces],
        [arguments, far, near, tiles, base, rates, *x_solve, early, y_faces, edge_joined, *received],
        [pltpu.VMEM((z.edge_rows, z.nx), F32)] * 2,
    )
    inside = exchange_inside(pay)
    group = call(
        merge_kernel,
        shaped(z.group_rows, z.nx),
        [rates, pay, *inside],
        [pltpu.VMEM((z.members, z.block_rows, z.nx), F32)],
    )
    across = exchange(group, z.groups_z, z.members)
    matrices = shaped(4 * z.ny, *z.tile)
    block_sums, block_transfers = call(
        inside_kernel,
        [shaped(z.members, 2 * z.lines, z.nx), shaped(z.members, *matrices.shape)],
        [rates, pay, *inside],
    )
    far_transfer = call(far_kernel, matrices, [rates, across[-1]])
    v, u, ends, sums, *sends = call(
        meet_kernel,
        [block, block, ends_shape, shaped(2 * z.ny, *z.tile)]
        + [shaped(z.nz * z.species, z.nx)] * halos,
        [rates, f, pay, group, block_sums, block_transfers, far_transfer, *across],
        [
            pltpu.VMEM((z.groups_z, 2 * z.lines, z.nx), F32),
            pltpu.VMEM((z.groups_z, *matrices.shape), F32),
            pltpu.VMEM((z.groups_z, z.group_rows - z.group_top, z.nx), F32),
        ],
    )

    received = swap(sends)
    tiles, halo = call(rows_kernel, [block, shaped(2 * z.ny, *z.tile)], [f, v, u, ends, sums])
    rows_with_halo = 1 if z.gy == 2 else z.ny
    base, f, joined = call(
        inner_kernel,
        [block, block, shaped(4 * z.pairs, rows_with_halo * z.nz, *z.tile)],
        [tiles, halo, rates, x_faces, arrhenius, proportions, y_faces, z_faces, *x_solve],
    )
    pay, f = call(
        second_kernel,
        [shaped(2, z.lines, z.nx), block],
        [tiles, halo, rates, y_faces, z_faces, *x_solve, base, f, joined, v, u, *received],
    )
    inside = exchange_inside(pay)
    within, *totals = call(
        total_kernel,
        [shaped(2, z.lines, z.nx)] + [shaped(z.lines, z.nx)] * (z.groups_z - 1),
        [pay, *inside],
    )
    across = exchange(totals[::-1], z.groups_z, z.members)
    return call(
        last_kernel,
        shaped(z.species, z.ny, z.nz, z.nx),
        [within, f, v, u, ends, *across[::-1]],
        [pltpu.VMEM((z.species * z.tiles, z.nx), F32), pltpu.SemaphoreType.DMA((z.ny,))],
        out_spec=hbm,
    )


def solution(mesh):
    def device_program(starting_densities, *others):
        sizes = Sizes(mesh, starting_densities.shape)
        return per_device(sizes, starting_densities, *others)

    return jax.shard_map(
        device_program,
        mesh=mesh,
        in_specs=(
            P(None, "gy", "gz", None),
            P("gy", "gz", None),
            P("gy", "gz", None),
            P(),
            P(),
            P(),
            P(),
        ),
        out_specs=P(None, "gy", "gz", None),
        check_vma=False,
    )
```

```python
import functools

import jax
import jax.numpy as jnp
from jax import lax
from jax.experimental import pallas as pl
from jax.experimental.pallas import tpu as pltpu
from jax.sharding import PartitionSpec as P

F32 = jnp.float32


class Sizes:
    def __init__(self, mesh, block):
        self.species, self.ny, self.nz, self.nx = block
        self.tiles = self.ny * self.nz
        self.lines = self.ny * self.species
        self.devices = mesh.shape["gz"]
        self.gy = mesh.shape["gy"]
        self.levels = (self.nx - 1).bit_length()
        self.pairs = (self.levels - 1) // 2
        self.tile = (self.species, self.nx)
        padded = -(-self.ny // 8) * 8
        self.edge_rows = self.lines + padded
        self.members = 1 << (self.devices.bit_length() // 2)
        self.groups_z = self.devices // self.members
        self.partners = (1, 3, 2) if self.members == 4 else tuple(range(1, self.members))
        self.faces_at = 2 * self.lines
        self.block_rows = self.faces_at + self.tiles + padded
        self.group_top = self.faces_at + self.members * self.tiles
        self.group_rows = self.group_top + padded

    def conductance(self, arguments):
        start = self.species * self.tiles
        return arguments.at[start : start + self.tiles]

    def warmth(self, arguments):
        start = (self.species + 1) * self.tiles
        return arguments.at[start : start + self.tiles]

    def groups(self, size):
        for base in range(0, self.tiles, size):
            yield range(base, min(base + size, self.tiles))


def column(ref, z):
    square = (z.species, z.species)
    mine = lax.broadcasted_iota(jnp.int32, square, 0) == lax.broadcasted_iota(jnp.int32, square, 1)
    values = jnp.where(mine, jnp.broadcast_to(ref[...], square), 0.0)
    return jnp.broadcast_to(jnp.sum(values, axis=1, keepdims=True), z.tile)


def spread(ref, row, z):
    return jnp.broadcast_to(ref[pl.ds(row, 1), :], z.tile)


def per_line(z, y):
    return slice(y * z.species, (y + 1) * z.species)


def along_x(v, by, nx):
    return pltpu.roll(v, by % nx, v.ndim - 1)


def flag(condition):
    return jnp.where(condition, 1.0, 0.0).astype(F32)


def inner(axis, count):
    me = lax.axis_index(axis)
    return flag(me > 0), flag(me < count - 1)


def edges_kernel(z, c_ref, far_ref, near_ref, *y_refs):
    k_ref = z.conductance(c_ref)
    odd = lax.axis_index("gz") % 2
    for ref, row in ((near_ref, (1 - odd) * (z.nz - 1)), (far_ref, odd * (z.nz - 1))):
        for y in range(z.ny):
            at = y * z.nz + row
            ref[per_line(z, y), :] = c_ref[pl.ds(at, z.species, stride=z.tiles), :]
            ref[z.lines + y : z.lines + y + 1, :] = k_ref[pl.ds(at, 1), :]
        ref[z.lines + z.ny :, :] = jnp.zeros((z.edge_rows - z.lines - z.ny, z.nx), F32)
    for ref, y in zip(y_refs, y_picks(z)):
        for i in range(z.nz):
            ref[i * z.species : (i + 1) * z.species, :] = c_ref[
                pl.ds(y * z.nz + i, z.species, stride=z.tiles), :
            ]
        start = y * z.nz if isinstance(y, int) else pl.multiple_of(y * z.nz, z.nz)
        ref[z.nz * z.species :, :] = k_ref[pl.ds(start, z.nz), :]


def y_picks(z):
    if z.gy == 2:
        return [jnp.where(lax.axis_index("gy") == 1, 0, z.ny - 1)]
    return [z.ny - 1, 0]


def coefficients_kernel(z, arguments, sigma_ref, rates_ref, faces, left_ref, right_ref, inverse_ref):
    sigma = column(sigma_ref, z)
    rho = 4.0 * sigma
    rates_ref[0] = rho
    rates_ref[1] = 0.015 * sigma
    rates_ref[2] = 4096.0 * sigma
    rates_ref[3] = 1.0 / (1024.0 * sigma)
    k = z.conductance(arguments)[...]
    lanes = lax.broadcasted_iota(jnp.int32, k.shape, 1)
    faces[0] = 0.5 * (k + jnp.where(lanes == 0, 0.0, along_x(k, 1, z.nx)))
    faces[1] = 0.5 * (k + jnp.where(lanes == z.nx - 1, 0.0, along_x(k, -1, z.nx)))
    lanes = lax.broadcasted_iota(jnp.int32, z.tile, 1)
    tiles = range(z.tiles)
    e, d = [], []
    for t in tiles:
        before = rho * spread(faces.at[0], t, z)
        after = rho * spread(faces.at[1], t, z)
        d.append(1.0 + (before + after))
        e.append(jnp.where(lanes == 0, 0.0, before))
    for level in range(z.levels):
        stride = 1 << level
        half = 2 * stride == z.nx
        for t in tiles:
            r = 1.0 / d[t]
            above = along_x(e[t], -stride, z.nx)
            r_before = along_x(r, stride, z.nx)
            left = e[t] * r_before
            right = above * (r_before if half else along_x(r, -stride, z.nx))
            left_ref[level, t] = left + right if half else left
            if not half:
                right_ref[level, t] = right
            d[t] = d[t] - e[t] * left - above * right
            if not half:
                e[t] = left * along_x(e[t], stride, z.nx)
    for t in tiles:
        inverse_ref[t] = 1.0 / d[t]


def source_kernel(
    z, c_ref, frequency_ref, barrier_ref, proportions_ref, rates_ref, faces,
    tiles_ref, arrhenius_ref, base_ref, heat_ref,
):
    frequency, barrier = column(frequency_ref, z), column(barrier_ref, z)
    heat_ref[...] = 1.0 - 1.0 / z.warmth(c_ref)[...]
    for t in range(z.tiles):
        tiles_ref[t] = c_ref[pl.ds(t, z.species, stride=z.tiles), :]
        arrhenius_ref[t] = frequency * jnp.exp(barrier * spread(heat_ref, t, z))
    base_sides(z, tiles_ref, rates_ref, faces, arrhenius_ref, proportions_ref, base_ref)


def base_sides(z, tiles_ref, rates_ref, faces, arrhenius_ref, proportions_ref, base_ref):
    lanes = lax.broadcasted_iota(jnp.int32, z.tile, 1)
    rate = rates_ref[0]
    reacting = jnp.concatenate(
        [arrhenius_ref[t] * jnp.tanh(tiles_ref[t]) for t in range(z.tiles)], axis=1
    )
    source = jnp.dot(
        proportions_ref[...],
        reacting,
        precision=lax.Precision.HIGHEST,
        preferred_element_type=F32,
    )
    for t in range(z.tiles):
        v = tiles_ref[t]
        before = jnp.where(lanes == 0, 0.0, along_x(v, 1, z.nx))
        after = jnp.where(lanes == z.nx - 1, 0.0, along_x(v, -1, z.nx))
        lap = rate * (
            spread(faces.at[1], t, z) * (after - v) - spread(faces.at[0], t, z) * (v - before)
        )
        base_ref[t] = v + lap + source[:, t * z.nx : (t + 1) * z.nx]


def edge_places(z):
    return [(y, row) for y in range(z.ny) for row in sorted({0, z.nz - 1})]


def join_levels(z, t, left, right, joined, at):
    for pair in range(z.pairs):
        stride = 4**pair
        l1, r1, l2, r2 = (ref[2 * pair + n, t] for n in range(2) for ref in (left, right))
        factors = (
            l1 + l2 * along_x(r1, 2 * stride, z.nx),
            r1 + r2 * along_x(l1, -2 * stride, z.nx),
            l2 * along_x(l1, 2 * stride, z.nx),
            r2 * along_x(r1, -2 * stride, z.nx),
        )
        for n, factor in enumerate(factors):
            joined[4 * pair + n, at] = factor


def right_sides(
    z, places, tiles_ref, base_ref, z_halo, y_halo, rates_ref, y_faces, z_faces, left, right, inverse, f_ref,
    joined=None,
):
    rate_y, rate_z = rates_ref[1], rates_ref[2]
    section, lap = [], []
    for y, row in places:
        t = y * z.nz + row
        v = tiles_ref[t]
        z_before = tiles_ref[t - 1] if row else z_halo(0, y)
        z_after = tiles_ref[t + 1] if row < z.nz - 1 else z_halo(1, y)
        if isinstance(y, int):
            y_before = tiles_ref[t - z.nz] if y else y_halo(0, row)
            y_after = tiles_ref[t + z.nz] if y < z.ny - 1 else y_halo(1, row)
        else:
            y_before = jnp.where(y > 0, tiles_ref[jnp.maximum(y - 1, 0) * z.nz + row], y_halo(0, row))
            y_after = jnp.where(
                y < z.ny - 1, tiles_ref[jnp.minimum(y + 1, z.ny - 1) * z.nz + row], y_halo(1, row)
            )
        flux = [spread(faces.at[n], t, z) for faces in (y_faces, z_faces) for n in range(2)]
        lap_y = rate_y * (flux[1] * (y_after - v) - flux[0] * (v - y_before))
        lap_z = rate_z * (flux[3] * (z_after - v) - flux[2] * (v - z_before))
        lap.append(lap_z)
        section.append(base_ref[t] + lap_y + lap_z)
    pairs = z.pairs if joined else 0
    for pair in range(pairs):
        stride = 4**pair
        for i, (y, row) in enumerate(places):
            t = y * z.nz + row
            factors = [joined(4 * pair + n, i) for n in range(4)]
            factors[2:2] = left[2 * pair + 1, t], right[2 * pair + 1, t]
            terms = []
            for factor, by in zip(factors, (1, -1, 2, -2, 3, -3)):
                terms.append(factor * along_x(section[i], by * stride, z.nx))
            section[i] = section[i] + ((terms[0] + terms[1]) + (terms[2] + terms[3])) + (terms[4] + terms[5])
    for level in range(2 * pairs, z.levels):
        stride = 1 << level
        for i, (y, row) in enumerate(places):
            t = y * z.nz + row
            before = along_x(section[i], stride, z.nx)
            more = left[level, t] * before
            if 2 * stride < z.nx:
                more = more + right[level, t] * along_x(section[i], -stride, z.nx)
            section[i] = section[i] + more
    for i, (y, row) in enumerate(places):
        t = y * z.nz + row
        f_ref[t] = section[i] * inverse[t] - 0.5 * lap[i]


def y_halos(z, received):
    low, high = received[0], received[-1]
    low_mask, high_mask = inner("gy", z.gy)

    def halo(side, row):
        lines = per_line(z, row)
        return high[lines, :] * high_mask if side else low[lines, :] * low_mask

    return halo


def send_sums(z, f_ref, v_ref, u_ref, pay_ref):
    for y in range(z.ny):
        tiles = range(y * z.nz, (y + 1) * z.nz)
        pay_ref[0, per_line(z, y), :] = functools.reduce(jnp.add, [v_ref[t] * f_ref[t] for t in tiles])
        pay_ref[1, per_line(z, y), :] = functools.reduce(jnp.add, [u_ref[t] * f_ref[t] for t in tiles])


def total_kernel(z, pay_ref, *refs):
    inside = refs[: z.members - 1]
    within_ref, *out_refs = refs[z.members - 1 :]
    me = lax.axis_index("gz")
    group, member = me // z.members, me % z.members
    below = above = jnp.zeros((z.lines, z.nx), F32)
    rising, falling = pay_ref[0], pay_ref[1]
    for k, ref in zip(z.partners, inside):
        lower = (member ^ k) < member
        up, down = ref[0], ref[1]
        rising, falling = rising + up, falling + down
        below = below + jnp.where(lower, up, 0.0)
        above = above + jnp.where(lower, 0.0, down)
    within_ref[0] = below
    within_ref[1] = above
    for i, ref in enumerate(reversed(out_refs)):
        ref[...] = jnp.where((group ^ (i + 1)) > group, rising, falling)


def z_face_pair(z, k_ref, low, high):
    rows = lax.broadcasted_iota(jnp.int32, (z.nz, z.nx), 0)
    for y in range(z.ny):
        here = k_ref[y * z.nz : (y + 1) * z.nz, :]
        before, after = (jnp.broadcast_to(row, here.shape) for row in (low(y), high(y)))
        yield (
            here + jnp.where(rows == 0, before, pltpu.roll(here, 1, 0)),
            here + jnp.where(rows == z.nz - 1, after, pltpu.roll(here, z.nz - 1, 0)),
        )


def early_kernel(z, arguments, tiles_ref, base_ref, rates_ref, left_ref, right_ref, inverse_ref, *refs):
    halos = 1 if z.gy == 2 else 2
    received = refs[:halos]
    f_ref, y_faces, joined_ref, z_faces = refs[halos:]
    for i, (y, row) in enumerate(edge_places(z)):
        join_levels(z, y * z.nz + row, left_ref, right_ref, joined_ref, i)
    k_ref = z.conductance(arguments)
    k = k_ref[...]
    low, high = received[0], received[-1]
    low_mask, high_mask = inner("gy", z.gy)
    k_base = z.nz * z.species
    below = jnp.concatenate([low[k_base:, :] * low_mask, k[: z.tiles - z.nz]], axis=0)
    above = jnp.concatenate([k[z.nz :], high[k_base:, :] * high_mask], axis=0)
    y_faces[0] = 0.5 * (k + below)
    y_faces[1] = 0.5 * (k + above)
    nothing = jnp.zeros((1, z.nx), F32)
    for y, (before, after) in enumerate(z_face_pair(z, k_ref, lambda y: nothing, lambda y: nothing)):
        own = slice(y * z.nz, (y + 1) * z.nz)
        z_faces[0, own, :] = 0.5 * before
        z_faces[1, own, :] = 0.5 * after
    places = [(y, row) for y in range(z.ny) for row in range(1, z.nz - 1)]
    right_sides(
        z, places, tiles_ref, base_ref, None, y_halos(z, received), rates_ref, y_faces, z_faces,
        left_ref, right_ref, inverse_ref, f_ref,
    )


def first_kernel(
    z, arguments, far_ref, near_ref, tiles_ref, base_ref, rates_ref, left_ref, right_ref, inverse_ref,
    early_ref, y_faces, joined_ref, *refs
):
    halos = 1 if z.gy == 2 else 2
    received = refs[:halos]
    pay_ref, f_ref, z_faces, from_below, from_above = refs[halos:]
    k_ref = z.conductance(arguments)
    odd = lax.axis_index("gz") % 2 == 1
    from_below[...] = jnp.where(odd, near_ref[...], far_ref[...])
    from_above[...] = jnp.where(odd, far_ref[...], near_ref[...])
    z_low, z_high = inner("gz", z.devices)
    pay_ref[z.faces_at + z.tiles :, :] = jnp.zeros((z.block_rows - z.faces_at - z.tiles, z.nx), F32)

    def k_low(y):
        return from_below[z.lines + y : z.lines + y + 1, :] * z_low

    def k_high(y):
        return from_above[z.lines + y : z.lines + y + 1, :] * z_high

    for y, (before, after) in enumerate(z_face_pair(z, k_ref, k_low, k_high)):
        own = slice(y * z.nz, (y + 1) * z.nz)
        z_faces[0, own, :] = 0.5 * before
        z_faces[1, own, :] = 0.5 * after
        pay_ref[z.faces_at + y * z.nz : z.faces_at + (y + 1) * z.nz, :] = 1.0 / before
        top = z.faces_at + z.tiles + y
        pay_ref[top : top + 1, :] = 1.0 / after[z.nz - 1 :, :]

    def z_halo(side, y):
        lines = per_line(z, y)
        return from_above[lines, :] * z_high if side else from_below[lines, :] * z_low

    for y in range(z.ny):
        for row in range(1, z.nz - 1):
            f_ref[y * z.nz + row] = early_ref[y * z.nz + row]
    right_sides(
        z, edge_places(z), tiles_ref, base_ref, z_halo, y_halos(z, received), rates_ref, y_faces, z_faces,
        left_ref, right_ref, inverse_ref, f_ref, lambda n, i: joined_ref[n, i],
    )
    ohms = rates_ref[3]
    zero, one = jnp.zeros(z.tile, F32), jnp.ones(z.tile, F32)
    for y in range(z.ny):
        p, q, first, second = (one, zero), (zero, one), zero, zero
        for i in range(z.nz):
            ohm = ohms * spread(pay_ref, z.faces_at + y * z.nz + i, z)
            p, q = advance(p, ohm), advance(q, ohm)
            f = f_ref[y * z.nz + i]
            first = first + p[0] * f
            second = second + q[0] * f
        pay_ref[per_line(z, y), :] = first
        pay_ref[per_line(z, z.ny + y), :] = second


def advance(state, ohm):
    v, w = state
    v = v + w * ohm
    return v, w + v


def merge_kernel(z, rates_ref, pay_ref, *refs):
    *received, group_ref, order = refs
    me = lax.axis_index("gz") % z.members
    order[me] = pay_ref[...]
    for k, ref in zip(z.partners, received):
        order[me ^ k] = ref[...]
    ohms = rates_ref[3]
    zero, one = jnp.zeros(z.tile, F32), jnp.ones(z.tile, F32)
    for y in range(z.ny):
        p, q, first, second = (one, zero), (zero, one), zero, zero
        for j in range(z.members):
            s1, s2 = order[j, per_line(z, y), :], order[j, per_line(z, z.ny + y), :]
            first = first + (p[0] * s1 + p[1] * s2)
            second = second + (q[0] * s1 + q[1] * s2)
            if j < z.members - 1:
                for i in range(z.nz):
                    ohm = ohms * spread(order.at[j], z.faces_at + y * z.nz + i, z)
                    p, q = advance(p, ohm), advance(q, ohm)
        group_ref[per_line(z, y), :] = first
        group_ref[per_line(z, z.ny + y), :] = second
    for j in range(z.members):
        start = z.faces_at + j * z.tiles
        group_ref[start : start + z.tiles, :] = order[j, z.faces_at : z.faces_at + z.tiles, :]
    group_ref[z.group_top :, :] = order[z.members - 1, z.faces_at + z.tiles :, :]


def transfers(z, rates_ref, refs, blocks):
    ohms = rates_ref[3]
    zero, one = jnp.zeros(z.tile, F32), jnp.ones(z.tile, F32)

    def block(j, state):
        state = list(state)
        start = z.faces_at + j * z.tiles
        for i in range(z.nz):
            for n, ref in enumerate(refs):
                for y in range(z.ny):
                    ohm = ohms * spread(ref, start + y * z.nz + i, z)
                    at = 4 * (n * z.ny + y)
                    state[at : at + 2] = advance(state[at : at + 2], ohm)
                    state[at + 2 : at + 4] = advance(state[at + 2 : at + 4], ohm)
        return tuple(state)

    state = (one, zero, zero, one) * (z.ny * len(refs))
    if blocks <= 4:
        for j in range(blocks):
            state = block(j, state)
    else:
        state = lax.fori_loop(0, blocks, block, state)
    return [state[4 * z.ny * n : 4 * z.ny * (n + 1)] for n in range(len(refs))]


def inside_kernel(z, rates_ref, *refs):
    *blocks, sums_ref, transfers_ref = refs
    me = lax.axis_index("gz") % z.members
    for k, ref, matrix in zip((0, *z.partners), blocks, transfers(z, rates_ref, blocks, 1)):
        sums_ref[me ^ k] = ref[: 2 * z.lines, :]
        for n, value in enumerate(matrix):
            transfers_ref[me ^ k, n] = value


def far_kernel(z, rates_ref, group_ref, out_ref):
    (matrix,) = transfers(z, rates_ref, [group_ref], z.members)
    for n, value in enumerate(matrix):
        out_ref[n] = value


def both_ways(z, rates_ref, own_ref, blocks, groups, top_ref, v_ref, u_ref, ends_ref, sums_ref):
    me = lax.axis_index("gz")
    group, member = me // z.members, me % z.members
    ohms = rates_ref[3]
    zero, one = jnp.zeros(z.tile, F32), jnp.ones(z.tile, F32)
    ys = range(z.ny)

    def ohm(ref, row):
        return ohms * spread(ref, row, z)

    def totals(sums, j, y):
        return sums[j, per_line(z, y), :], sums[j, per_line(z, z.ny + y), :]

    def up(refs, j, state):
        sums, matrices = refs
        out = []
        for y in ys:
            v, w, total = state[3 * y : 3 * y + 3]
            s1, s2 = totals(sums, j, y)
            pv, pw, qv, qw = (matrices[j, 4 * y + n] for n in range(4))
            out += [pv * v + qv * w, pw * v + qw * w, total + (v * s1 + w * s2)]
        return tuple(out)

    def down(refs, j, state):
        sums, matrices = refs
        out = []
        for y in ys:
            u, w, total = state[3 * y : 3 * y + 3]
            s1, s2 = totals(sums, j, y)
            pv, pw, qv, qw = (matrices[j, 4 * y + n] for n in range(4))
            u, w = qw * u + qv * w, pw * u + pv * w
            out += [u, w, total + (u * s1 - w * s2)]
        return tuple(out)

    state = (zero, one, zero) * z.ny
    state = lax.fori_loop(0, group, lambda j, s: up(groups, j, s), state)
    state = lax.fori_loop(0, member, lambda j, s: up(blocks, j, s), state)
    rising = []
    for y in ys:
        pair = state[3 * y : 3 * y + 2]
        sums_ref[y] = state[3 * y + 2]
        ends_ref[y] = pair[0]
        for i in range(z.nz):
            pair = advance(pair, ohm(own_ref, z.faces_at + y * z.nz + i))
            v_ref[y * z.nz + i] = pair[0]
            if i == 0:
                rising.append(pair)
        ends_ref[z.ny + y] = pair[0] + pair[1] * ohm(own_ref, z.faces_at + z.tiles + y)

    state = ()
    for y in ys:
        state += (ohm(top_ref, y), one, zero)
    last = z.groups_z - 1
    state = lax.fori_loop(0, last - group, lambda i, s: down(groups, last - i, s), state)
    last = z.members - 1
    state = lax.fori_loop(0, last - member, lambda i, s: down(blocks, last - i, s), state)
    for y in ys:
        u, w, total = state[3 * y : 3 * y + 3]
        sums_ref[z.ny + y] = total
        ends_ref[3 * z.ny + y] = u - w * ohm(own_ref, z.faces_at + z.tiles + y)
        for i in reversed(range(z.nz)):
            u_ref[y * z.nz + i] = u
            if i == 0:
                v, wv = rising[y]
                ends_ref[4 * z.ny + y] = 1.0 / (wv * u + v * w)
            w = w + u
            u = u + w * ohm(own_ref, z.faces_at + y * z.nz + i)
        ends_ref[2 * z.ny + y] = u


def solve_row(z, y, sums, f_ref, v_ref, u_ref, ends_ref, store):
    below, above = sums
    scale = ends_ref[4 * z.ny + y]
    after = [None] * z.nz
    total = above
    for i in reversed(range(z.nz)):
        t = y * z.nz + i
        after[i] = total
        total = total + u_ref[t] * f_ref[t]
    low = scale * (ends_ref[2 * z.ny + y] * below + ends_ref[y] * total)
    total = below
    for i in range(z.nz):
        t = y * z.nz + i
        total = total + v_ref[t] * f_ref[t]
        store(i, scale * (u_ref[t] * total + v_ref[t] * after[i]))
    high = scale * (ends_ref[3 * z.ny + y] * total + ends_ref[z.ny + y] * above)
    return low, high


def meet_kernel(z, rates_ref, f_ref, pay_ref, own_group, block_sums, block_transfers, far_transfer, *refs):
    across, refs = refs[: z.groups_z - 1], refs[z.groups_z - 1 :]
    v_ref, u_ref, ends_ref, sums_ref, *y_refs, group_sums, group_transfers, tops = refs
    group = lax.axis_index("gz") // z.members
    near = transfers(z, rates_ref, across[:-1], z.members)
    for i, ref in enumerate((own_group, *across)):
        group_sums[group ^ i] = ref[: 2 * z.lines, :]
        tops[group ^ i] = ref[z.group_top :, :]
    for i, matrix in enumerate(near):
        for n, value in enumerate(matrix):
            group_transfers[group ^ (i + 1), n] = value
    group_transfers[group ^ len(across)] = far_transfer[...]
    both_ways(
        z, rates_ref, pay_ref, (block_sums, block_transfers), (group_sums, group_transfers),
        tops.at[z.groups_z - 1], v_ref, u_ref, ends_ref, sums_ref,
    )
    for ref, y in zip(y_refs, y_picks(z)):

        def store(i, value):
            ref[i * z.species : (i + 1) * z.species, :] = value

        solve_row(z, y, (sums_ref[y], sums_ref[z.ny + y]), f_ref, v_ref, u_ref, ends_ref, store)


def rows_kernel(z, f_ref, v_ref, u_ref, ends_ref, sums_ref, tiles_ref, halo_ref):
    for y in range(z.ny):

        def store(i, value):
            tiles_ref[y * z.nz + i] = value

        low, high = solve_row(
            z, y, (sums_ref[y], sums_ref[z.ny + y]), f_ref, v_ref, u_ref, ends_ref, store
        )
        halo_ref[y] = low
        halo_ref[z.ny + y] = high


def halo_rows(z):
    if z.gy == 2:
        core = lax.axis_index("gy")
        return y_picks(z), [core + j for j in range(z.ny - 1)]
    return list(range(z.ny)), []


def places_of(z, ys):
    return [(y, row) for y in ys for row in range(z.nz)]


def inner_kernel(
    z, tiles_ref, halo_ref, rates_ref, x_faces, arrhenius_ref, proportions_ref, y_faces, z_faces,
    left_ref, right_ref, inverse_ref, base_ref, f_ref, joined_ref
):
    ys, _ = halo_rows(z)
    for i, (y, row) in enumerate(places_of(z, ys)):
        join_levels(z, y * z.nz + row, left_ref, right_ref, joined_ref, i)
    base_sides(z, tiles_ref, rates_ref, x_faces, arrhenius_ref, proportions_ref, base_ref)
    _, ys = halo_rows(z)
    zero = jnp.zeros(z.tile, F32)
    if ys:
        right_sides(
            z, places_of(z, ys), tiles_ref, base_ref, lambda side, y: halo_ref[side * z.ny + y],
            lambda side, row: zero, rates_ref, y_faces, z_faces, left_ref, right_ref, inverse_ref, f_ref,
        )


def second_kernel(
    z, tiles_ref, halo_ref, rates_ref, y_faces, z_faces, left_ref, right_ref, inverse_ref, base_ref,
    inner_ref, joined_ref, v_ref, u_ref, *refs
):
    halos = 1 if z.gy == 2 else 2
    received = refs[:halos]
    pay_ref, f_ref = refs[halos:]
    ys, done = halo_rows(z)
    for y, row in places_of(z, done):
        f_ref[y * z.nz + row] = inner_ref[y * z.nz + row]
    right_sides(
        z, places_of(z, ys), tiles_ref, base_ref, lambda side, y: halo_ref[side * z.ny + y],
        y_halos(z, received), rates_ref, y_faces, z_faces, left_ref, right_ref, inverse_ref, f_ref,
        lambda n, i: joined_ref[n, i],
    )
    send_sums(z, f_ref, v_ref, u_ref, pay_ref)


def last_kernel(z, within_ref, f_ref, v_ref, u_ref, ends_ref, *refs):
    *across, out_hbm, rows_ref, sems = refs
    group = lax.axis_index("gz") // z.members
    below, above = within_ref[0], within_ref[1]
    for i, ref in enumerate(reversed(across)):
        lower = (group ^ (i + 1)) < group
        value = ref[...]
        below = below + jnp.where(lower, value, 0.0)
        above = above + jnp.where(lower, 0.0, value)
    blocks = rows_ref.reshape(z.species, z.ny, z.nz, z.nx)
    copies = []
    for y in range(z.ny):

        def store(i, value):
            rows_ref[pl.ds(y * z.nz + i, z.species, stride=z.tiles), :] = value

        sums = below[per_line(z, y)], above[per_line(z, y)]
        solve_row(z, y, sums, f_ref, v_ref, u_ref, ends_ref, store)
        copies.append(pltpu.make_async_copy(blocks.at[:, y], out_hbm.at[:, y], sems.at[y]))
        copies[-1].start()
    for copy in copies:
        copy.wait()


def per_device(z, c, k, warm, sigma, frequency, barrier, proportions):
    in_vmem = pl.BlockSpec(memory_space=pltpu.VMEM)
    hbm = pl.BlockSpec(memory_space=pltpu.HBM)

    def shaped(*shape):
        return jax.ShapeDtypeStruct(shape, F32)

    def call(kernel, outs, ins, scratch=(), spec=in_vmem, out_spec=in_vmem, us=0.5):
        return pl.pallas_call(
            functools.partial(kernel, z),
            out_shape=outs,
            in_specs=[spec] * len(ins),
            out_specs=jax.tree.map(lambda _: out_spec, outs),
            scratch_shapes=list(scratch),
            compiler_params=pltpu.CompilerParams(vmem_limit_bytes=48 * 2**20),
            cost_estimate=pl.CostEstimate(
                flops=0, bytes_accessed=int(us * 3.69e6), transcendentals=0
            ),
        )(*ins)

    def shift(value, axis, by):
        count = lax.axis_size(axis)
        return lax.ppermute(value, axis, [(i, (i + by) % count) for i in range(count)])

    def swap(sends):
        return [shift(value, "gy", by) for value, by in zip(sends, (1, -1))]

    arguments = jnp.concatenate([v.reshape(-1, z.nx) for v in (c, k, warm)])
    halos = 1 if z.gy == 2 else 2
    block = shaped(z.tiles, *z.tile)
    ends_shape = shaped(5 * z.ny, *z.tile)

    def exchange(value, count, unit):
        values = value if isinstance(value, list) else [value] * (count - 1)
        pairs = [[(i, i ^ (k * unit)) for i in range(z.devices)] for k in range(1, count)]
        if isinstance(value, list):
            return [lax.ppermute(v, "gz", p) for v, p in zip(values[::-1], pairs[::-1])][::-1]
        return [lax.ppermute(v, "gz", p) for v, p in zip(values, pairs)]

    def exchange_inside(value):
        received = exchange(value, z.members, 1)
        return [received[k - 1] for k in z.partners]

    def neighbours(near, far):
        last = z.devices - 1
        links = [(i, i + 1) for i in range(1, last, 2)]
        links = [pair for i, j in links for pair in ((i, j), (j, i))]
        ends = [(i, i) for i in (0, last)]
        far_pairs = [(i * z.gy + n, j * z.gy + n) for i, j in links for n in range(z.gy)]
        far_pairs += [(i * z.gy + n, j * z.gy + (n ^ 1)) for i, j in ends for n in range(z.gy)]
        far = lax.ppermute(far, ("gz", "gy"), far_pairs)
        return exchange(near, 2, 1)[0], far

    far, near, *sends = call(
        edges_kernel,
        [shaped(z.edge_rows, z.nx)] * 2 + [shaped(z.nz * (z.species + 1), z.nx)] * halos,
        [arguments],
    )
    near, far = neighbours(near, far)
    received = swap(sends)
    levels = shaped(z.levels, z.tiles, *z.tile)
    faces = shaped(2, z.tiles, z.nx)
    rates, x_faces, left, right, inverse = call(
        coefficients_kernel,
        [shaped(4, *z.tile), faces, levels, levels, block],
        [arguments, sigma.reshape(1, -1)],
        us=1.0,
    )
    vectors = [shift(v, "gy", 1).reshape(1, -1) for v in (frequency, barrier)]
    tiles, arrhenius, base = call(
        source_kernel,
        [block] * 3,
        [arguments, *vectors, proportions, rates, x_faces],
        [pltpu.VMEM((z.tiles, z.nx), F32)],
    )
    x_solve = [left, right, inverse]
    early, y_faces, edge_joined = call(
        early_kernel,
        [block, faces, shaped(4 * z.pairs, len(edge_places(z)), *z.tile)],
        [arguments, tiles, base, rates, *x_solve, *received],
        [pltpu.VMEM((2, z.tiles, z.nx), F32)],
    )
    pay, f, z_faces = call(
        first_kernel,
        [shaped(z.block_rows, z.nx), block, faces],
        [arguments, far, near, tiles, base, rates, *x_solve, early, y_faces, edge_joined, *received],
        [pltpu.VMEM((z.edge_rows, z.nx), F32)] * 2,
    )
    inside = exchange_inside(pay)
    group = call(
        merge_kernel,
        shaped(z.group_rows, z.nx),
        [rates, pay, *inside],
        [pltpu.VMEM((z.members, z.block_rows, z.nx), F32)],
    )
    across = exchange(group, z.groups_z, z.members)
    matrices = shaped(4 * z.ny, *z.tile)
    block_sums, block_transfers = call(
        inside_kernel,
        [shaped(z.members, 2 * z.lines, z.nx), shaped(z.members, *matrices.shape)],
        [rates, pay, *inside],
    )
    far_transfer = call(far_kernel, matrices, [rates, across[-1]])
    v, u, ends, sums, *sends = call(
        meet_kernel,
        [block, block, ends_shape, shaped(2 * z.ny, *z.tile)]
        + [shaped(z.nz * z.species, z.nx)] * halos,
        [rates, f, pay, group, block_sums, block_transfers, far_transfer, *across],
        [
            pltpu.VMEM((z.groups_z, 2 * z.lines, z.nx), F32),
            pltpu.VMEM((z.groups_z, *matrices.shape), F32),
            pltpu.VMEM((z.groups_z, z.group_rows - z.group_top, z.nx), F32),
        ],
    )

    received = swap(sends)
    tiles, halo = call(rows_kernel, [block, shaped(2 * z.ny, *z.tile)], [f, v, u, ends, sums])
    rows_with_halo = 1 if z.gy == 2 else z.ny
    base, f, joined = call(
        inner_kernel,
        [block, block, shaped(4 * z.pairs, rows_with_halo * z.nz, *z.tile)],
        [tiles, halo, rates, x_faces, arrhenius, proportions, y_faces, z_faces, *x_solve],
    )
    pay, f = call(
        second_kernel,
        [shaped(2, z.lines, z.nx), block],
        [tiles, halo, rates, y_faces, z_faces, *x_solve, base, f, joined, v, u, *received],
    )
    inside = exchange_inside(pay)
    within, *totals = call(
        total_kernel,
        [shaped(2, z.lines, z.nx)] + [shaped(z.lines, z.nx)] * (z.groups_z - 1),
        [pay, *inside],
    )
    across = exchange(totals[::-1], z.groups_z, z.members)
    return call(
        last_kernel,
        shaped(z.species, z.ny, z.nz, z.nx),
        [within, f, v, u, ends, *across[::-1]],
        [pltpu.VMEM((z.species * z.tiles, z.nx), F32), pltpu.SemaphoreType.DMA((z.ny,))],
        out_spec=hbm,
    )


def solution(mesh):
    def device_program(starting_densities, *others):
        sizes = Sizes(mesh, starting_densities.shape)
        return per_device(sizes, starting_densities, *others)

    return jax.shard_map(
        device_program,
        mesh=mesh,
        in_specs=(
            P(None, "gy", "gz", None),
            P("gy", "gz", None),
            P("gy", "gz", None),
            P(),
            P(),
            P(),
            P(),
        ),
        out_specs=P(None, "gy", "gz", None),
        check_vma=False,
    )
```

```python
import functools

import jax
import jax.numpy as jnp
from jax import lax
from jax.experimental import pallas as pl
from jax.experimental.pallas import tpu as pltpu
from jax.sharding import PartitionSpec as P

F32 = jnp.float32


class Sizes:
    def __init__(self, mesh, block):
        self.species, self.ny, self.nz, self.nx = block
        self.tiles = self.ny * self.nz
        self.lines = self.ny * self.species
        self.devices = mesh.shape["gz"]
        self.gy = mesh.shape["gy"]
        self.levels = (self.nx - 1).bit_length()
        self.pairs = (self.levels - 1) // 2
        self.tile = (self.species, self.nx)
        padded = -(-self.ny // 8) * 8
        self.edge_rows = self.lines + padded
        self.members = 1 << (self.devices.bit_length() // 2)
        self.groups_z = self.devices // self.members
        self.partners = (1, 3, 2) if self.members == 4 else tuple(range(1, self.members))
        self.faces_at = 2 * self.lines
        self.block_rows = self.faces_at + self.tiles + padded
        self.group_top = self.faces_at + self.members * self.tiles
        self.group_rows = self.group_top + padded

    def conductance(self, arguments):
        start = self.species * self.tiles
        return arguments.at[start : start + self.tiles]

    def warmth(self, arguments):
        start = (self.species + 1) * self.tiles
        return arguments.at[start : start + self.tiles]

    def groups(self, size):
        for base in range(0, self.tiles, size):
            yield range(base, min(base + size, self.tiles))


def column(ref, z):
    square = (z.species, z.species)
    mine = lax.broadcasted_iota(jnp.int32, square, 0) == lax.broadcasted_iota(jnp.int32, square, 1)
    values = jnp.where(mine, jnp.broadcast_to(ref[...], square), 0.0)
    return jnp.broadcast_to(jnp.sum(values, axis=1, keepdims=True), z.tile)


def spread(ref, row, z):
    return jnp.broadcast_to(ref[pl.ds(row, 1), :], z.tile)


def per_line(z, y):
    return slice(y * z.species, (y + 1) * z.species)


def along_x(v, by, nx):
    return pltpu.roll(v, by % nx, v.ndim - 1)


def flag(condition):
    return jnp.where(condition, 1.0, 0.0).astype(F32)


def inner(axis, count):
    me = lax.axis_index(axis)
    return flag(me > 0), flag(me < count - 1)


def edges_kernel(z, c_ref, far_ref, near_ref, *y_refs):
    k_ref = z.conductance(c_ref)
    odd = lax.axis_index("gz") % 2
    for ref, row in ((near_ref, (1 - odd) * (z.nz - 1)), (far_ref, odd * (z.nz - 1))):
        for y in range(z.ny):
            at = y * z.nz + row
            ref[per_line(z, y), :] = c_ref[pl.ds(at, z.species, stride=z.tiles), :]
            ref[z.lines + y : z.lines + y + 1, :] = k_ref[pl.ds(at, 1), :]
        ref[z.lines + z.ny :, :] = jnp.zeros((z.edge_rows - z.lines - z.ny, z.nx), F32)
    for ref, y in zip(y_refs, y_picks(z)):
        for i in range(z.nz):
            ref[i * z.species : (i + 1) * z.species, :] = c_ref[
                pl.ds(y * z.nz + i, z.species, stride=z.tiles), :
            ]
        start = y * z.nz if isinstance(y, int) else pl.multiple_of(y * z.nz, z.nz)
        ref[z.nz * z.species :, :] = k_ref[pl.ds(start, z.nz), :]


def y_picks(z):
    if z.gy == 2:
        return [jnp.where(lax.axis_index("gy") == 1, 0, z.ny - 1)]
    return [z.ny - 1, 0]


def coefficients_kernel(z, arguments, sigma_ref, rates_ref, faces, left_ref, right_ref, inverse_ref):
    sigma = column(sigma_ref, z)
    rho = 4.0 * sigma
    rates_ref[0] = rho
    rates_ref[1] = 0.015 * sigma
    rates_ref[2] = 4096.0 * sigma
    rates_ref[3] = 1.0 / (1024.0 * sigma)
    k = z.conductance(arguments)[...]
    lanes = lax.broadcasted_iota(jnp.int32, k.shape, 1)
    faces[0] = 0.5 * (k + jnp.where(lanes == 0, 0.0, along_x(k, 1, z.nx)))
    faces[1] = 0.5 * (k + jnp.where(lanes == z.nx - 1, 0.0, along_x(k, -1, z.nx)))
    lanes = lax.broadcasted_iota(jnp.int32, z.tile, 1)
    tiles = range(z.tiles)
    e, d = [], []
    for t in tiles:
        before = rho * spread(faces.at[0], t, z)
        after = rho * spread(faces.at[1], t, z)
        d.append(1.0 + (before + after))
        e.append(jnp.where(lanes == 0, 0.0, before))
    for level in range(z.levels):
        stride = 1 << level
        half = 2 * stride == z.nx
        for t in tiles:
            r = 1.0 / d[t]
            above = along_x(e[t], -stride, z.nx)
            r_before = along_x(r, stride, z.nx)
            left = e[t] * r_before
            right = above * (r_before if half else along_x(r, -stride, z.nx))
            left_ref[level, t] = left + right if half else left
            if not half:
                right_ref[level, t] = right
            d[t] = d[t] - e[t] * left - above * right
            if not half:
                e[t] = left * along_x(e[t], stride, z.nx)
    for t in tiles:
        inverse_ref[t] = 1.0 / d[t]


def source_kernel(
    z, c_ref, frequency_ref, barrier_ref, proportions_ref, rates_ref, faces,
    tiles_ref, arrhenius_ref, base_ref, heat_ref,
):
    frequency, barrier = column(frequency_ref, z), column(barrier_ref, z)
    heat_ref[...] = 1.0 - 1.0 / z.warmth(c_ref)[...]
    for t in range(z.tiles):
        tiles_ref[t] = c_ref[pl.ds(t, z.species, stride=z.tiles), :]
        arrhenius_ref[t] = frequency * jnp.exp(barrier * spread(heat_ref, t, z))
    base_sides(z, tiles_ref, rates_ref, faces, arrhenius_ref, proportions_ref, base_ref)


def base_sides(z, tiles_ref, rates_ref, faces, arrhenius_ref, proportions_ref, base_ref):
    lanes = lax.broadcasted_iota(jnp.int32, z.tile, 1)
    rate = rates_ref[0]
    reacting = jnp.concatenate(
        [arrhenius_ref[t] * jnp.tanh(tiles_ref[t]) for t in range(z.tiles)], axis=1
    )
    source = jnp.dot(
        proportions_ref[...],
        reacting,
        precision=lax.Precision.HIGHEST,
        preferred_element_type=F32,
    )
    for t in range(z.tiles):
        v = tiles_ref[t]
        before = jnp.where(lanes == 0, 0.0, along_x(v, 1, z.nx))
        after = jnp.where(lanes == z.nx - 1, 0.0, along_x(v, -1, z.nx))
        lap = rate * (
            spread(faces.at[1], t, z) * (after - v) - spread(faces.at[0], t, z) * (v - before)
        )
        base_ref[t] = v + lap + source[:, t * z.nx : (t + 1) * z.nx]


def edge_places(z):
    return [(y, row) for y in range(z.ny) for row in sorted({0, z.nz - 1})]


def join_levels(z, t, left, right, joined, at):
    for pair in range(z.pairs):
        stride = 4**pair
        l1, r1, l2, r2 = (ref[2 * pair + n, t] for n in range(2) for ref in (left, right))
        factors = (
            l1 + l2 * along_x(r1, 2 * stride, z.nx),
            r1 + r2 * along_x(l1, -2 * stride, z.nx),
            l2 * along_x(l1, 2 * stride, z.nx),
            r2 * along_x(r1, -2 * stride, z.nx),
        )
        for n, factor in enumerate(factors):
            joined[4 * pair + n, at] = factor


def right_sides(
    z, places, tiles_ref, base_ref, z_halo, y_halo, rates_ref, y_faces, z_faces, left, right, inverse, f_ref,
    joined=None,
):
    rate_y, rate_z = rates_ref[1], rates_ref[2]
    section, lap = [], []
    for y, row in places:
        t = y * z.nz + row
        v = tiles_ref[t]
        z_before = tiles_ref[t - 1] if row else z_halo(0, y)
        z_after = tiles_ref[t + 1] if row < z.nz - 1 else z_halo(1, y)
        if isinstance(y, int):
            y_before = tiles_ref[t - z.nz] if y else y_halo(0, row)
            y_after = tiles_ref[t + z.nz] if y < z.ny - 1 else y_halo(1, row)
        else:
            y_before = jnp.where(y > 0, tiles_ref[jnp.maximum(y - 1, 0) * z.nz + row], y_halo(0, row))
            y_after = jnp.where(
                y < z.ny - 1, tiles_ref[jnp.minimum(y + 1, z.ny - 1) * z.nz + row], y_halo(1, row)
            )
        flux = [spread(faces.at[n], t, z) for faces in (y_faces, z_faces) for n in range(2)]
        lap_y = rate_y * (flux[1] * (y_after - v) - flux[0] * (v - y_before))
        lap_z = rate_z * (flux[3] * (z_after - v) - flux[2] * (v - z_before))
        lap.append(lap_z)
        section.append(base_ref[t] + lap_y + lap_z)
    pairs = z.pairs if joined else 0
    for pair in range(pairs):
        stride = 4**pair
        for i, (y, row) in enumerate(places):
            t = y * z.nz + row
            factors = [joined(4 * pair + n, i) for n in range(4)]
            factors[2:2] = left[2 * pair + 1, t], right[2 * pair + 1, t]
            terms = []
            for factor, by in zip(factors, (1, -1, 2, -2, 3, -3)):
                terms.append(factor * along_x(section[i], by * stride, z.nx))
            section[i] = section[i] + ((terms[0] + terms[1]) + (terms[2] + terms[3])) + (terms[4] + terms[5])
    for level in range(2 * pairs, z.levels):
        stride = 1 << level
        for i, (y, row) in enumerate(places):
            t = y * z.nz + row
            before = along_x(section[i], stride, z.nx)
            more = left[level, t] * before
            if 2 * stride < z.nx:
                more = more + right[level, t] * along_x(section[i], -stride, z.nx)
            section[i] = section[i] + more
    for i, (y, row) in enumerate(places):
        t = y * z.nz + row
        f_ref[t] = section[i] * inverse[t] - 0.5 * lap[i]


def y_halos(z, received):
    low, high = received[0], received[-1]
    low_mask, high_mask = inner("gy", z.gy)

    def halo(side, row):
        lines = per_line(z, row)
        return high[lines, :] * high_mask if side else low[lines, :] * low_mask

    return halo


def send_sums(z, f_ref, v_ref, u_ref, pay_ref):
    for y in range(z.ny):
        tiles = range(y * z.nz, (y + 1) * z.nz)
        pay_ref[0, per_line(z, y), :] = functools.reduce(jnp.add, [v_ref[t] * f_ref[t] for t in tiles])
        pay_ref[1, per_line(z, y), :] = functools.reduce(jnp.add, [u_ref[t] * f_ref[t] for t in tiles])


def total_kernel(z, pay_ref, *refs):
    inside = refs[: z.members - 1]
    within_ref, *out_refs = refs[z.members - 1 :]
    me = lax.axis_index("gz")
    group, member = me // z.members, me % z.members
    below = above = jnp.zeros((z.lines, z.nx), F32)
    rising, falling = pay_ref[0], pay_ref[1]
    for k, ref in zip(z.partners, inside):
        lower = (member ^ k) < member
        up, down = ref[0], ref[1]
        rising, falling = rising + up, falling + down
        below = below + jnp.where(lower, up, 0.0)
        above = above + jnp.where(lower, 0.0, down)
    within_ref[0] = below
    within_ref[1] = above
    for i, ref in enumerate(reversed(out_refs)):
        ref[...] = jnp.where((group ^ (i + 1)) > group, rising, falling)


def z_face_pair(z, k_ref, low, high):
    rows = lax.broadcasted_iota(jnp.int32, (z.nz, z.nx), 0)
    for y in range(z.ny):
        here = k_ref[y * z.nz : (y + 1) * z.nz, :]
        before, after = (jnp.broadcast_to(row, here.shape) for row in (low(y), high(y)))
        yield (
            here + jnp.where(rows == 0, before, pltpu.roll(here, 1, 0)),
            here + jnp.where(rows == z.nz - 1, after, pltpu.roll(here, z.nz - 1, 0)),
        )


def early_kernel(z, arguments, tiles_ref, base_ref, rates_ref, left_ref, right_ref, inverse_ref, *refs):
    halos = 1 if z.gy == 2 else 2
    received = refs[:halos]
    f_ref, y_faces, joined_ref, z_faces = refs[halos:]
    for i, (y, row) in enumerate(edge_places(z)):
        join_levels(z, y * z.nz + row, left_ref, right_ref, joined_ref, i)
    k_ref = z.conductance(arguments)
    k = k_ref[...]
    low, high = received[0], received[-1]
    low_mask, high_mask = inner("gy", z.gy)
    k_base = z.nz * z.species
    below = jnp.concatenate([low[k_base:, :] * low_mask, k[: z.tiles - z.nz]], axis=0)
    above = jnp.concatenate([k[z.nz :], high[k_base:, :] * high_mask], axis=0)
    y_faces[0] = 0.5 * (k + below)
    y_faces[1] = 0.5 * (k + above)
    nothing = jnp.zeros((1, z.nx), F32)
    for y, (before, after) in enumerate(z_face_pair(z, k_ref, lambda y: nothing, lambda y: nothing)):
        own = slice(y * z.nz, (y + 1) * z.nz)
        z_faces[0, own, :] = 0.5 * before
        z_faces[1, own, :] = 0.5 * after
    places = [(y, row) for y in range(z.ny) for row in range(1, z.nz - 1)]
    right_sides(
        z, places, tiles_ref, base_ref, None, y_halos(z, received), rates_ref, y_faces, z_faces,
        left_ref, right_ref, inverse_ref, f_ref,
    )


def first_kernel(
    z, arguments, far_ref, near_ref, tiles_ref, base_ref, rates_ref, left_ref, right_ref, inverse_ref,
    early_ref, y_faces, joined_ref, *refs
):
    halos = 1 if z.gy == 2 else 2
    received = refs[:halos]
    pay_ref, f_ref, z_faces, from_below, from_above = refs[halos:]
    k_ref = z.conductance(arguments)
    odd = lax.axis_index("gz") % 2 == 1
    from_below[...] = jnp.where(odd, near_ref[...], far_ref[...])
    from_above[...] = jnp.where(odd, far_ref[...], near_ref[...])
    z_low, z_high = inner("gz", z.devices)
    pay_ref[z.faces_at + z.tiles :, :] = jnp.zeros((z.block_rows - z.faces_at - z.tiles, z.nx), F32)

    def k_low(y):
        return from_below[z.lines + y : z.lines + y + 1, :] * z_low

    def k_high(y):
        return from_above[z.lines + y : z.lines + y + 1, :] * z_high

    for y, (before, after) in enumerate(z_face_pair(z, k_ref, k_low, k_high)):
        own = slice(y * z.nz, (y + 1) * z.nz)
        z_faces[0, own, :] = 0.5 * before
        z_faces[1, own, :] = 0.5 * after
        pay_ref[z.faces_at + y * z.nz : z.faces_at + (y + 1) * z.nz, :] = 1.0 / before
        top = z.faces_at + z.tiles + y
        pay_ref[top : top + 1, :] = 1.0 / after[z.nz - 1 :, :]

    def z_halo(side, y):
        lines = per_line(z, y)
        return from_above[lines, :] * z_high if side else from_below[lines, :] * z_low

    for y in range(z.ny):
        for row in range(1, z.nz - 1):
            f_ref[y * z.nz + row] = early_ref[y * z.nz + row]
    right_sides(
        z, edge_places(z), tiles_ref, base_ref, z_halo, y_halos(z, received), rates_ref, y_faces, z_faces,
        left_ref, right_ref, inverse_ref, f_ref, lambda n, i: joined_ref[n, i],
    )
    ohms = rates_ref[3]
    zero, one = jnp.zeros(z.tile, F32), jnp.ones(z.tile, F32)
    for y in range(z.ny):
        p, q, first, second = (one, zero), (zero, one), zero, zero
        for i in range(z.nz):
            ohm = ohms * spread(pay_ref, z.faces_at + y * z.nz + i, z)
            p, q = advance(p, ohm), advance(q, ohm)
            f = f_ref[y * z.nz + i]
            first = first + p[0] * f
            second = second + q[0] * f
        pay_ref[per_line(z, y), :] = first
        pay_ref[per_line(z, z.ny + y), :] = second


def advance(state, ohm):
    v, w = state
    v = v + w * ohm
    return v, w + v


def merge_kernel(z, rates_ref, pay_ref, *refs):
    *received, group_ref, order = refs
    me = lax.axis_index("gz") % z.members
    order[me] = pay_ref[...]
    for k, ref in zip(z.partners, received):
        order[me ^ k] = ref[...]
    ohms = rates_ref[3]
    zero, one = jnp.zeros(z.tile, F32), jnp.ones(z.tile, F32)
    for y in range(z.ny):
        p, q, first, second = (one, zero), (zero, one), zero, zero
        for j in range(z.members):
            s1, s2 = order[j, per_line(z, y), :], order[j, per_line(z, z.ny + y), :]
            first = first + (p[0] * s1 + p[1] * s2)
            second = second + (q[0] * s1 + q[1] * s2)
            if j < z.members - 1:
                for i in range(z.nz):
                    ohm = ohms * spread(order.at[j], z.faces_at + y * z.nz + i, z)
                    p, q = advance(p, ohm), advance(q, ohm)
        group_ref[per_line(z, y), :] = first
        group_ref[per_line(z, z.ny + y), :] = second
    for j in range(z.members):
        start = z.faces_at + j * z.tiles
        group_ref[start : start + z.tiles, :] = order[j, z.faces_at : z.faces_at + z.tiles, :]
    group_ref[z.group_top :, :] = order[z.members - 1, z.faces_at + z.tiles :, :]


def transfers(z, rates_ref, refs, blocks):
    ohms = rates_ref[3]
    zero, one = jnp.zeros(z.tile, F32), jnp.ones(z.tile, F32)

    def block(j, state):
        state = list(state)
        start = z.faces_at + j * z.tiles
        for i in range(z.nz):
            for n, ref in enumerate(refs):
                for y in range(z.ny):
                    ohm = ohms * spread(ref, start + y * z.nz + i, z)
                    at = 4 * (n * z.ny + y)
                    state[at : at + 2] = advance(state[at : at + 2], ohm)
                    state[at + 2 : at + 4] = advance(state[at + 2 : at + 4], ohm)
        return tuple(state)

    state = (one, zero, zero, one) * (z.ny * len(refs))
    if blocks <= 4:
        for j in range(blocks):
            state = block(j, state)
    else:
        state = lax.fori_loop(0, blocks, block, state)
    return [state[4 * z.ny * n : 4 * z.ny * (n + 1)] for n in range(len(refs))]


def inside_kernel(z, rates_ref, *refs):
    *blocks, sums_ref, transfers_ref = refs
    me = lax.axis_index("gz") % z.members
    for k, ref, matrix in zip((0, *z.partners), blocks, transfers(z, rates_ref, blocks, 1)):
        sums_ref[me ^ k] = ref[: 2 * z.lines, :]
        for n, value in enumerate(matrix):
            transfers_ref[me ^ k, n] = value


def far_kernel(z, rates_ref, group_ref, out_ref):
    (matrix,) = transfers(z, rates_ref, [group_ref], z.members)
    for n, value in enumerate(matrix):
        out_ref[n] = value


def both_ways(z, rates_ref, own_ref, blocks, groups, top_ref, v_ref, u_ref, ends_ref, sums_ref):
    me = lax.axis_index("gz")
    group, member = me // z.members, me % z.members
    ohms = rates_ref[3]
    zero, one = jnp.zeros(z.tile, F32), jnp.ones(z.tile, F32)
    ys = range(z.ny)

    def ohm(ref, row):
        return ohms * spread(ref, row, z)

    def totals(sums, j, y):
        return sums[j, per_line(z, y), :], sums[j, per_line(z, z.ny + y), :]

    def up(refs, j, state):
        sums, matrices = refs
        out = []
        for y in ys:
            v, w, total = state[3 * y : 3 * y + 3]
            s1, s2 = totals(sums, j, y)
            pv, pw, qv, qw = (matrices[j, 4 * y + n] for n in range(4))
            out += [pv * v + qv * w, pw * v + qw * w, total + (v * s1 + w * s2)]
        return tuple(out)

    def down(refs, j, state):
        sums, matrices = refs
        out = []
        for y in ys:
            u, w, total = state[3 * y : 3 * y + 3]
            s1, s2 = totals(sums, j, y)
            pv, pw, qv, qw = (matrices[j, 4 * y + n] for n in range(4))
            u, w = qw * u + qv * w, pw * u + pv * w
            out += [u, w, total + (u * s1 - w * s2)]
        return tuple(out)

    state = (zero, one, zero) * z.ny
    for j in range(z.groups_z - 1):
        state = tuple(jnp.where(j < group, a, b) for a, b in zip(up(groups, j, state), state))
    for j in range(z.members - 1):
        state = tuple(jnp.where(j < member, a, b) for a, b in zip(up(blocks, j, state), state))
    rising = []
    for y in ys:
        pair = state[3 * y : 3 * y + 2]
        sums_ref[y] = state[3 * y + 2]
        ends_ref[y] = pair[0]
        for i in range(z.nz):
            pair = advance(pair, ohm(own_ref, z.faces_at + y * z.nz + i))
            v_ref[y * z.nz + i] = pair[0]
            if i == 0:
                rising.append(pair)
        ends_ref[z.ny + y] = pair[0] + pair[1] * ohm(own_ref, z.faces_at + z.tiles + y)

    state = ()
    for y in ys:
        state += (ohm(top_ref, y), one, zero)
    for j in reversed(range(1, z.groups_z)):
        state = tuple(jnp.where(j > group, a, b) for a, b in zip(down(groups, j, state), state))
    for j in reversed(range(1, z.members)):
        state = tuple(jnp.where(j > member, a, b) for a, b in zip(down(blocks, j, state), state))
    for y in ys:
        u, w, total = state[3 * y : 3 * y + 3]
        sums_ref[z.ny + y] = total
        ends_ref[3 * z.ny + y] = u - w * ohm(own_ref, z.faces_at + z.tiles + y)
        for i in reversed(range(z.nz)):
            u_ref[y * z.nz + i] = u
            if i == 0:
                v, wv = rising[y]
                ends_ref[4 * z.ny + y] = 1.0 / (wv * u + v * w)
            w = w + u
            u = u + w * ohm(own_ref, z.faces_at + y * z.nz + i)
        ends_ref[2 * z.ny + y] = u


def solve_row(z, y, sums, f_ref, v_ref, u_ref, ends_ref, store):
    below, above = sums
    scale = ends_ref[4 * z.ny + y]
    after = [None] * z.nz
    total = above
    for i in reversed(range(z.nz)):
        t = y * z.nz + i
        after[i] = total
        total = total + u_ref[t] * f_ref[t]
    low = scale * (ends_ref[2 * z.ny + y] * below + ends_ref[y] * total)
    total = below
    for i in range(z.nz):
        t = y * z.nz + i
        total = total + v_ref[t] * f_ref[t]
        store(i, scale * (u_ref[t] * total + v_ref[t] * after[i]))
    high = scale * (ends_ref[3 * z.ny + y] * total + ends_ref[z.ny + y] * above)
    return low, high


def meet_kernel(z, rates_ref, f_ref, pay_ref, own_group, block_sums, block_transfers, far_transfer, *refs):
    across, refs = refs[: z.groups_z - 1], refs[z.groups_z - 1 :]
    v_ref, u_ref, ends_ref, sums_ref, *y_refs, group_sums, group_transfers, tops = refs
    group = lax.axis_index("gz") // z.members
    near = transfers(z, rates_ref, across[:-1], z.members)
    for i, ref in enumerate((own_group, *across)):
        group_sums[group ^ i] = ref[: 2 * z.lines, :]
        tops[group ^ i] = ref[z.group_top :, :]
    for i, matrix in enumerate(near):
        for n, value in enumerate(matrix):
            group_transfers[group ^ (i + 1), n] = value
    group_transfers[group ^ len(across)] = far_transfer[...]
    both_ways(
        z, rates_ref, pay_ref, (block_sums, block_transfers), (group_sums, group_transfers),
        tops.at[z.groups_z - 1], v_ref, u_ref, ends_ref, sums_ref,
    )
    for ref, y in zip(y_refs, y_picks(z)):

        def store(i, value):
            ref[i * z.species : (i + 1) * z.species, :] = value

        solve_row(z, y, (sums_ref[y], sums_ref[z.ny + y]), f_ref, v_ref, u_ref, ends_ref, store)


def rows_kernel(z, f_ref, v_ref, u_ref, ends_ref, sums_ref, tiles_ref, halo_ref):
    for y in range(z.ny):

        def store(i, value):
            tiles_ref[y * z.nz + i] = value

        low, high = solve_row(
            z, y, (sums_ref[y], sums_ref[z.ny + y]), f_ref, v_ref, u_ref, ends_ref, store
        )
        halo_ref[y] = low
        halo_ref[z.ny + y] = high


def halo_rows(z):
    if z.gy == 2:
        core = lax.axis_index("gy")
        return y_picks(z), [core + j for j in range(z.ny - 1)]
    return list(range(z.ny)), []


def places_of(z, ys):
    return [(y, row) for y in ys for row in range(z.nz)]


def inner_kernel(
    z, tiles_ref, halo_ref, rates_ref, x_faces, arrhenius_ref, proportions_ref, y_faces, z_faces,
    left_ref, right_ref, inverse_ref, base_ref, f_ref, joined_ref
):
    ys, _ = halo_rows(z)
    for i, (y, row) in enumerate(places_of(z, ys)):
        join_levels(z, y * z.nz + row, left_ref, right_ref, joined_ref, i)
    base_sides(z, tiles_ref, rates_ref, x_faces, arrhenius_ref, proportions_ref, base_ref)
    _, ys = halo_rows(z)
    zero = jnp.zeros(z.tile, F32)
    if ys:
        right_sides(
            z, places_of(z, ys), tiles_ref, base_ref, lambda side, y: halo_ref[side * z.ny + y],
            lambda side, row: zero, rates_ref, y_faces, z_faces, left_ref, right_ref, inverse_ref, f_ref,
        )


def second_kernel(
    z, tiles_ref, halo_ref, rates_ref, y_faces, z_faces, left_ref, right_ref, inverse_ref, base_ref,
    inner_ref, joined_ref, v_ref, u_ref, *refs
):
    halos = 1 if z.gy == 2 else 2
    received = refs[:halos]
    pay_ref, f_ref = refs[halos:]
    ys, done = halo_rows(z)
    for y, row in places_of(z, done):
        f_ref[y * z.nz + row] = inner_ref[y * z.nz + row]
    right_sides(
        z, places_of(z, ys), tiles_ref, base_ref, lambda side, y: halo_ref[side * z.ny + y],
        y_halos(z, received), rates_ref, y_faces, z_faces, left_ref, right_ref, inverse_ref, f_ref,
        lambda n, i: joined_ref[n, i],
    )
    send_sums(z, f_ref, v_ref, u_ref, pay_ref)


def last_kernel(z, within_ref, f_ref, v_ref, u_ref, ends_ref, *refs):
    *across, out_hbm, rows_ref, sems = refs
    group = lax.axis_index("gz") // z.members
    below, above = within_ref[0], within_ref[1]
    for i, ref in enumerate(reversed(across)):
        lower = (group ^ (i + 1)) < group
        value = ref[...]
        below = below + jnp.where(lower, value, 0.0)
        above = above + jnp.where(lower, 0.0, value)
    blocks = rows_ref.reshape(z.species, z.ny, z.nz, z.nx)
    copies = []
    for y in range(z.ny):

        def store(i, value):
            rows_ref[pl.ds(y * z.nz + i, z.species, stride=z.tiles), :] = value

        sums = below[per_line(z, y)], above[per_line(z, y)]
        solve_row(z, y, sums, f_ref, v_ref, u_ref, ends_ref, store)
        copies.append(pltpu.make_async_copy(blocks.at[:, y], out_hbm.at[:, y], sems.at[y]))
        copies[-1].start()
    for copy in copies:
        copy.wait()


def per_device(z, c, k, warm, sigma, frequency, barrier, proportions):
    in_vmem = pl.BlockSpec(memory_space=pltpu.VMEM)
    hbm = pl.BlockSpec(memory_space=pltpu.HBM)

    def shaped(*shape):
        return jax.ShapeDtypeStruct(shape, F32)

    def call(kernel, outs, ins, scratch=(), spec=in_vmem, out_spec=in_vmem, us=0.5):
        return pl.pallas_call(
            functools.partial(kernel, z),
            out_shape=outs,
            in_specs=[spec] * len(ins),
            out_specs=jax.tree.map(lambda _: out_spec, outs),
            scratch_shapes=list(scratch),
            compiler_params=pltpu.CompilerParams(vmem_limit_bytes=48 * 2**20),
            cost_estimate=pl.CostEstimate(
                flops=0, bytes_accessed=int(us * 3.69e6), transcendentals=0
            ),
        )(*ins)

    def shift(value, axis, by):
        count = lax.axis_size(axis)
        return lax.ppermute(value, axis, [(i, (i + by) % count) for i in range(count)])

    def swap(sends):
        return [shift(value, "gy", by) for value, by in zip(sends, (1, -1))]

    arguments = jnp.concatenate([v.reshape(-1, z.nx) for v in (c, k, warm)])
    halos = 1 if z.gy == 2 else 2
    block = shaped(z.tiles, *z.tile)
    ends_shape = shaped(5 * z.ny, *z.tile)

    def exchange(value, count, unit):
        values = value if isinstance(value, list) else [value] * (count - 1)
        pairs = [[(i, i ^ (k * unit)) for i in range(z.devices)] for k in range(1, count)]
        if isinstance(value, list):
            return [lax.ppermute(v, "gz", p) for v, p in zip(values[::-1], pairs[::-1])][::-1]
        return [lax.ppermute(v, "gz", p) for v, p in zip(values, pairs)]

    def exchange_inside(value):
        received = exchange(value, z.members, 1)
        return [received[k - 1] for k in z.partners]

    def neighbours(near, far):
        last = z.devices - 1
        links = [(i, i + 1) for i in range(1, last, 2)]
        links = [pair for i, j in links for pair in ((i, j), (j, i))]
        ends = [(i, i) for i in (0, last)]
        far_pairs = [(i * z.gy + n, j * z.gy + n) for i, j in links for n in range(z.gy)]
        far_pairs += [(i * z.gy + n, j * z.gy + (n ^ 1)) for i, j in ends for n in range(z.gy)]
        far = lax.ppermute(far, ("gz", "gy"), far_pairs)
        return exchange(near, 2, 1)[0], far

    far, near, *sends = call(
        edges_kernel,
        [shaped(z.edge_rows, z.nx)] * 2 + [shaped(z.nz * (z.species + 1), z.nx)] * halos,
        [arguments],
    )
    near, far = neighbours(near, far)
    received = swap(sends)
    levels = shaped(z.levels, z.tiles, *z.tile)
    faces = shaped(2, z.tiles, z.nx)
    rates, x_faces, left, right, inverse = call(
        coefficients_kernel,
        [shaped(4, *z.tile), faces, levels, levels, block],
        [arguments, sigma.reshape(1, -1)],
        us=1.0,
    )
    vectors = [shift(v, "gy", 1).reshape(1, -1) for v in (frequency, barrier)]
    tiles, arrhenius, base = call(
        source_kernel,
        [block] * 3,
        [arguments, *vectors, proportions, rates, x_faces],
        [pltpu.VMEM((z.tiles, z.nx), F32)],
    )
    x_solve = [left, right, inverse]
    early, y_faces, edge_joined = call(
        early_kernel,
        [block, faces, shaped(4 * z.pairs, len(edge_places(z)), *z.tile)],
        [arguments, tiles, base, rates, *x_solve, *received],
        [pltpu.VMEM((2, z.tiles, z.nx), F32)],
    )
    pay, f, z_faces = call(
        first_kernel,
        [shaped(z.block_rows, z.nx), block, faces],
        [arguments, far, near, tiles, base, rates, *x_solve, early, y_faces, edge_joined, *received],
        [pltpu.VMEM((z.edge_rows, z.nx), F32)] * 2,
    )
    inside = exchange_inside(pay)
    group = call(
        merge_kernel,
        shaped(z.group_rows, z.nx),
        [rates, pay, *inside],
        [pltpu.VMEM((z.members, z.block_rows, z.nx), F32)],
    )
    across = exchange(group, z.groups_z, z.members)
    matrices = shaped(4 * z.ny, *z.tile)
    block_sums, block_transfers = call(
        inside_kernel,
        [shaped(z.members, 2 * z.lines, z.nx), shaped(z.members, *matrices.shape)],
        [rates, pay, *inside],
    )
    far_transfer = call(far_kernel, matrices, [rates, across[-1]])
    v, u, ends, sums, *sends = call(
        meet_kernel,
        [block, block, ends_shape, shaped(2 * z.ny, *z.tile)]
        + [shaped(z.nz * z.species, z.nx)] * halos,
        [rates, f, pay, group, block_sums, block_transfers, far_transfer, *across],
        [
            pltpu.VMEM((z.groups_z, 2 * z.lines, z.nx), F32),
            pltpu.VMEM((z.groups_z, *matrices.shape), F32),
            pltpu.VMEM((z.groups_z, z.group_rows - z.group_top, z.nx), F32),
        ],
    )

    received = swap(sends)
    tiles, halo = call(rows_kernel, [block, shaped(2 * z.ny, *z.tile)], [f, v, u, ends, sums])
    rows_with_halo = 1 if z.gy == 2 else z.ny
    base, f, joined = call(
        inner_kernel,
        [block, block, shaped(4 * z.pairs, rows_with_halo * z.nz, *z.tile)],
        [tiles, halo, rates, x_faces, arrhenius, proportions, y_faces, z_faces, *x_solve],
    )
    pay, f = call(
        second_kernel,
        [shaped(2, z.lines, z.nx), block],
        [tiles, halo, rates, y_faces, z_faces, *x_solve, base, f, joined, v, u, *received],
    )
    inside = exchange_inside(pay)
    within, *totals = call(
        total_kernel,
        [shaped(2, z.lines, z.nx)] + [shaped(z.lines, z.nx)] * (z.groups_z - 1),
        [pay, *inside],
    )
    across = exchange(totals[::-1], z.groups_z, z.members)
    return call(
        last_kernel,
        shaped(z.species, z.ny, z.nz, z.nx),
        [within, f, v, u, ends, *across[::-1]],
        [pltpu.VMEM((z.species * z.tiles, z.nx), F32), pltpu.SemaphoreType.DMA((z.ny,))],
        out_spec=hbm,
    )


def solution(mesh):
    def device_program(starting_densities, *others):
        sizes = Sizes(mesh, starting_densities.shape)
        return per_device(sizes, starting_densities, *others)

    return jax.shard_map(
        device_program,
        mesh=mesh,
        in_specs=(
            P(None, "gy", "gz", None),
            P("gy", "gz", None),
            P("gy", "gz", None),
            P(),
            P(),
            P(),
            P(),
        ),
        out_specs=P(None, "gy", "gz", None),
        check_vma=False,
    )
```
